128 devices in a mesh: seq: 16 (over x_hi, y, core), fsdp: 8 (over z, x_lo).
Axes of the slice: x: 4 (x_hi: 2, x_lo: 2; x = x_hi * 2 + x_lo), y: 4, z: 4, core: 2. Of those that a mesh axis runs over, the one named last changes fastest.
Arguments:
- tokens: bfloat16 [8, 2048, 1024], P('fsdp', 'seq'), may hold values from -6 to 6
- segment: int32 [8, 2048], P('fsdp'), may hold values from 0 to 8, as said below
- ln_gain: bfloat16 [2, 1024], P(None, 'fsdp'), may hold values from 0.5 to 2
- ln_bias: bfloat16 [2, 1024], P(None, 'fsdp'), may hold values from -3 to 3
- w_qkv: bfloat16 [2, 1024, 3072], P(None, 'fsdp'), may hold values from -0.1875 to 0.1875
- w_out: bfloat16 [2, 1024, 1024], P(None, 'fsdp'), may hold values from -0.75 to 0.75
- w_in: bfloat16 [2, 1024, 4096], P(None, 'fsdp'), may hold values from -0.1875 to 0.1875
- b_in: bfloat16 [2, 4096], P(None, 'fsdp'), may hold values from -4 to 4
- w_fc: bfloat16 [2, 4096, 1024], P(None, 'fsdp'), may hold values from -0.09375 to 0.09375
- b_fc: bfloat16 [2, 1024], P(None, 'fsdp'), may hold values from -3 to 3
- cotangent: bfloat16 [8, 2048, 1024], P('fsdp', 'seq'), may hold values from -6 to 6
Outputs:
- mixed_out: bfloat16 [8, 2048, 1024], P('fsdp', 'seq')
- grad_tokens: float32 [8, 2048, 1024], P('fsdp', 'seq')
- grad_gain: float32 [2, 1024], P(None, 'fsdp')
- grad_shift: float32 [2, 1024], P(None, 'fsdp')
- grad_qkv: float32 [2, 1024, 3072], P(None, 'fsdp')
- grad_out: float32 [2, 1024, 1024], P(None, 'fsdp')
- grad_in: float32 [2, 1024, 4096], P(None, 'fsdp')
- grad_in_bias: float32 [2, 4096], P(None, 'fsdp')
- grad_fc: float32 [2, 4096, 1024], P(None, 'fsdp')
- grad_fc_bias: float32 [2, 1024], P(None, 'fsdp')
The draws below stay inside these ranges and needn't reach their ends.
Inputs may be any that keep to these rules, and one draw needn't show every extreme that they name: Within each group segment numbers never fall along the tokens; the prompt (segment 0) holds 1040 to 1536 tokens; every continuation holds one token or more.
All inputs are finite; a program needn't handle non-finite values.
Results may differ from the reference program's by a relative error of at most 0.022.
Values may be sent and summed in bfloat16 or wider, within the bound.
No kernel may reach another device: no remote copies, remote signals or barrier semaphores. Data moves between devices by JAX's collectives and lax.ppermute only.
A program may use at most 256 MiB of HBM per device.

```python
import math
import jax
import jax.numpy as jnp
from jax import lax

D = 1024
HEADS = 16
FF = 4096
HEAD_DIM = 64
ROT = 32
LAYERS = 2
CONTS = 8
GROUP = 2048
GROUPS = 8


def draw_segment(key, part):
    key = jax.random.fold_in(key, 11)
    first_key, second_key = jax.random.split(key)
    steps_back = jax.random.randint(first_key, (GROUPS,), 0, GROUP // 64)
    not_first = (jnp.arange(GROUPS) > 0).astype(jnp.int32)
    prompt = 3 * GROUP // 4 - 16 * steps_back * not_first
    remain = GROUP - prompt
    shares = jax.random.randint(second_key, (GROUPS, CONTS), 1, 3)
    running = jnp.cumsum(shares, axis=1)
    whole = running[:, -1:]
    bounds = prompt[:, None] + remain[:, None] * running // whole
    places = jnp.arange(GROUP, dtype=jnp.int32)
    base = (places[None, :] >= prompt[:, None]).astype(jnp.int32)
    later = jnp.sum((places[None, :, None] >= bounds[:, None, :CONTS - 1]).astype(jnp.int32), axis=2)
    return (base + later).astype(jnp.int32)


def shard_levels(stream_key, extent, cuts, smallest, high):
    loudness, own = 1.0, jax.random.fold_in(stream_key, 6)
    for position, shards_of in cuts:
        heights = jnp.exp(jax.random.uniform(jax.random.fold_in(own, position), (shards_of,), jnp.float32, smallest / len(cuts), high / len(cuts)))
        loudness = loudness * jnp.repeat(heights, extent[position] // shards_of).reshape([-1 if axis == position else 1 for axis in range(len(extent))])
    return loudness


def bell_draw(own_key, dims, width, limit, shards=(), kind=jnp.bfloat16):
    values = width * jax.random.normal(own_key, dims, jnp.float32)
    if shards:
        values = values * shard_levels(own_key, dims, shards, -0.22, 0.18)
    return jnp.clip(values, -limit, limit).astype(kind)


def setup_inputs(seed: int = 0) -> dict:
    splits = jax.random.split(jax.random.key(seed), 12)
    return {
        "tokens": bell_draw(splits[0], (GROUPS, GROUP, D), 1.0, 6.0, ((0, 8), (1, 16))),
        "segment": draw_segment(jax.random.fold_in(splits[11], 71), 0),
        "ln_gain": jnp.clip(jnp.exp(math.log(2.0) - 1.3862944 * jax.random.uniform(splits[2], (LAYERS, D), jnp.float32) ** shard_levels(splits[2], (LAYERS, D), ((1, 8),), -0.2, 0.2)), 0.5, 2.0).astype(jnp.bfloat16),
        "ln_bias": bell_draw(splits[3], (LAYERS, D), 0.5, 3.0, ((1, 8),)),
        "w_qkv": bell_draw(splits[4], (LAYERS, D, 3 * D), D ** -0.5, 0.1875, ((1, 8),)),
        "w_out": bell_draw(splits[5], (LAYERS, D, D), (D // 16) ** -0.5, 0.75, ((1, 8),)),
        "w_in": bell_draw(splits[6], (LAYERS, D, FF), D ** -0.5, 0.1875, ((1, 8),)),
        "b_in": bell_draw(splits[7], (LAYERS, FF), 1.0, 4.0, ((1, 8),)),
        "w_fc": bell_draw(splits[8], (LAYERS, FF, D), FF ** -0.5, 0.09375, ((1, 8),)),
        "b_fc": bell_draw(splits[9], (LAYERS, D), 0.5, 3.0, ((1, 8),)),
        "cotangent": bell_draw(splits[10], (GROUPS, GROUP, D), 1.0, 6.0, ((0, 8), (1, 16))),
    }


@jax.custom_vjp
def low(v):
    return lax.optimization_barrier(v.astype(jnp.bfloat16)).astype(jnp.float32)

@jax.custom_vjp
def low_back(v):
    return v

def low_keep(v):
    return (low(v), None)

def low_pass(kept, grad):
    return (grad,)

def back_keep(v):
    return (v, None)

def back_low(kept, grad):
    return (low(grad),)
low.defvjp(low_keep, low_pass)
low_back.defvjp(back_keep, back_low)

def product(left, right):
    return jnp.dot(left, right, precision=lax.Precision.HIGHEST, preferred_element_type=jnp.float32)

def positions_of(group_seg):
    token_index = jnp.arange(group_seg.shape[0], dtype=jnp.int32)
    labels = jnp.arange(CONTS + 1, dtype=jnp.int32)
    member = (group_seg[:, None] == labels[None, :]).astype(jnp.int32)
    counts = lax.optimization_barrier(jnp.sum(member, axis=0))
    starts = jnp.cumsum(counts) - counts
    own_start = lax.optimization_barrier(jnp.sum(member * starts[None, :], axis=1))
    return token_index - own_start + jnp.where(group_seg > 0, counts[0], 0)

def angles(positions):
    half = ROT // 2
    inverse = 10000.0 ** (-2.0 * jnp.arange(half, dtype=jnp.float32) / ROT)
    phase = positions.astype(jnp.float32)[:, None] * inverse[None, :]
    return (jnp.cos(phase), jnp.sin(phase))

def rotate(field, cosine, sine):
    lead = field.shape[:-1]
    pairs = field[..., :ROT].reshape(lead + (ROT // 2, 2))
    even = pairs[..., 0]
    odd = pairs[..., 1]
    cos_b = cosine[:, None, :]
    sin_b = sine[:, None, :]
    turned = jnp.stack([even * cos_b - odd * sin_b, odd * cos_b + even * sin_b], axis=-1).reshape(lead + (ROT,))
    return jnp.concatenate([turned, field[..., ROT:]], axis=-1)

def norm_part(inputs, gain, shift):
    average = lax.optimization_barrier(jnp.mean(inputs, axis=-1, keepdims=True))
    centred = inputs - average
    variance = lax.optimization_barrier(jnp.mean(centred * centred, axis=-1, keepdims=True))
    return centred * lax.rsqrt(variance + 1e-05) * gain + shift

def visible(row_start, block_len, group_seg):
    key_index = jnp.arange(group_seg.shape[0], dtype=jnp.int32)
    row_index = row_start + jnp.arange(block_len, dtype=jnp.int32)
    row_seg = lax.dynamic_slice_in_dim(group_seg, row_start, block_len, 0)
    same = (group_seg[None, :] == 0) | (group_seg[None, :] == row_seg[:, None])
    return (key_index[None, :] <= row_index[:, None]) & same

def attend(queries, keys_rot, values, group_seg):
    length = queries.shape[0]
    block_len = min(512, length)
    scaling = HEAD_DIM ** (-0.5)

    def one_block(row_start):
        rows_q = lax.dynamic_slice_in_dim(queries, row_start, block_len, 0)
        allowed = visible(row_start, block_len, group_seg)
        scores = low_back(jnp.einsum('qhd,khd->hqk', rows_q, keys_rot, precision=lax.Precision.HIGHEST) * scaling)
        scores = jnp.where(allowed[None], scores, -1e+30)
        attn_probs = jax.nn.softmax(scores, axis=-1)
        return jnp.einsum('hqk,khd->qhd', low(attn_probs), values, precision=lax.Precision.HIGHEST)
    starts = jnp.arange(length // block_len, dtype=jnp.int32) * block_len
    mixed = lax.map(jax.checkpoint(one_block), starts)
    return mixed.reshape(length, queries.shape[1], queries.shape[2])

def one_layer(inputs, weights, group_seg, cosine, sine):
    gain, shift, w_q, w_o, w_i, bias_i, w_f, bias_f = weights
    length = inputs.shape[0]
    normed = low(norm_part(inputs, gain, shift))
    joined = low_back(low(product(normed, w_q))).reshape(length, 3, HEADS, HEAD_DIM)
    queries = low(rotate(joined[:, 0], cosine, sine))
    keys_rot = low(rotate(joined[:, 1], cosine, sine))
    values = joined[:, 2]
    mixed = attend(queries, keys_rot, values, group_seg)
    mixed = low_back(low(mixed)).reshape(length, D)
    branch = low_back(product(mixed, w_o))
    pre_act = low_back(product(normed, w_i)) + bias_i
    active = low(jax.nn.gelu(pre_act, approximate=True))
    feed = low_back(product(active, w_f)) + bias_f
    return inputs + branch + feed

def reference(tokens, segment, ln_gain, ln_bias, w_qkv, w_out, w_in, b_in, w_fc, b_fc, cotangent):
    params = (ln_gain.astype(jnp.float32), ln_bias.astype(jnp.float32), w_qkv.astype(jnp.float32), w_out.astype(jnp.float32), w_in.astype(jnp.float32), b_in.astype(jnp.float32), w_fc.astype(jnp.float32), b_fc.astype(jnp.float32))
    start = tokens.astype(jnp.float32)

    def forward(first, weights):

        def per_group(running, group_item):
            inputs, group_seg = group_item
            cosine, sine = angles(positions_of(group_seg))
            for layer_no in range(LAYERS):
                layer_weights = tuple((w[layer_no] for w in weights))
                inputs = one_layer(inputs, layer_weights, group_seg, cosine, sine)
            return (running, inputs)
        unused, result = lax.scan(per_group, jnp.zeros((), jnp.float32), (first, segment))
        return result
    result, pull = jax.vjp(forward, start, params)
    d_tokens, d_weights = pull(cotangent.astype(jnp.float32))
    return (result.astype(jnp.bfloat16), d_tokens, d_weights[0], d_weights[1], d_weights[2], d_weights[3], d_weights[4], d_weights[5], d_weights[6], d_weights[7])
```

```python
import functools
import numpy as np
import jax
import jax.numpy as jnp
from jax import lax
from jax.experimental import pallas as pl
from jax.experimental.pallas import tpu as pltpu
from jax.sharding import Mesh, PartitionSpec as P

HEADS = 16
ROT = 32
LAYERS = 2
CONTS = 8
D = 1024
FF = 4096
HALF = 1024
BLK = 128
QB = 256
AXES = ("xh", "y", "core", "z", "xl")
FS = ("z", "xl")
f32 = jnp.float32
bf16 = jnp.bfloat16
NT = (((1,), (1,)), ((), ()))


def shift(x, axis, by, size):
    return lax.ppermute(x, axis, [(i, (i + by) % size) for i in range(size)])


def pick(x, index, axis=0):
    return lax.dynamic_index_in_dim(x, index, axis, keepdims=False)


def gather_tokens(own):
    y = lax.axis_index("y")
    c = lax.axis_index("core")
    parts = [own, shift(own, "y", -1, 4), shift(own, "y", 2, 4), shift(own, "y", 1, 4)]
    mine = jnp.stack(parts)
    other = shift(mine, "core", 1, 2)
    pair = jnp.where(c == 0, jnp.stack([mine, other], 1), jnp.stack([other, mine], 1))
    twice = jnp.concatenate([pair, pair], 0)
    ordered = lax.dynamic_slice_in_dim(twice, (4 - y) % 4, 4, 0)
    return ordered.reshape(HALF, own.shape[1])


def scatter_tokens(partial):
    y = lax.axis_index("y")
    c = lax.axis_index("core")
    blocks = partial.reshape(4, 2, BLK, partial.shape[1])
    away = pick(blocks, 1 - c, 1).astype(bf16)
    got = shift(away, "core", 1, 2)
    both = pick(blocks, c, 1).astype(f32) + got.astype(f32)
    low = both.astype(bf16)
    total = pick(both, y)
    for by in (2, 1, 3):
        total = total + shift(pick(low, (y + by) % 4), "y", by, 4).astype(f32)
    return total


def head_masks(shape, axis):
    lane = lax.broadcasted_iota(jnp.int32, shape, axis)
    return [lane < 64, lane >= 64]


def seen(i, kk, qseg_ref, kseg_ref):
    q0 = i * QB
    qs = qseg_ref[0:1, q0 : q0 + QB]
    ks = kseg_ref[0:kk, 0:1]
    key = lax.broadcasted_iota(jnp.int32, (kk, QB), 0)
    query = q0 + lax.broadcasted_iota(jnp.int32, (kk, QB), 1)
    return (key <= query) & ((ks == 0) | (ks == qs))


def attn_own_kernel(q_ref, k_ref, vt_ref, qseg_ref, kseg_ref, acc_ref, m_ref, l_ref):
    masks = head_masks((HALF, BLK), 1)
    zero = jnp.zeros((), bf16)
    km = [jnp.where(masks[h], k_ref[...], zero) for h in range(2)]
    for i in range(HALF // QB):
        cols = slice(i * QB, (i + 1) * QB)
        kk = (i + 1) * QB
        allowed = seen(i, kk, qseg_ref, kseg_ref)
        for h in range(2):
            s = lax.dot_general(km[h][:kk], q_ref[cols, :], NT, preferred_element_type=f32)
            s = jnp.where(allowed, s, -1e30)
            m = jnp.max(s, axis=0, keepdims=True)
            p = jnp.exp(s - m)
            l_ref[h : h + 1, cols] = jnp.sum(p, axis=0, keepdims=True)
            m_ref[h : h + 1, cols] = m
            rows = slice(h * 64, h * 64 + 64)
            acc_ref[rows, cols] = jnp.dot(
                vt_ref[rows, :kk], p.astype(bf16), preferred_element_type=f32
            )


def attn_full_kernel(flag_ref, q_ref, k_ref, vt_ref, acc_ref, m_ref, l_ref, out_ref, lse_ref, tmp_ref):
    upper = flag_ref[0] == 1

    @pl.when(upper)
    def _():
        masks = head_masks((HALF, BLK), 1)
        zero = jnp.zeros((), bf16)
        km = [jnp.where(masks[h], k_ref[...], zero) for h in range(2)]
        for i in range(HALF // QB):
            cols = slice(i * QB, (i + 1) * QB)
            for h in range(2):
                rows = slice(h * 64, h * 64 + 64)
                s = lax.dot_general(km[h], q_ref[cols, :], NT, preferred_element_type=f32)
                m0 = m_ref[h : h + 1, cols]
                m = jnp.maximum(m0, jnp.max(s, axis=0, keepdims=True))
                p = jnp.exp(s - m)
                a = jnp.exp(m0 - m)
                l = l_ref[h : h + 1, cols] * a + jnp.sum(p, axis=0, keepdims=True)
                o = jnp.dot(vt_ref[rows, :], p.astype(bf16), preferred_element_type=f32)
                tmp_ref[rows, cols] = (acc_ref[rows, cols] * a + o) / l
                lse_ref[h : h + 1, cols] = m + jnp.log(l)

    @pl.when(jnp.logical_not(upper))
    def _():
        for h in range(2):
            rows = slice(h * 64, h * 64 + 64)
            l = l_ref[h : h + 1, :]
            tmp_ref[rows, :] = acc_ref[rows, :] / l
            lse_ref[h : h + 1, :] = m_ref[h : h + 1, :] + jnp.log(l)

    out_ref[...] = jnp.transpose(tmp_ref[...]).astype(bf16)


def row_delta(attn_ref, do_ref):
    prod = attn_ref[...].astype(f32) * do_ref[...].astype(f32)
    head = lax.broadcasted_iota(jnp.int32, (8, BLK), 0)
    lane = lax.broadcasted_iota(jnp.int32, (8, BLK), 1) // 64
    pickers = jnp.where(head == lane, 1.0, 0.0).astype(f32)
    return lax.dot_general(
        pickers, prod, NT, precision=lax.Precision.HIGHEST, preferred_element_type=f32
    )


def grad_block(km, vm, kt, qm, dom, q_blk, do_blk, lse, delta, allowed):
    s = lax.dot_general(km, q_blk, NT, preferred_element_type=f32)
    p = jnp.exp(s - lse)
    if allowed is not None:
        p = jnp.where(allowed, p, 0.0)
    dp = lax.dot_general(vm, do_blk, NT, preferred_element_type=f32)
    ds = (p * (dp - delta)).astype(bf16)
    dqt = jnp.dot(kt, ds, preferred_element_type=f32)
    dk = jnp.dot(ds, qm, preferred_element_type=f32)
    dv = jnp.dot(p.astype(bf16), dom, preferred_element_type=f32)
    return dqt, dk, dv


def grad_setup(q_ref, k_ref, v_ref, do_ref):
    masks = head_masks((HALF, BLK), 1)
    zero = jnp.zeros((), bf16)
    cut = lambda ref: [jnp.where(masks[h], ref[...], zero) for h in range(2)]
    return cut(q_ref), cut(k_ref), cut(v_ref), cut(do_ref)


def grad_full_kernel(flag_ref, q_ref, k_ref, kt_ref, v_ref, do_ref, attn_ref, lse_ref, dqt_ref, dk_ref, dv_ref, acck, accv):
    upper = flag_ref[0] == 1

    @pl.when(upper)
    def _():
        delta = row_delta(attn_ref, do_ref)
        qm, km, vm, dom = grad_setup(q_ref, k_ref, v_ref, do_ref)
        for i in range(HALF // QB):
            cols = slice(i * QB, (i + 1) * QB)
            for h in range(2):
                rows = slice(h * 64, h * 64 + 64)
                dqt, dk, dv = grad_block(
                    km[h], vm[h], kt_ref[rows, :], qm[h][cols], dom[h][cols],
                    q_ref[cols, :], do_ref[cols, :],
                    lse_ref[h : h + 1, cols], delta[h : h + 1, cols], None,
                )
                dqt_ref[rows, cols] = dqt
                if i == 0 and h == 0:
                    acck[...] = dk
                    accv[...] = dv
                else:
                    acck[...] += dk
                    accv[...] += dv
        dk_ref[...] = acck[...].astype(bf16)
        dv_ref[...] = accv[...].astype(bf16)

    @pl.when(jnp.logical_not(upper))
    def _():
        dqt_ref[...] = jnp.zeros_like(dqt_ref)
        dk_ref[...] = jnp.zeros_like(dk_ref)
        dv_ref[...] = jnp.zeros_like(dv_ref)


def grad_own_kernel(q_ref, k_ref, kt_ref, v_ref, do_ref, attn_ref, lse_ref, qseg_ref, kseg_ref, dqt0_ref, dq_ref, dk_ref, dv_ref, tmp):
    delta = row_delta(attn_ref, do_ref)
    qm, km, vm, dom = grad_setup(q_ref, k_ref, v_ref, do_ref)
    dk_ref[...] = jnp.zeros_like(dk_ref)
    dv_ref[...] = jnp.zeros_like(dv_ref)
    for i in range(HALF // QB):
        cols = slice(i * QB, (i + 1) * QB)
        kk = (i + 1) * QB
        allowed = seen(i, kk, qseg_ref, kseg_ref)
        for h in range(2):
            rows = slice(h * 64, h * 64 + 64)
            dqt, dk, dv = grad_block(
                km[h][:kk], vm[h][:kk], kt_ref[rows, :kk], qm[h][cols], dom[h][cols],
                q_ref[cols, :], do_ref[cols, :],
                lse_ref[h : h + 1, cols], delta[h : h + 1, cols], allowed,
            )
            tmp[rows, cols] = (dqt + dqt0_ref[rows, cols]) * 0.125
            dk_ref[:kk, :] += dk
            dv_ref[:kk, :] += dv
    dq_ref[...] = jnp.transpose(tmp[...])


PARAMS = pltpu.CompilerParams(vmem_limit_bytes=48 * 1024 * 1024)
VM = pl.BlockSpec(memory_space=pltpu.VMEM)
SM = pl.BlockSpec(memory_space=pltpu.SMEM)


def shaped(*args):
    return [jax.ShapeDtypeStruct(s, t) for s, t in args]


def attn_own(q, k, vt, qseg, kseg):
    return pl.pallas_call(
        attn_own_kernel,
        out_shape=shaped(((BLK, HALF), f32), ((2, HALF), f32), ((2, HALF), f32)),
        in_specs=[VM] * 5,
        out_specs=[VM] * 3,
        compiler_params=PARAMS,
        name="attn_own",
    )(q, k, vt, qseg, kseg)


def attn_full(flag, q, k, vt, acc, m, l):
    return pl.pallas_call(
        attn_full_kernel,
        out_shape=shaped(((HALF, BLK), bf16), ((2, HALF), f32)),
        in_specs=[SM] + [VM] * 6,
        out_specs=[VM] * 2,
        scratch_shapes=[pltpu.VMEM((BLK, HALF), f32)],
        compiler_params=PARAMS,
        name="attn_full",
    )(flag, q, k, vt, acc, m, l)


def grad_full(flag, q, k, kt, v, do, attn, lse):
    return pl.pallas_call(
        grad_full_kernel,
        out_shape=shaped(((BLK, HALF), f32), ((HALF, BLK), bf16), ((HALF, BLK), bf16)),
        in_specs=[SM] + [VM] * 7,
        out_specs=[VM] * 3,
        scratch_shapes=[pltpu.VMEM((HALF, BLK), f32)] * 2,
        compiler_params=PARAMS,
        name="grad_full",
    )(flag, q, k, kt, v, do, attn, lse)


def grad_own(q, k, kt, v, do, attn, lse, qseg, kseg, dqt0):
    return pl.pallas_call(
        grad_own_kernel,
        out_shape=shaped(((HALF, BLK), f32), ((HALF, BLK), f32), ((HALF, BLK), f32)),
        in_specs=[VM] * 10,
        out_specs=[VM] * 3,
        scratch_shapes=[pltpu.VMEM((BLK, HALF), f32)],
        compiler_params=PARAMS,
        name="grad_own",
    )(q, k, kt, v, do, attn, lse, qseg, kseg, dqt0)


def positions_of(group_seg):
    token_index = jnp.arange(group_seg.shape[0], dtype=jnp.int32)
    labels = jnp.arange(CONTS + 1, dtype=jnp.int32)
    member = (group_seg[:, None] == labels[None, :]).astype(jnp.int32)
    counts = jnp.sum(member, axis=0)
    starts = jnp.cumsum(counts) - counts
    own_start = jnp.sum(member * starts[None, :], axis=1)
    return token_index - own_start + jnp.where(group_seg > 0, counts[0], 0)


def rope_tables(positions):
    lane = jnp.arange(BLK, dtype=jnp.int32) % 64
    inverse = 10000.0 ** (-2.0 * (lane // 2).astype(f32) / ROT)
    turned = lane < ROT
    phase = positions.astype(f32)[:, None] * jnp.where(turned, inverse, 0.0)[None, :]
    sign = jnp.where(lane % 2 == 0, -1.0, 1.0)
    return jnp.cos(phase), jnp.sin(phase) * sign[None, :]


SWAP = np.zeros((BLK, BLK), np.float32)
for _i in range(BLK):
    SWAP[_i ^ 1, _i] = 1.0


def rope(v, cosine, sine):
    swap = jnp.asarray(SWAP, v.dtype)
    precision = lax.Precision.HIGHEST if v.dtype == f32 else None
    partner = jnp.dot(v, swap, precision=precision, preferred_element_type=f32)
    return v.astype(f32) * cosine + partner * sine


def stats(x):
    average = jnp.mean(x, axis=-1, keepdims=True)
    centred = x - average
    variance = jnp.mean(centred * centred, axis=-1, keepdims=True)
    inv = lax.rsqrt(variance + 1e-05)
    return centred * inv, inv


def gelu(x):
    return jax.nn.gelu(x, approximate=True)


def forward_layer(normed, w, ctx):
    wq, wi, wf, wo, bias_i = w
    cosine, sine, flag, qseg, kseg = ctx
    qkv = jnp.dot(normed, wq, preferred_element_type=f32).astype(bf16)
    k = rope(qkv[:, 128:256], cosine, sine).astype(bf16)
    v = qkv[:, 256:]
    far = lax.ppermute(jnp.concatenate([k, v], 1), "xh", [(0, 1)])
    q = (rope(qkv[:, :128], cosine, sine).astype(bf16).astype(f32) * 0.125).astype(bf16)
    pre = jnp.dot(normed, wi, preferred_element_type=f32) + bias_i
    active = gelu(pre).astype(bf16)
    feed = jnp.dot(active, wf, preferred_element_type=f32)
    acc, m, l = attn_own(q, k, v.T, qseg, kseg)
    k0 = far[:, :128]
    v0 = far[:, 128:]
    attn, lse = attn_full(flag, q, k0, v0.T, acc, m, l)
    branch = jnp.dot(attn, wo, preferred_element_type=f32)
    return scatter_tokens(feed + branch), (normed, q, k, v, k0, v0, attn, lse, pre, active)


def backward_layer(g, gr, w, saved, gain, xhat, inv, ctx):
    wq, wi, wf, wo, bias_i = w
    cosine, sine, flag, qseg, kseg = ctx
    normed, q, k, v, k0, v0, attn, lse, pre, active = saved
    dattn = lax.dot_general(gr, wo, NT, preferred_element_type=f32).astype(bf16)
    dqt0, dk0, dv0 = grad_full(flag, q, k0, k0.T, v0, dattn, attn, lse)
    back = lax.ppermute(jnp.concatenate([dk0, dv0], 1), "xh", [(1, 0)])
    d_active = lax.dot_general(gr, wf, NT, preferred_element_type=f32)
    unused, pull = jax.vjp(gelu, pre)
    d_pre = pull(d_active)[0]
    d_bias_i = jnp.sum(d_pre, axis=0)
    d_pre = d_pre.astype(bf16)
    outer = lambda a, b: lax.dot_general(a, b, (((0,), (0,)), ((), ())), preferred_element_type=f32).astype(bf16)
    g_f = outer(active, gr)
    g_o = outer(attn, gr)
    g_i = outer(normed, d_pre)
    dq, dk, dv = grad_own(q, k, k.T, v, dattn, attn, lse, qseg, kseg, dqt0)
    dk = dk + back[:, :128].astype(f32)
    dv = dv + back[:, 128:].astype(f32)
    d_qkv = jnp.concatenate(
        [rope(dq, cosine, -sine).astype(bf16), rope(dk, cosine, -sine).astype(bf16), dv.astype(bf16)], 1
    )
    g_q = outer(normed, d_qkv)
    partial = lax.dot_general(d_pre, wi, NT, preferred_element_type=f32)
    partial = partial + lax.dot_general(d_qkv, wq, NT, preferred_element_type=f32)
    dn = scatter_tokens(partial)
    d_shift = jnp.sum(dn, axis=0)
    d_gain = jnp.sum(dn * xhat, axis=0)
    dx = dn * gain
    dx = inv * (dx - jnp.mean(dx, -1, keepdims=True) - xhat * jnp.mean(dx * xhat, -1, keepdims=True))
    return g + dx, (g_q, g_i, g_f, g_o, d_bias_i, d_gain, d_shift, jnp.sum(g, axis=0))


ROWS = 144


def transpose_owner(x):
    pairs = [(j * 8 + f, f * 8 + j) for j in range(8) for f in range(8)]
    return lax.ppermute(x, ("y", "core", "z", "xl"), pairs)


def fetch_weights(layer, j, w_qkv, w_out, w_in, b_in, w_fc, small):
    wq = pick(w_qkv[layer].reshape(128, 3, 8, 128), j, 2).reshape(128, 384)
    wi = pick(w_in[layer].reshape(128, 8, 8, 64), j, 2).reshape(128, 512)
    wf = pick(w_fc[layer].reshape(8, 64, D), j, 0).reshape(128, 512)
    wo = transpose_owner(pick(w_out[layer].reshape(8, 16, D), j, 0)).reshape(128, 128)
    body = jnp.concatenate([wq, wi, wf, wo], 1)
    bias = pick(b_in[layer].reshape(8, 64), j, 0)
    row = jnp.concatenate([bias, small])
    row = jnp.pad(row, (0, 1536 - row.shape[0]))[None]
    body = jnp.concatenate([body, jnp.pad(row, ((0, ROWS - 129), (0, 0)))], 0)
    full = lax.all_to_all(jnp.broadcast_to(body[None], (8, ROWS, 1536)), FS, 0, 0, tiled=True)
    main = full[:, :128]
    wq = main[:, :, :384].reshape(D, 384)
    wi = main[:, :, 384:896].reshape(D, 512)
    wf = main[:, :, 896:1408].reshape(512, D)
    wo = main[:, :, 1408:].reshape(128, D)
    bias_i = full[:, 128, :64].reshape(512).astype(f32)
    rest = full[:, 128, 64 : 64 + small.shape[0]]
    return (wq, wi, wf, wo, bias_i), rest


def reduce_layer(grads):
    g_q, g_i, g_f, g_o, d_bias_i, d_gain, d_shift, d_bias_f = grads
    body = jnp.concatenate(
        [
            g_q.reshape(8, 128, 384),
            g_i.reshape(8, 128, 512),
            g_f.reshape(8, 128, 512),
            g_o.reshape(8, 128, 128),
        ],
        2,
    )
    row = jnp.concatenate(
        [d_bias_i.reshape(8, 64), d_gain.reshape(8, 128), d_shift.reshape(8, 128), d_bias_f.reshape(8, 128)], 1
    ).astype(bf16)
    row = jnp.pad(row[:, None], ((0, 0), (0, ROWS - 129), (0, 1536 - 448)))
    body = jnp.concatenate([body, row], 1)
    got = lax.all_to_all(body, FS, 0, 0, tiled=True)
    half = jnp.sum(got.astype(f32), axis=0)
    whole = (half + shift(half.astype(bf16), "xh", 1, 2).astype(f32)).astype(bf16)
    piece = whole[:128, 1408:].reshape(16, D)
    piece = transpose_owner(piece).reshape(128, 128)
    whole = jnp.concatenate([whole[:, :1408], jnp.pad(piece, ((0, ROWS - 128), (0, 0)))], 1)
    y = lax.axis_index("y")
    c = lax.axis_index("core")
    parts = [whole, shift(whole, "y", -1, 4), shift(whole, "y", 2, 4), shift(whole, "y", 1, 4)]
    mine = jnp.stack(parts)
    other = shift(mine, "core", 1, 2)
    pair = jnp.where(c == 0, jnp.stack([mine, other], 1), jnp.stack([other, mine], 1))
    twice = jnp.concatenate([pair, pair], 0)
    allj = lax.dynamic_slice_in_dim(twice, (4 - y) % 4, 4, 0).reshape(8, ROWS, 1536)
    main = allj[:, :128].astype(f32)
    o_q = main[:, :, :384].reshape(8, 128, 3, 128).transpose(1, 2, 0, 3).reshape(128, 3 * D)
    o_i = main[:, :, 384:896].reshape(8, 128, 8, 64).transpose(1, 2, 0, 3).reshape(128, FF)
    o_f = main[:, :, 896:1408].reshape(512, D)
    o_o = main[:, :, 1408:].reshape(128, D)
    rows = allj[:, 128].astype(f32)
    o_bi = rows[:, :64].reshape(512)
    sums = jnp.sum(rows[:, 64:448], axis=0)
    return o_q, o_i, o_f, o_o, o_bi, sums[:128], sums[128:256], sums[256:384]


def body(tokens, segment, ln_gain, ln_bias, w_qkv, w_out, w_in, b_in, w_fc, b_fc, cotangent):
    xh = lax.axis_index("xh")
    j = lax.axis_index("y") * 2 + lax.axis_index("core")
    own = tokens[0]
    all_tokens = gather_tokens(own)
    small = jnp.concatenate([ln_gain.reshape(-1), ln_bias.reshape(-1), b_fc.reshape(-1)])
    w0, rest = fetch_weights(0, j, w_qkv, w_out, w_in, b_in, w_fc, small)
    w1, _ = fetch_weights(1, j, w_qkv, w_out, w_in, b_in, w_fc, small)
    weights = (w0, w1)
    rest = rest.reshape(8, 3, 2, 128).transpose(1, 2, 0, 3).reshape(3, 2, D).astype(f32)
    gain, bias, bias_f = rest[0], rest[1], rest[2]
    gr_top = gather_tokens(cotangent[0])

    group_seg = segment[0]
    positions = positions_of(group_seg)
    start = xh * HALF
    seg = lax.dynamic_slice_in_dim(group_seg, start, HALF, 0)
    cosine, sine = rope_tables(lax.dynamic_slice_in_dim(positions, start, HALF, 0))
    flag = xh.astype(jnp.int32).reshape(1)
    qseg = jnp.broadcast_to(seg[None, :], (8, HALF))
    kseg = jnp.broadcast_to(seg[:, None], (HALF, BLK))
    ctx = (cosine, sine, flag, qseg, kseg)

    x0 = own.astype(f32)
    xhat_all, _ = stats(all_tokens.astype(f32))
    normed0 = (xhat_all * gain[0] + bias[0]).astype(bf16)
    delta0, saved0 = forward_layer(normed0, weights[0], ctx)
    x1 = x0 + delta0 + bias_f[0]
    xhat1, inv1 = stats(x1)
    normed1 = gather_tokens((xhat1 * gain[1] + bias[1]).astype(bf16))
    delta1, saved1 = forward_layer(normed1, weights[1], ctx)
    mixed_out = (x1 + delta1 + bias_f[1]).astype(bf16)

    g2 = cotangent[0].astype(f32)
    g1, grads1 = backward_layer(g2, gr_top, weights[1], saved1, gain[1], xhat1, inv1, ctx)
    out1 = reduce_layer(grads1)
    gr1 = gather_tokens(g1.astype(bf16))
    xhat0, inv0 = stats(x0)
    g0, grads0 = backward_layer(g1, gr1, weights[0], saved0, gain[0], xhat0, inv0, ctx)
    out0 = reduce_layer(grads0)
    o_q, o_i, o_f, o_o, o_bi, o_g, o_s, o_bf = [jnp.stack([a, b]) for a, b in zip(out0, out1)]
    return mixed_out[None], g0[None], o_g, o_s, o_q, o_o, o_i, o_bi, o_f, o_bf


def solution(mesh):
    fine = Mesh(mesh.devices.reshape(2, 4, 2, 4, 2), AXES)
    seq = ("xh", "y", "core")
    tok = P(FS, seq, None)
    two = P(None, FS)
    three = P(None, FS, None)
    in_specs = (tok, P(FS, None), two, two, three, three, three, two, three, two, tok)
    out_specs = (tok, tok, two, two, three, three, three, two, three, two)
    return jax.shard_map(body, mesh=fine, in_specs=in_specs, out_specs=out_specs, check_vma=False)
```

```python
import functools
import jax
import jax.numpy as jnp
from jax import lax
from jax.experimental import pallas as pl
from jax.experimental.pallas import tpu as pltpu
from jax.sharding import Mesh, PartitionSpec as P

ROT = 32
CONTS = 8
D = 1024
HALF = 1024
BLK = 128
QB = 256
AXES = ("xh", "y", "core", "z", "xl")
FS = ("z", "xl")
f32 = jnp.float32
bf16 = jnp.bfloat16
NT = (((1,), (1,)), ((), ()))
VM = pl.BlockSpec(memory_space=pltpu.VMEM)
SM = pl.BlockSpec(memory_space=pltpu.SMEM)
ANY = pl.BlockSpec(memory_space=pl.ANY)
HBM = pl.BlockSpec(memory_space=pltpu.HBM)
MB = 1024 * 1024


def sds(*args):
    return [jax.ShapeDtypeStruct(s, t) for s, t in args]


class Far:
    def __init__(self, ref, copy):
        self.ref, self.copy = ref, copy

    def here(self):
        if self.copy is not None:
            self.copy.wait()
            self.copy = None
        return self.ref

    def __getitem__(self, index):
        return self.here()[index]

    @property
    def shape(self):
        return self.ref.shape


class Out:
    def __init__(self, ref, copy):
        self.ref, self.copy, self.sent = ref, copy, False

    def __getitem__(self, index):
        return self.ref[index]

    def __setitem__(self, index, value):
        self.ref[index] = value

    @property
    def dtype(self):
        return self.ref.dtype

    @property
    def shape(self):
        return self.ref.shape

    def send(self):
        self.copy.start()
        self.sent = True


COST = 0.001
LIMIT = 51


def call(kernel, name, outs, args, us, scratch=(), limit=None, after=(), raw=(), vm=(), out_raw=(), out_vm=(), alias=None):
    n, m = len(args), len(outs)
    fetched = [i for i in range(1, n) if i not in raw and i not in vm]
    staged = [i for i in range(m) if i not in out_raw and i not in out_vm]

    def run(*refs):
        ins = list(refs[:n])
        results = list(refs[n + len(after) : n + len(after) + m])
        rest = list(refs[n + len(after) + m :])
        own, rest = rest[: len(scratch)], rest[len(scratch) :]
        sems = rest[-1]
        copies = []
        for k, i in enumerate(fetched):
            copy = pltpu.make_async_copy(ins[i], rest[k], sems.at[k])
            copies.append(copy)
            ins[i] = Far(rest[k], copy)
        for copy in copies:
            copy.start()
        for k, i in enumerate(staged):
            ref = rest[len(fetched) + k]
            results[i] = Out(ref, pltpu.make_async_copy(ref, results[i], sems.at[len(fetched) + k]))
        kernel(*ins, *results, *own)
        for i in fetched:
            ins[i].here()
        for i in staged:
            if not results[i].sent:
                results[i].send()
        for i in staged:
            results[i].copy.wait()

    room = [pltpu.VMEM(args[i].shape, args[i].dtype) for i in fetched]
    room += [pltpu.VMEM(outs[i][0], outs[i][1]) for i in staged]
    return pl.pallas_call(
        run,
        out_shape=sds(*outs),
        in_specs=[SM] + [VM if i in vm else HBM for i in range(1, n)] + [ANY] * len(after),
        out_specs=[VM if i in out_vm else HBM for i in range(m)],
        scratch_shapes=list(scratch) + room + [pltpu.SemaphoreType.DMA((max(1, len(room)),))],
        input_output_aliases=alias or {},
        compiler_params=pltpu.CompilerParams(vmem_limit_bytes=(limit or LIMIT) * MB),
        cost_estimate=pl.CostEstimate(flops=int(us * COST * 1e9), bytes_accessed=int(us * COST * 1e6), transcendentals=0),
        name=name,
    )(*args, *after)


def dma(n):
    return pltpu.SemaphoreType.DMA((n,))


def copy_all(pairs, sems):
    copies = [pltpu.make_async_copy(a, b, sems.at[i]) for i, (a, b) in enumerate(pairs)]
    for copy in copies:
        copy.start()
    return copies


def wait_all(copies):
    for copy in copies:
        copy.wait()


def shift(x, axis, by, size):
    return lax.ppermute(x, axis, [(i, (i + by) % size) for i in range(size)])


def gather_blocks(own, hold=None):
    one = shift(own, "y", -1, 4)
    three = shift(own, "y", 1, 4)
    two = shift(own, "y", 2, 4)
    if hold is not None:
        one, two, three = hold(one, two, three)
    blocks = []
    for mine in (own, one, two, three):
        blocks += [mine, shift(mine, "core", 1, 2)]
    return blocks


def spread(low):
    return [shift(low[r - 1], "y", r, 4) for r in (1, 2, 3)]


def transpose_owner(x):
    pairs = [(j * 8 + f, f * 8 + j) for j in range(8) for f in range(8)]
    return lax.ppermute(x, ("y", "core", "z", "xl"), pairs)


def gate(ids, x, after):
    (out,) = call(lambda *refs: None, "gate", [(x.shape, x.dtype)], (ids, x), 1, raw=(1,), out_raw=(0,), after=after, alias={1: 0})
    return out


def gate_all(ids, xs, after):
    n = len(xs)
    return call(
        lambda *refs: None, "gate", [(x.shape, x.dtype) for x in xs], (ids, *xs), 1, raw=range(1, n + 1), out_raw=range(n),
        after=after, alias={i + 1: i for i in range(n)},
    )


def gather_fsdp(ids, x, got, after=()):
    (pair,) = call(
        pair_kernel, "pair", [((2,) + x.shape, bf16)], (ids, x, got), 2, [dma(2)], out_raw=(0,), after=after, limit=62,
    )
    return [pair, shift(pair, "z", -1, 4), shift(pair, "z", 2, 4), shift(pair, "z", 1, 4)]


def weight_copies(ids, pairs, cols, room):
    if len(pairs) == 1:
        return [(pairs[0].at[:, :, cols], room)]
    out = []
    for r in range(4):
        out.append((pairs[r].at[:, :, cols], room.at[pl.ds(2 * lax.rem(ids[4] + r, 4), 2)]))
    return out


def slot(ids, r, s):
    y = lax.rem(ids[0] + r, 4)
    c = ids[1] if s == 0 else 1 - ids[1]
    return y * 2 + c


def rows_of(ids, r, s, n=BLK):
    return pl.ds(pl.multiple_of(slot(ids, r, s) * n, n), n)


def turn(v, cosine, sine):
    lane = lax.broadcasted_iota(jnp.int32, v.shape, 1)
    partner = jnp.where(lane % 2 == 0, pltpu.roll(v, BLK - 1, 1), pltpu.roll(v, 1, 1))
    return v * cosine + partner * sine


def stats(x):
    average = jnp.mean(x, axis=-1, keepdims=True)
    centred = x - average
    variance = jnp.mean(centred * centred, axis=-1, keepdims=True)
    inv = lax.rsqrt(variance + 1e-05)
    return centred * inv, inv


def gelu_both(x):
    a = 0.7978845608028654
    b = 0.044715
    sq = x * x
    t = jnp.tanh(a * x * (1.0 + b * sq))
    half = 0.5 * (1.0 + t)
    slope = half + 0.5 * x * (1.0 - t * t) * a * (1.0 + 3.0 * b * sq)
    return x * half, slope


def dot(a, b):
    return jnp.dot(a, b, preferred_element_type=f32)


def dot_nt(a, b):
    return lax.dot_general(a, b, NT, preferred_element_type=f32)


def pack_q_kernel(ids, wq, gain, bias, bfc, bin_, q0, room, small, binv, sems, out_sems):
    j = ids[0] * 2 + ids[1]
    pairs = []
    for part in range(3):
        cols = pl.ds(pl.multiple_of(part * D + j * BLK, BLK), BLK)
        pairs.append((wq.at[0, :, cols], room.at[0:BLK, part * BLK : part * BLK + BLK]))
    pairs += [(ref, small.at[i]) for i, ref in enumerate((gain, bias, bfc))]
    pairs.append((bin_, binv))
    wait_all(copy_all(pairs, sems))
    chunk = binv[:, pl.ds(pl.multiple_of((j // 2) * BLK, BLK), BLK)].astype(f32)
    chunk = jnp.where(j % 2 == 1, pltpu.roll(chunk, 64, 1), chunk)
    lane = lax.broadcasted_iota(jnp.int32, (1, BLK), 1)
    row2 = jnp.where(lane < 64, chunk[0:1], pltpu.roll(chunk, 64, 1)[1:2])
    blank = jnp.zeros((13, BLK), f32)
    cols = [jnp.concatenate([small[i].astype(f32), row2, blank], 0) for i in range(3)]
    room[BLK:, :] = jnp.concatenate(cols, 1).astype(bf16)
    wait_all(copy_all([(room, q0.at[f]) for f in range(8)], out_sems))


def pack_layer(layer, ids, wi, wf, out, chunks, sems, more=()):
    j = ids[0] * 2 + ids[1]
    rows = pl.ds(pl.multiple_of(j * 64, 64), 64)
    pairs = []
    for f in range(8):
        cols = pl.ds(pl.multiple_of(f * 512 + (j // 2) * BLK, BLK), BLK)
        pairs.append((wi.at[layer, :, cols], chunks.at[f]))
    pairs.append((wf.at[layer, rows, 0:512], out.ref.at[0:64, 512:1024]))
    pairs.append((wf.at[layer, rows, 512:1024], out.ref.at[64:128, 512:1024]))
    wait_all(copy_all(pairs + list(more), sems))
    lane = lax.broadcasted_iota(jnp.int32, (BLK, BLK), 1)
    odd = j % 2 == 1
    for pair in range(4):
        a = chunks[2 * pair].astype(f32)
        b = chunks[2 * pair + 1].astype(f32)
        first = jnp.where(odd, pltpu.roll(a, 64, 1), a)
        second = jnp.where(odd, b, pltpu.roll(b, 64, 1))
        out[:, pair * BLK : pair * BLK + BLK] = jnp.where(lane < 64, first, second).astype(bf16)


def pack_first_kernel(ids, wi, wf, out, chunks, sems):
    pack_layer(0, ids, wi, wf, out, chunks, sems)


def pack_second_kernel(ids, wi, wf, wq, out, chunks, sems):
    j = ids[0] * 2 + ids[1]
    more = []
    for part in range(3):
        cols = pl.ds(pl.multiple_of(part * D + j * BLK, BLK), BLK)
        more.append((wq.at[1, :, cols], out.ref.at[:, D + part * BLK : D + part * BLK + BLK]))
    pack_layer(1, ids, wi, wf, out, chunks, sems, more)


def pass_kernel(layer, ids, x, out, sems):
    wait_all(copy_all([(x.at[layer], out.ref)], sems))


def join_kernel(ids, a, b, out, sems):
    wait_all(copy_all([(a, out.ref.at[0:BLK]), (b, out.ref.at[BLK : 2 * BLK])], sems))


def pair_kernel(ids, own, got, out, sems):
    xl = ids[3]
    wait_all(copy_all([(own.here(), out.at[xl]), (got.here(), out.at[1 - xl])], sems))


def four_kernel(ids, own, got, out, sems):
    xl = ids[3]
    mine, other = own.here(), got.here()
    wait_all(copy_all([(src, out.at[z, at]) for z in range(4) for src, at in ((mine, xl), (other, 1 - xl))], sems))


def params_part(rows_of_f, gain, bias, bfc, bi):
    lane = lax.broadcasted_iota(jnp.int32, (1, BLK), 1)
    for f in range(8):
        cols = slice(f * BLK, f * BLK + BLK)
        rows = rows_of_f[f].astype(f32)
        gain[:, cols] = rows[0:2, 0:BLK]
        bias[:, cols] = rows[0:2, BLK : 2 * BLK]
        bfc[:, cols] = rows[0:2, 2 * BLK :]
    for pair in range(4):
        a = rows_of_f[2 * pair].astype(f32)[2:3, :BLK]
        b = rows_of_f[2 * pair + 1].astype(f32)[2:3, :BLK]
        cols = slice(pair * BLK, pair * BLK + BLK)
        bi[0:1, cols] = jnp.where(lane < 64, a, pltpu.roll(b, 64, 1))
        bi[1:2, cols] = jnp.where(lane < 64, pltpu.roll(a, 64, 1), b)


def qkv_part(normed, w, cosine, sine, q, kv):
    for i in range(HALF // QB):
        rows = slice(i * QB, i * QB + QB)
        out = dot(normed[rows, :], w).astype(bf16).astype(f32)
        cb = cosine[rows, :]
        sb = sine[rows, :]
        kv[rows, :BLK] = turn(out[:, BLK : 2 * BLK], cb, sb).astype(bf16)
        kv[rows, BLK:] = out[:, 2 * BLK :].astype(bf16)
        q[rows, :] = (turn(out[:, :BLK], cb, sb).astype(bf16).astype(f32) * 0.125).astype(bf16)


def take_blocks(ids, blocks, room, sems, at=0):
    part = slice(at, at + BLK)
    return copy_all([(blocks[2 * r + s].at[part], room.at[rows_of(ids, r, s)]) for r in range(4) for s in range(2)], sems)


def qkv_first_kernel(ids, *refs):
    blocks, (wq, cosine, sine), refs = refs[:8], refs[8:11], refs[11:]
    normed, xhat, q, kv, gain, bias, bfc, bi, raw, sems = refs
    copies = take_blocks(ids, blocks, raw, sems)
    w = wq.here()
    params_part([w[f, BLK:, :] for f in range(8)], gain, bias, bfc, bi)
    wait_all(copies)
    for i in range(HALF // QB):
        rows = slice(i * QB, i * QB + QB)
        x, _ = stats(raw[rows, :].astype(f32))
        xhat[rows, :] = x.astype(bf16)
        normed[rows, :] = (x * gain[0:1, :] + bias[0:1, :]).astype(bf16)
    xhat.send()
    normed.send()
    qkv_part(normed, w[:, :BLK, :].reshape(D, 384), cosine, sine, q, kv)


def qkv_kernel(ids, *refs):
    blocks, w, (cosine, sine), (normed, q, kv, wq, sems, wsem) = refs[:8], refs[8:9], refs[9:11], refs[11:]
    copies = copy_all(weight_copies(ids, w, slice(1024, 1408), wq), wsem)
    copies += take_blocks(ids, blocks, normed.ref, sems)
    wait_all(copies)
    normed.send()
    qkv_part(normed, wq[...].reshape(D, 384), cosine, sine, q, kv)


def ff_kernel(layer, ids, normed, bi, *refs):
    w, (active, slope, feed, wi, wf, va, vs, vf, wsems, sems) = refs[:-10], refs[-10:]
    copies = copy_all(weight_copies(ids, w, slice(0, 512), wi), wsems.at[0])
    late = copy_all(weight_copies(ids, w, slice(512, 1024), wf), wsems.at[1])
    normed.here()
    wait_all(copies)
    left = right = None
    sent = []
    for i in range(HALF // QB):
        rows = slice(i * QB, i * QB + QB)
        pre = dot(normed[rows, :], wi[...].reshape(D, 512)) + bi[layer : layer + 1, :]
        act, der = gelu_both(pre)
        act = act.astype(bf16)
        va[rows, :] = act
        vs[rows, :] = der.astype(bf16)
        if i == 0:
            wait_all(late)
            left, right = wf[:, 0:64, :].reshape(512, 512), wf[:, 64:128, :].reshape(512, 512)
        vf[rows, :512] = dot(act, left).astype(bf16)
        vf[rows, 512:] = dot(act, right).astype(bf16)
        pairs = [(v.at[rows], out.at[rows]) for v, out in ((va, active), (vs, slope), (vf, feed))]
        sent += copy_all(pairs, sems.at[i])
    wait_all(sent)


def ff(ids, layer, normed, w, bi):
    room = lambda *shape: pltpu.VMEM(shape, bf16)
    return call(
        functools.partial(ff_kernel, layer), "ff", [((HALF, 512), bf16), ((HALF, 512), bf16), ((HALF, D), bf16)],
        (ids, normed, bi, *w), 5,
        [room(8, BLK, 512), room(8, BLK, 512), room(HALF, 512), room(HALF, 512), room(HALF, D),
         pltpu.SemaphoreType.DMA((2, 4)), pltpu.SemaphoreType.DMA((4, 3))],
        raw=range(3, 3 + len(w)), out_raw=(0, 1, 2), limit=62 - 11 * layer,
    )


def head_cut(x):
    lane = lax.broadcasted_iota(jnp.int32, x.shape, 1)
    zero = jnp.zeros((), x.dtype)
    return [jnp.where(lane < 64, x, zero), jnp.where(lane >= 64, x, zero)]


def seen(i, kk, qseg, kseg):
    q0 = i * QB
    qs = qseg[0:1, q0 : q0 + QB]
    ks = kseg[0:kk, 0:1]
    key = lax.broadcasted_iota(jnp.int32, (kk, QB), 0)
    query = q0 + lax.broadcasted_iota(jnp.int32, (kk, QB), 1)
    return (key <= query) & ((ks == 0) | (ks == qs))


def flip(x):
    return jnp.transpose(x.astype(f32)).astype(bf16)


def attn_own_kernel(ids, q, kv, qseg, acc, m_out, l_out):
    qseg = qseg[...]
    kseg = jnp.transpose(qseg)
    km = head_cut(kv[:, :BLK])
    vt = flip(kv[:, BLK:])
    for i in range(HALF // QB):
        cols = slice(i * QB, (i + 1) * QB)
        kk = (i + 1) * QB
        allowed = seen(i, kk, qseg, kseg)
        for h in range(2):
            rows = slice(h * 64, h * 64 + 64)
            s = jnp.where(allowed, dot_nt(km[h][:kk], q[cols, :]), -1e30)
            m = jnp.max(s, axis=0, keepdims=True)
            p = jnp.exp(s - m)
            l_out[h : h + 1, cols] = jnp.sum(p, axis=0, keepdims=True)
            m_out[h : h + 1, cols] = m
            acc[rows, cols] = dot(vt[rows, :kk], p.astype(bf16))


def split_rows(ids, mine, away, block):
    for r in range(4):
        away[r] = block(rows_of(ids, r, 1)).astype(bf16)
    away.send()
    for r in range(4):
        mine[r] = block(rows_of(ids, r, 0)).astype(bf16)


def attn_full_kernel(ids, q, kv0, acc, m_in, l_in, feed, wo, attn, lse, mine, away, tmp):
    upper = ids[2] == 1
    for ref in (q, kv0, acc, m_in, l_in):
        ref.here()

    @pl.when(upper)
    def _():
        km = head_cut(kv0[:, :BLK])
        vt = flip(kv0[:, BLK:])
        for i in range(HALF // QB):
            cols = slice(i * QB, (i + 1) * QB)
            for h in range(2):
                rows = slice(h * 64, h * 64 + 64)
                s = dot_nt(km[h], q[cols, :])
                m0 = m_in[h : h + 1, cols]
                m = jnp.maximum(m0, jnp.max(s, axis=0, keepdims=True))
                p = jnp.exp(s - m)
                a = jnp.exp(m0 - m)
                l = l_in[h : h + 1, cols] * a + jnp.sum(p, axis=0, keepdims=True)
                o = dot(vt[rows, :], p.astype(bf16))
                tmp[rows, cols] = (acc[rows, cols] * a + o) / l
                lse[h : h + 1, cols] = m + jnp.log(l)

    @pl.when(jnp.logical_not(upper))
    def _():
        for h in range(2):
            rows = slice(h * 64, h * 64 + 64)
            l = l_in[h : h + 1, :]
            tmp[rows, :] = acc[rows, :] / l
            lse[h : h + 1, :] = m_in[h : h + 1, :] + jnp.log(l)

    attn[...] = jnp.transpose(tmp[...]).astype(bf16)
    attn.send()
    lse.send()
    split_rows(ids, mine, away, lambda rows: feed[rows, :].astype(f32) + dot(attn[rows, :], wo[...]))


def mid_kernel(ids, mine, got, total, one, two, three):
    for r, out in ((1, one), (2, two), (3, three)):
        out[...] = (mine[r].astype(f32) + got[r].astype(f32)).astype(bf16)
    total[...] = mine[0].astype(f32) + got[0].astype(f32)


def summed(total, one, two, three):
    return total[...] + one[...].astype(f32) + two[...].astype(f32) + three[...].astype(f32)


def fwd_end_kernel(ids, total, one, two, three, x, gain, bias, bfc, x_new, normed):
    new = x[...].astype(f32) + summed(total, one, two, three) + bfc[0:1, :]
    x_new[...] = new
    xhat, _ = stats(new)
    normed[...] = (xhat * gain[1:2, :] + bias[1:2, :]).astype(bf16)


def last_end_kernel(ids, total, one, two, three, x, bfc, out):
    out[...] = (x[...] + summed(total, one, two, three) + bfc[1:2, :]).astype(bf16)


def grad_in_kernel(at, ids, *refs):
    blocks, (wo, gr, dattn, sems) = refs[:8], refs[8:]
    wait_all(take_blocks(ids, blocks, gr.ref, sems, at))
    gr.send()
    dattn[...] = dot_nt(gr[...], wo[...]).astype(bf16)


def row_delta(attn, do):
    prod = attn[...].astype(f32) * do[...].astype(f32)
    head = lax.broadcasted_iota(jnp.int32, (8, BLK), 0)
    lane = lax.broadcasted_iota(jnp.int32, (8, BLK), 1) // 64
    pickers = jnp.where(head == lane, 1.0, 0.0).astype(f32)
    return lax.dot_general(pickers, prod, NT, precision=lax.Precision.HIGHEST, preferred_element_type=f32)


def grad_block(km, vm, kt, qm, dom, q_blk, do_blk, lse, delta, allowed):
    p = jnp.exp(dot_nt(km, q_blk) - lse)
    if allowed is not None:
        p = jnp.where(allowed, p, 0.0)
    dp = dot_nt(vm, do_blk)
    ds = (p * (dp - delta)).astype(bf16)
    return dot(kt, ds), dot(ds, qm), dot(p.astype(bf16), dom)


def grad_full_kernel(ids, q, kv0, do, attn, lse, dqt, dkv, acck, accv):
    upper = ids[2] == 1
    for ref in (q, kv0, do, attn, lse):
        ref.here()

    @pl.when(upper)
    def _():
        delta = row_delta(attn, do)
        qm, km, vm, dom = [head_cut(x) for x in (q[...], kv0[:, :BLK], kv0[:, BLK:], do[...])]
        kt = flip(kv0[:, :BLK])
        for i in range(HALF // QB):
            cols = slice(i * QB, (i + 1) * QB)
            for h in range(2):
                rows = slice(h * 64, h * 64 + 64)
                dq, dk, dv = grad_block(
                    km[h], vm[h], kt[rows, :], qm[h][cols], dom[h][cols], q[cols, :], do[cols, :],
                    lse[h : h + 1, cols], delta[h : h + 1, cols], None,
                )
                dqt[rows, cols] = dq
                if i == 0 and h == 0:
                    acck[...] = dk
                    accv[...] = dv
                else:
                    acck[...] += dk
                    accv[...] += dv
        dkv[:, :BLK] = acck[...].astype(bf16)
        dkv[:, BLK:] = accv[...].astype(bf16)

    @pl.when(jnp.logical_not(upper))
    def _():
        dqt[...] = jnp.zeros(dqt.shape, f32)
        dkv[...] = jnp.zeros(dkv.shape, bf16)


def grad_own_kernel(ids, q, kv, do, attn, lse, qseg, dqt0, dq_out, dk_out, dv_out, tmp):
    qseg = qseg[...]
    kseg = jnp.transpose(qseg)
    delta = row_delta(attn, do)
    qm, km, vm, dom = [head_cut(x) for x in (q[...], kv[:, :BLK], kv[:, BLK:], do[...])]
    kt = flip(kv[:, :BLK])
    dk_out[...] = jnp.zeros(dk_out.shape, f32)
    dv_out[...] = jnp.zeros(dv_out.shape, f32)
    for i in range(HALF // QB):
        cols = slice(i * QB, (i + 1) * QB)
        kk = (i + 1) * QB
        allowed = seen(i, kk, qseg, kseg)
        for h in range(2):
            rows = slice(h * 64, h * 64 + 64)
            dq, dk, dv = grad_block(
                km[h][:kk], vm[h][:kk], kt[rows, :kk], qm[h][cols], dom[h][cols], q[cols, :], do[cols, :],
                lse[h : h + 1, cols], delta[h : h + 1, cols], allowed,
            )
            tmp[rows, cols] = (dq + dqt0[rows, cols]) * 0.125
            dk_out[:kk, :] += dk
            dv_out[:kk, :] += dv
    dq_out[...] = jnp.transpose(tmp[...])


def ff_back_outer_kernel(ids, gr, slope, active, attn, normed, *refs):
    w, (part, dbi, out, wi, wf, vd, v, wsems, sems) = refs[:-9], refs[-9:]
    copies = copy_all(weight_copies(ids, w, slice(512, 1024), wf), wsems.at[0])
    late = copy_all(weight_copies(ids, w, slice(0, 512), wi), wsems.at[1])
    gr.here()
    slope.here()
    wait_all(copies)
    left, right = wf[:, 0:64, :].reshape(512, 512), wf[:, 64:128, :].reshape(512, 512)
    total = jnp.zeros((1, 512), f32)
    for i in range(HALF // QB):
        rows = slice(i * QB, i * QB + QB)
        d = (dot_nt(gr[rows, :512], left) + dot_nt(gr[rows, 512:], right)) * slope[rows, :].astype(f32)
        total = total + jnp.sum(d, axis=0, keepdims=True)
        d = d.astype(bf16)
        vd[rows, :] = d
        if i == 0:
            wait_all(late)
        part[rows, :] = dot_nt(d, wi[...].reshape(D, 512)).astype(bf16)
    part.send()
    dbi[...] = jnp.concatenate([total, jnp.zeros((7, 512), f32)], 0)
    wait_all(outer_rows(out, v, sems, active, gr, attn, normed, vd))


def ff_back_outer(ids, rows, gr, slope, active, attn, normed, w, after):
    room = lambda *shape: pltpu.VMEM(shape, bf16)
    return call(
        ff_back_outer_kernel, "ff_back_outer", [((HALF, D), bf16), ((8, 512), f32), ((8, rows, 512), bf16)],
        (ids, gr, slope, active, attn, normed, *w), 9,
        [room(8, BLK, 512), room(8, BLK, 512), room(HALF, 512), room(8, 288, 512), pltpu.SemaphoreType.DMA((2, 4)),
         pltpu.SemaphoreType.DMA((3, 2))],
        raw=range(6, 6 + len(w)), out_raw=(2,), after=after,
    )


def combine_rows(ids, dq, dk, dv, back, cosine, sine, dqkv):
    cb = cosine[...]
    sb = -sine[...]
    dqkv[:, :BLK] = turn(dq[...], cb, sb).astype(bf16)
    dqkv[:, BLK : 2 * BLK] = turn(dk[...] + back[:, :BLK].astype(f32), cb, sb).astype(bf16)
    dqkv[:, 2 * BLK :] = (dv[...] + back[:, BLK:].astype(f32)).astype(bf16)


def combine_kernel(ids, dq, dk, dv, back, cosine, sine, part, w1, normed, _, mine, away, payload, dqkv, out, wq, wsem):
    copies = copy_all(weight_copies(ids, (w1,), slice(1024, 1408), wq), wsem)
    combine_rows(ids, dq, dk, dv, back, cosine, sine, dqkv)
    wait_all(copies)
    w = wq[...].reshape(D, 384)
    split_rows(ids, mine, away, lambda rows: part[rows, :].astype(f32) + dot_nt(dqkv[rows, :], w))
    mine.send()
    g_q = outer(normed[...], dqkv[...])
    for f in range(8):
        pack_rows(out, f, g_q)
    wait_all(copy_all([(out, payload.at[:, 288:384])], wsem))


def combine_first_kernel(ids, dq, dk, dv, back, cosine, sine, part, wq0, xhat, normed, sums1, dbi0, dbi1, *refs):
    _, mine, away, payload, dqkv, out, sems = refs
    combine_rows(ids, dq, dk, dv, back, cosine, sine, dqkv)
    w = wq0[:, :BLK, :].reshape(D, 384)
    gain = jnp.zeros((1, D), f32)
    base = jnp.zeros((1, D), f32)
    for s, to in ((1, away), (0, mine)):
        for r in range(4):
            rows = rows_of(ids, r, s)
            block = part[rows, :].astype(f32) + dot_nt(dqkv[rows, :], w)
            to[r] = block.astype(bf16)
            gain = gain + jnp.sum(block * xhat[rows, :].astype(f32), axis=0, keepdims=True)
            base = base + jnp.sum(block, axis=0, keepdims=True)
        to.send()
    g_q = outer(normed[...], dqkv[...])
    lane = lax.broadcasted_iota(jnp.int32, (1, BLK), 1)
    blank = jnp.zeros((13, 384), f32)
    none = jnp.zeros((1, 256), f32)
    for f in range(8):
        pack_rows(out, f, g_q)
        cols = slice(f * BLK, f * BLK + BLK)
        row0 = jnp.concatenate([gain[:, cols], base[:, cols], sums1[3:4, cols]], 1)
        row1 = jnp.concatenate([sums1[0:1, cols], sums1[1:2, cols], sums1[2:3, cols]], 1)
        half = slice((f // 2) * BLK, (f // 2) * BLK + BLK)
        a = dbi0[0:1, half]
        b = dbi1[0:1, half]
        if f % 2 == 0:
            b = pltpu.roll(b, 64, 1)
        else:
            a = pltpu.roll(a, 64, 1)
        row2 = jnp.concatenate([jnp.where(lane < 64, a, b), none], 1)
        out[f, 96:112, :384] = jnp.concatenate([row0, row1, row2, blank], 0).astype(bf16)
        out[f, 96:112, 384:] = jnp.zeros((16, 128), bf16)
    wait_all(copy_all([(out, payload.at[:, 288:400])], sems))


def norm_back(dn, x, gain_row, g):
    xhat, inv = stats(x[...].astype(f32))
    dx = dn * gain_row
    dx = inv * (dx - jnp.mean(dx, -1, keepdims=True) - xhat * jnp.mean(dx * xhat, -1, keepdims=True))
    return xhat, g[...].astype(f32) + dx


def bwd_end_kernel(ids, total, one, two, three, x, gain, g, g_new, gr, sums):
    dn = summed(total, one, two, three)
    xhat, new = norm_back(dn, x, gain[1:2, :], g)
    g_new[...] = new
    gr[...] = new.astype(bf16)
    col = lambda v: jnp.sum(v, axis=0, keepdims=True)
    top = col(g[...].astype(f32))
    sums[...] = jnp.concatenate([col(dn * xhat), col(dn), top, col(new), jnp.zeros((4, D), f32)], 0)


def bwd_last_kernel(ids, total, one, two, three, x, gain, g, g_new):
    _, new = norm_back(summed(total, one, two, three), x, gain[0:1, :], g)
    g_new[...] = new


def outer(a, b):
    return lax.dot_general(a, b, (((0,), (0,)), ((), ())), preferred_element_type=f32).astype(bf16)


def pack_rows(out, f, g_q):
    for part in range(3):
        for group in range(4):
            piece = g_q[f * 128 + group * 32 : f * 128 + group * 32 + 32, part * BLK : part * BLK + BLK]
            out[f, part * 32 : part * 32 + 32, group * BLK : group * BLK + BLK] = piece


def outer_rows(out, v, sems, active, gr, attn, normed, dpre):
    for half in range(2):
        cols = slice(half * 512, half * 512 + 512)
        g_f = outer(active[...], gr[:, cols])
        g_o = outer(attn[...], gr[:, cols])
        for f in range(8):
            v[f, 128 + 64 * half : 192 + 64 * half, :] = g_f[f * 64 : f * 64 + 64]
            v[f, 256 + 16 * half : 272 + 16 * half, :] = g_o[f * 16 : f * 16 + 16]
    first = copy_all([(v.at[:, 128:288], out.at[:, 128:288])], sems.at[0])
    for half in range(2):
        cols = slice(half * 512, half * 512 + 512)
        g_i = outer(normed[:, cols], dpre[...])
        for k in range(4):
            v[4 * half + k, 0:128, :] = g_i[k * 128 : k * 128 + 128]
        group = slice(4 * half, 4 * half + 4)
        first += copy_all([(v.at[group, 0:128], out.at[group, 0:128])], sems.at[1 + half])
    return first


def fsum_kernel(ids, *refs):
    gots, (low, piece) = refs[:-2], refs[-2:]
    at = 0
    for got in gots:
        rows, cols = got.shape[1:]
        for start in range(0, rows, 16):
            part = slice(start, start + 16)
            total = got[0, part, :].astype(f32)
            for f in range(1, 8):
                total = total + got[f, part, :].astype(f32)
            total = total.astype(bf16)
            if 256 <= at < 288:
                piece[at - 256 : at - 240, :] = total
            else:
                to = at if at < 256 else at - 32
                low[to : to + 16, :cols] = total
                if cols < 512:
                    low[to : to + 16, cols:] = jnp.zeros((16, 512 - cols), bf16)
            at += 16


def add_rows(terms, start, stop):
    total = terms[0][start:stop, :].astype(f32)
    for term in terms[1:]:
        total = total + term[start:stop, :].astype(f32)
    return total.astype(bf16)


def xsum_top_kernel(ids, low, got, main):
    main[...] = add_rows((low, got), 0, 352)


def xsum_last_kernel(ids, low, got, p0, p0_other, p1, p1_other, main):
    terms = (low, got)
    main[0:112, :] = add_rows(terms, 256, 368)
    main[112:368, :] = add_rows(terms, 0, 256)
    main[368:400, :] = add_rows((p0, p0_other), 0, 32)
    main[400:432, :] = add_rows((p1, p1_other), 0, 32)


def over_groups(ids, name, gots, after=()):
    rows = sum(got.shape[1] for got in gots)
    low, piece = call(fsum_kernel, name, [((rows - 32, 512), bf16), ((32, 512), bf16)], (ids, *gots), 3, after=after)
    return low, transpose_owner(piece)


def by_core(ids, mine, other):
    return jnp.where(ids[1] == 0, mine, other), jnp.where(ids[1] == 0, other, mine)


def place_in(ids, mine, other, y, at, o_i, o_f):
    lane = lax.broadcasted_iota(jnp.int32, (BLK, BLK), 1)
    for half in range(2):
        rows = slice(at + 128 + 64 * half, at + 192 + 64 * half)
        zero, one = by_core(ids, mine[y, rows, :], other[y, rows, :])
        cols = slice(half * 512, half * 512 + 512)
        o_f[y * BLK : y * BLK + 64, cols] = zero.astype(f32)
        o_f[y * BLK + 64 : y * BLK + BLK, cols] = one.astype(f32)
    for pair in range(4):
        cols = slice(pair * BLK, pair * BLK + BLK)
        a, b = by_core(ids, mine[y, at : at + BLK, cols].astype(f32), other[y, at : at + BLK, cols].astype(f32))
        even = 2 * pair * 512 + y * BLK
        o_i[:, even : even + BLK] = jnp.where(lane < 64, a, pltpu.roll(b, 64, 1))
        odd = even + 512
        o_i[:, odd : odd + BLK] = jnp.where(lane < 64, pltpu.roll(a, 64, 1), b)


def place_q(ids, mine, other, y, at, o_q):
    for part in range(3):
        rows = slice(at + part * 32, at + part * 32 + 32)
        start = part * D + 2 * y * BLK
        for group in range(4):
            cols = slice(group * BLK, group * BLK + BLK)
            zero, one = by_core(ids, mine[y, rows, cols], other[y, rows, cols])
            to = slice(group * 32, group * 32 + 32)
            o_q[to, start : start + BLK] = zero.astype(f32)
            o_q[to, start + BLK : start + 2 * BLK] = one.astype(f32)


def fetch_rows(ids, blocks, room_a, room_b, sems):
    pairs = []
    for r in range(4):
        y = lax.rem(ids[0] + r, 4)
        pairs += [(blocks[2 * r], room_a.at[y]), (blocks[2 * r + 1], room_b.at[y])]
    wait_all(copy_all(pairs, sems))


def assemble_top_kernel(ids, *refs):
    blocks, (o_i, o_f, o_q, vi, vf, vq, ra, rb, sems, out_sems) = refs[:8], refs[8:]
    fetch_rows(ids, blocks, ra, rb, sems)
    for y in range(4):
        place_in(ids, ra, rb, y, 0, vi, vf)
        place_q(ids, ra, rb, y, 256, vq)
    outs = copy_all([(vi, o_i.at[1]), (vf, o_f.at[1]), (vq, o_q.at[1])], out_sems)
    wait_all(outs)


def finish_kernel(ids, *refs):
    blocks, refs = refs[:8], refs[11:]
    o_i, o_f, o_q, o_o, o_g, o_s, o_bf, o_bi, vi, vf, vq, ra, rb, sems, out_sems = refs
    fetch_rows(ids, blocks, ra, rb, sems)
    total = jnp.zeros((16, 384), f32)
    lane = lax.broadcasted_iota(jnp.int32, (1, BLK), 1)
    for y in range(4):
        place_q(ids, ra, rb, y, 0, vq)
        place_in(ids, ra, rb, y, 112, vi, vf)
    outs = copy_all([(vi, o_i.at[0]), (vf, o_f.at[0]), (vq, o_q.at[0])], out_sems)
    for y in range(4):
        for layer in range(2):
            for half in range(2):
                at = 368 + 32 * layer + 16 * half
                zero, one = by_core(ids, ra[y, at : at + 16, :], rb[y, at : at + 16, :])
                cols = slice(half * 512, half * 512 + 512)
                o_o[layer, 32 * y : 32 * y + 16, cols] = zero.astype(f32)
                o_o[layer, 32 * y + 16 : 32 * y + 32, cols] = one.astype(f32)
        zero, one = by_core(ids, ra[y, 96:112, :384].astype(f32), rb[y, 96:112, :384].astype(f32))
        total = total + zero + one
        a, b = zero[2:3, :BLK], one[2:3, :BLK]
        cols = slice(y * BLK, y * BLK + BLK)
        o_bi[0:1, cols] = jnp.where(lane < 64, a, pltpu.roll(b, 64, 1))
        o_bi[1:2, cols] = jnp.where(lane < 64, pltpu.roll(a, 64, 1), b)
    o_g[...] = total[0:2, :BLK]
    o_s[...] = total[0:2, BLK : 2 * BLK]
    o_bf[...] = total[0:2, 2 * BLK :]
    wait_all(outs)


def positions_of(group_seg):
    token_index = jnp.arange(group_seg.shape[0], dtype=jnp.int32)
    labels = jnp.arange(CONTS + 1, dtype=jnp.int32)
    member = (group_seg[:, None] == labels[None, :]).astype(jnp.int32)
    counts = jnp.sum(member, axis=0)
    starts = jnp.cumsum(counts) - counts
    own_start = jnp.sum(member * starts[None, :], axis=1)
    return token_index - own_start + jnp.where(group_seg > 0, counts[0], 0)


def rope_tables(positions):
    lane = jnp.arange(BLK, dtype=jnp.int32) % 64
    inverse = 10000.0 ** (-2.0 * (lane // 2).astype(f32) / ROT)
    phase = positions.astype(f32)[:, None] * jnp.where(lane < ROT, inverse, 0.0)[None, :]
    sign = jnp.where(lane % 2 == 0, -1.0, 1.0)
    return jnp.cos(phase), jnp.sin(phase) * sign[None, :]


def scatter(ids, mine, away):
    got = shift(away, "core", 1, 2)
    blk = (BLK, D)
    total, one, two, three = call(
        mid_kernel, "rs_mid", [(blk, f32)] + [(blk, bf16)] * 3, (ids, mine, got), 2, vm=(2,), out_vm=(0, 1, 2, 3), limit=8
    )
    return [total] + spread([one, two, three]), one


def grad_in(ids, g_blocks, wo, at):
    return call(
        functools.partial(grad_in_kernel, at), "grad_in", [((HALF, D), bf16), ((HALF, BLK), bf16)], (ids, *g_blocks, wo), 3,
        [dma(8)], raw=range(1, 9),
    )


def body(tokens, segment, ln_gain, ln_bias, w_qkv, w_out, w_in, b_in, w_fc, b_fc, cotangent):
    xh = lax.axis_index("xh")
    ids = jnp.stack([lax.axis_index("y"), lax.axis_index("core"), xh, lax.axis_index("xl"), lax.axis_index("z")]).astype(jnp.int32)
    own = tokens[0]
    full = (HALF, D)
    blk = (BLK, D)
    head = (HALF, BLK)
    room = lambda shape, kind=f32: pltpu.VMEM(shape, kind)
    chunks = [room((8, BLK, BLK), bf16)]

    group_seg = segment[0]
    positions = positions_of(group_seg)
    seg = lax.dynamic_slice_in_dim(group_seg, xh * HALF, HALF, 0)
    cosine, sine = rope_tables(lax.dynamic_slice_in_dim(positions, xh * HALF, HALF, 0))
    qseg = jnp.broadcast_to(seg[None, :].astype(f32), (8, HALF))

    (both,) = call(
        join_kernel, "join", [((2 * BLK, D), bf16)], (ids, own, cotangent[0]), 1, [dma(2)], raw=(1, 2), limit=62
    )
    (p0,) = call(
        pack_first_kernel, "pack_first", [(blk, bf16)], (ids, w_in, w_fc), 3, chunks + [dma(10)], raw=(1, 2), limit=62, after=(both,),
    )
    other0 = shift(p0, "xl", 1, 2)
    (q0,) = call(
        pack_q_kernel, "pack_q", [((8, 144, 384), bf16)], (ids, w_qkv, ln_gain, ln_bias, b_fc, b_in), 3,
        [room((144, 384), bf16), room((3, 2, BLK), bf16), room((2, 512), bf16), dma(7), dma(8)],
        raw=(1, 2, 3, 4, 5), out_raw=(0,), after=(cosine, other0), limit=62,
    )
    wq0 = lax.all_to_all(q0, FS, 0, 0, tiled=True)
    (p1,) = call(
        pack_second_kernel, "pack_second", [((BLK, 1408), bf16)], (ids, w_in, w_fc, w_qkv), 3, chunks + [dma(13)], raw=(1, 2, 3), limit=62,
        after=(wq0,),
    )
    tok_blocks = gather_blocks(both, lambda *x: gate_all(ids, x, (q0,)))
    w0 = gather_fsdp(ids, p0, other0)

    def attend_own(layer, q, kv, normed, w):
        kv0 = lax.ppermute(kv, "xh", [(0, 1)])
        act = ff(ids, layer, normed, w, bi)
        own_part = call(
            attn_own_kernel, "attn_own", [((BLK, HALF), f32), ((2, HALF), f32), ((2, HALF), f32)], (ids, q, kv, qseg), 5
        )
        return kv0, act, own_part

    def attend_full(layer, q, kv0, act, own_part, after):
        active, slope, feed = act
        attn, lse, mine, away = call(
            attn_full_kernel, "attn_full", [(head, bf16), ((2, HALF), f32)] + [((4, BLK, D), bf16)] * 2,
            (ids, q, kv0, *own_part, feed, wo[layer]), 8, [room((BLK, HALF))], after=after,
        )
        return (kv0, active, slope, attn, lse), (mine, away)

    normed0, xhat0, q_0, kv_0, gain, bias, bfc, bi = call(
        qkv_first_kernel, "qkv_first",
        [(full, bf16), (full, bf16), (head, bf16), ((HALF, 256), bf16)] + [((2, D), f32)] * 3 + [((2, 512), f32)],
        (ids, *tok_blocks, wq0, cosine, sine), 6, [room(full, bf16), dma(8)], raw=range(1, 9), out_vm=(4, 5, 6, 7),
        limit=62,
    )

    def fetch_wo(layer, after):
        (out,) = call(
            functools.partial(pass_kernel, layer), "pass_wo", [(blk, bf16)], (ids, w_out), 1, [dma(1)], raw=(1,), after=after,
            limit=62,
        )
        return transpose_owner(out)

    wo = [fetch_wo(0, (q_0,))]
    kv0, act, own_part = attend_own(0, q_0, kv_0, normed0, w0)
    (four,) = call(
        four_kernel, "four", [((4, 2, BLK, 1408), bf16)], (ids, p1, shift(p1, "xl", 1, 2)), 2, [dma(8)], out_raw=(0,),
        after=(own_part[1],), limit=62,
    )
    saved0, ends = attend_full(0, q_0, kv0, act, own_part, ())
    w1 = [lax.all_to_all(gate(ids, four, (saved0[3],)), "z", 0, 0, tiled=True).reshape(8, BLK, 1408)]
    terms, sent = scatter(ids, *ends)
    x1, normed_own = call(
        fwd_end_kernel, "fwd_end", [(blk, f32), (blk, bf16)], (ids, *terms, own, gain, bias, bfc), 2,
        vm=range(1, 9), out_vm=(0, 1), limit=8,
    )
    blocks = gather_blocks(normed_own)
    normed1, q_1, kv_1 = call(
        qkv_kernel, "qkv", [(full, bf16), (head, bf16), ((HALF, 256), bf16)], (ids, *blocks, *w1, cosine, sine), 4,
        [room((8, BLK, 384), bf16), dma(8), dma(1)], raw=range(1, 10),
    )
    kv0, act, own_part = attend_own(1, q_1, kv_1, normed1, w1)
    wo.append(fetch_wo(1, (q_1,)))
    gr_top, dattn_top = grad_in(ids, tok_blocks, wo[1], BLK)
    saved1, ends = attend_full(1, q_1, kv0, act, own_part, ())
    terms, _ = scatter(ids, *ends)
    (mixed,) = call(
        last_end_kernel, "last_end", [(blk, bf16)], (ids, *terms, x1, bfc), 2, vm=range(1, 7), out_vm=(0,), limit=8
    )

    def back(q, kv, normed, w, saved, gr, dattn, rows):
        kv0, active, slope, attn, lse = saved
        dqt0, dkv0 = call(
            grad_full_kernel, "grad_full", [((BLK, HALF), f32), ((HALF, 256), bf16)], (ids, q, kv0, dattn, attn, lse), 8,
            [room(head)] * 2,
        )
        got = lax.ppermute(dkv0, "xh", [(1, 0)])
        part, dbi, payload = ff_back_outer(ids, rows, gr, slope, active, attn, normed, w, (dqt0,))
        pieces = call(
            grad_own_kernel, "grad_own", [(head, f32)] * 3, (ids, q, kv, dattn, attn, lse, qseg, dqt0), 5, [room((BLK, HALF))]
        )
        return pieces, got, payload, part, dbi

    part_outs = [((4, BLK, D), bf16), ((4, BLK, D), bf16)]
    pieces, got, payload1, part, dbi1 = back(q_1, kv_1, normed1, w1, saved1, gr_top, dattn_top, 384)
    mine, away, payload1 = call(
        combine_kernel, "combine", part_outs + [((8, 384, 512), bf16)],
        (ids, *pieces, got, cosine, sine, part, *w1, normed1, payload1), 6,
        [room((HALF, 384), bf16), room((8, 96, 512), bf16), room((8, BLK, 384), bf16), dma(1)], raw=(8, 10), out_raw=(2,),
        alias={10: 2}, after=(mixed,),
    )
    terms, sent = scatter(ids, mine, away)
    got_a = lax.all_to_all(payload1, FS, 0, 0, tiled=True)
    g1, gr1, sums1 = call(
        bwd_end_kernel, "bwd_end", [(blk, f32), (blk, bf16), ((8, D), f32)], (ids, *terms, x1, gain, cotangent[0]), 2,
        vm=range(1, 8), out_vm=(0, 1, 2), limit=8,
    )
    g_blocks = gather_blocks(gr1)
    gr, dattn = grad_in(ids, g_blocks, wo[0], 0)
    pieces, got, payload, part, dbi0 = back(q_0, kv_0, normed0, w0, saved0, gr, dattn, 400)
    low1, p1 = over_groups(ids, "fsum_top", (got_a,), pieces[:1])
    (main1,) = call(xsum_top_kernel, "xsum_top", [((352, 512), bf16)], (ids, low1, shift(low1, "xh", 1, 2)), 2)
    mine, away, payload = call(
        combine_first_kernel, "combine_first", part_outs + [((8, 400, 512), bf16)],
        (ids, *pieces, got, cosine, sine, part, wq0, xhat0, normed0, sums1, dbi0, dbi1, payload), 9,
        [room((HALF, 384), bf16), room((8, 112, 512), bf16), dma(1)], raw=(14,), out_raw=(2,), alias={14: 2}, after=(main1,),
    )
    terms, sent = scatter(ids, mine, away)
    (g0,) = call(
        bwd_last_kernel, "bwd_last", [(blk, f32)], (ids, *terms, own, gain, g1), 2, vm=range(1, 8), out_vm=(0,), limit=8
    )
    top_rows = gather_blocks(main1)
    shapes = [((2, BLK, 4096), f32), ((2, 512, D), f32), ((2, BLK, 3 * D), f32)]
    rooms = lambda n: [room(s[0][1:]) for s in shapes] + [room((4, n, 512), bf16)] * 2 + [dma(8), dma(3)]
    outs = call(assemble_top_kernel, "assemble_top", shapes, (ids, *top_rows), 5, rooms(352), raw=range(1, 9), out_raw=(0, 1, 2))
    low0, p0 = over_groups(ids, "fsum_first", (lax.all_to_all(payload, FS, 0, 0, tiled=True),), (g0, outs[2]))
    swap = lambda x: shift(x, "xh", 1, 2)
    (last,) = call(
        xsum_last_kernel, "xsum_last", [((432, 512), bf16)], (ids, low0, swap(low0), p0, swap(p0), p1, swap(p1)), 2,
    )
    last_blocks = gather_blocks(last)
    o_i, o_f, o_q, o_o, o_g, o_s, o_bf, o_bi = call(
        finish_kernel, "finish", shapes + [((2, BLK, D), f32)] + [((2, BLK), f32)] * 3 + [((2, 512), f32)],
        (ids, *last_blocks, *outs), 6, rooms(432), raw=range(1, 12), out_raw=(0, 1, 2),
        alias={9: 0, 10: 1, 11: 2},
    )
    return mixed[None], g0[None], o_g, o_s, o_q, o_o, o_i, o_bi, o_f, o_bf


def solution(mesh):
    fine = Mesh(mesh.devices.reshape(2, 4, 2, 4, 2), AXES)
    seq = ("xh", "y", "core")
    tok = P(FS, seq, None)
    two = P(None, FS)
    three = P(None, FS, None)
    in_specs = (tok, P(FS, None), two, two, three, three, three, two, three, two, tok)
    out_specs = (tok, tok, two, two, three, three, three, two, three, two)
    return jax.shard_map(body, mesh=fine, in_specs=in_specs, out_specs=out_specs, check_vma=False)
```

```python
import functools
import jax
import jax.numpy as jnp
from jax import lax
from jax.experimental import pallas as pl
from jax.experimental.pallas import tpu as pltpu
from jax.sharding import Mesh, PartitionSpec as P

ROT = 32
CONTS = 8
D = 1024
HALF = 1024
BLK = 128
QB = 256
AXES = ("xh", "y", "core", "z", "xl")
FS = ("z", "xl")
f32 = jnp.float32
bf16 = jnp.bfloat16
NT = (((1,), (1,)), ((), ()))
VM = pl.BlockSpec(memory_space=pltpu.VMEM)
SM = pl.BlockSpec(memory_space=pltpu.SMEM)
ANY = pl.BlockSpec(memory_space=pl.ANY)
HBM = pl.BlockSpec(memory_space=pltpu.HBM)
MB = 1024 * 1024


def sds(*args):
    return [jax.ShapeDtypeStruct(s, t) for s, t in args]


class Far:
    def __init__(self, ref, copy):
        self.ref, self.copy = ref, copy

    def here(self):
        if self.copy is not None:
            self.copy.wait()
            self.copy = None
        return self.ref

    def __getitem__(self, index):
        return self.here()[index]

    @property
    def shape(self):
        return self.ref.shape


class Out:
    def __init__(self, ref, copy):
        self.ref, self.copy, self.sent = ref, copy, False

    def __getitem__(self, index):
        return self.ref[index]

    def __setitem__(self, index, value):
        self.ref[index] = value

    @property
    def dtype(self):
        return self.ref.dtype

    @property
    def shape(self):
        return self.ref.shape

    def send(self):
        self.copy.start()
        self.sent = True


COST = 0.001
LIMIT = 51


def call(kernel, name, outs, args, us, scratch=(), limit=None, after=(), raw=(), vm=(), out_raw=(), out_vm=(), alias=None):
    n, m = len(args), len(outs)
    fetched = [i for i in range(1, n) if i not in raw and i not in vm]
    staged = [i for i in range(m) if i not in out_raw and i not in out_vm]

    def run(*refs):
        ins = list(refs[:n])
        results = list(refs[n + len(after) : n + len(after) + m])
        rest = list(refs[n + len(after) + m :])
        own, rest = rest[: len(scratch)], rest[len(scratch) :]
        sems = rest[-1]
        copies = []
        for k, i in enumerate(fetched):
            copy = pltpu.make_async_copy(ins[i], rest[k], sems.at[k])
            copies.append(copy)
            ins[i] = Far(rest[k], copy)
        for copy in copies:
            copy.start()
        for k, i in enumerate(staged):
            ref = rest[len(fetched) + k]
            results[i] = Out(ref, pltpu.make_async_copy(ref, results[i], sems.at[len(fetched) + k]))
        kernel(*ins, *results, *own)
        for i in fetched:
            ins[i].here()
        for i in staged:
            if not results[i].sent:
                results[i].send()
        for i in staged:
            results[i].copy.wait()

    room = [pltpu.VMEM(args[i].shape, args[i].dtype) for i in fetched]
    room += [pltpu.VMEM(outs[i][0], outs[i][1]) for i in staged]
    return pl.pallas_call(
        run,
        out_shape=sds(*outs),
        in_specs=[SM] + [VM if i in vm else HBM for i in range(1, n)] + [ANY] * len(after),
        out_specs=[VM if i in out_vm else HBM for i in range(m)],
        scratch_shapes=list(scratch) + room + [pltpu.SemaphoreType.DMA((max(1, len(room)),))],
        input_output_aliases=alias or {},
        compiler_params=pltpu.CompilerParams(vmem_limit_bytes=(limit or LIMIT) * MB),
        cost_estimate=pl.CostEstimate(flops=int(us * COST * 1e9), bytes_accessed=int(us * COST * 1e6), transcendentals=0),
        name=name,
    )(*args, *after)


def dma(n):
    return pltpu.SemaphoreType.DMA((n,))


def copy_all(pairs, sems):
    copies = [pltpu.make_async_copy(a, b, sems.at[i]) for i, (a, b) in enumerate(pairs)]
    for copy in copies:
        copy.start()
    return copies


def wait_all(copies):
    for copy in copies:
        copy.wait()


def shift(x, axis, by, size):
    return lax.ppermute(x, axis, [(i, (i + by) % size) for i in range(size)])


def gather_blocks(own, hold=None):
    one = shift(own, "y", -1, 4)
    three = shift(own, "y", 1, 4)
    two = shift(own, "y", 2, 4)
    if hold is not None:
        one, two, three = hold(one, two, three)
    blocks = []
    for mine in (own, one, two, three):
        blocks += [mine, shift(mine, "core", 1, 2)]
    return blocks


def spread(low):
    return [shift(low[r - 1], "y", r, 4) for r in (1, 2, 3)]


def transpose_owner(x):
    pairs = [(j * 8 + f, f * 8 + j) for j in range(8) for f in range(8)]
    return lax.ppermute(x, ("y", "core", "z", "xl"), pairs)


def gate(ids, x, after):
    (out,) = call(lambda *refs: None, "gate", [(x.shape, x.dtype)], (ids, x), 1, raw=(1,), out_raw=(0,), after=after, alias={1: 0})
    return out


def gate_all(ids, xs, after):
    n = len(xs)
    return call(
        lambda *refs: None, "gate", [(x.shape, x.dtype) for x in xs], (ids, *xs), 1, raw=range(1, n + 1), out_raw=range(n),
        after=after, alias={i + 1: i for i in range(n)},
    )


def gather_fsdp(ids, x, got, after=()):
    (pair,) = call(
        pair_kernel, "pair", [((2,) + x.shape, bf16)], (ids, x, got), 2, [dma(2)], out_raw=(0,), after=after, limit=62,
    )
    return [pair, shift(pair, "z", -1, 4), shift(pair, "z", 2, 4), shift(pair, "z", 1, 4)]


def weight_copies(ids, pairs, cols, room):
    if len(pairs) == 1:
        return [(pairs[0].at[:, :, cols], room)]
    out = []
    for r in range(4):
        out.append((pairs[r].at[:, :, cols], room.at[pl.ds(2 * lax.rem(ids[4] + r, 4), 2)]))
    return out


def slot(ids, r, s):
    y = lax.rem(ids[0] + r, 4)
    c = ids[1] if s == 0 else 1 - ids[1]
    return y * 2 + c


def rows_of(ids, r, s, n=BLK):
    return pl.ds(pl.multiple_of(slot(ids, r, s) * n, n), n)


def turn(v, cosine, sine):
    lane = lax.broadcasted_iota(jnp.int32, v.shape, 1)
    partner = jnp.where(lane % 2 == 0, pltpu.roll(v, BLK - 1, 1), pltpu.roll(v, 1, 1))
    return v * cosine + partner * sine


def stats(x):
    average = jnp.mean(x, axis=-1, keepdims=True)
    centred = x - average
    variance = jnp.mean(centred * centred, axis=-1, keepdims=True)
    inv = lax.rsqrt(variance + 1e-05)
    return centred * inv, inv


def gelu_both(x):
    a = 0.7978845608028654
    b = 0.044715
    sq = x * x
    t = jnp.tanh(a * x * (1.0 + b * sq))
    half = 0.5 * (1.0 + t)
    slope = half + 0.5 * x * (1.0 - t * t) * a * (1.0 + 3.0 * b * sq)
    return x * half, slope


def dot(a, b):
    return jnp.dot(a, b, preferred_element_type=f32)


def dot_nt(a, b):
    return lax.dot_general(a, b, NT, preferred_element_type=f32)


def pack_q_kernel(ids, wq, gain, bias, bfc, bin_, q0, room, small, binv, sems, out_sems):
    j = ids[0] * 2 + ids[1]
    pairs = []
    for part in range(3):
        cols = pl.ds(pl.multiple_of(part * D + j * BLK, BLK), BLK)
        pairs.append((wq.at[0, :, cols], room.at[0:BLK, part * BLK : part * BLK + BLK]))
    pairs += [(ref, small.at[i]) for i, ref in enumerate((gain, bias, bfc))]
    pairs.append((bin_, binv))
    wait_all(copy_all(pairs, sems))
    chunk = binv[:, pl.ds(pl.multiple_of((j // 2) * BLK, BLK), BLK)].astype(f32)
    chunk = jnp.where(j % 2 == 1, pltpu.roll(chunk, 64, 1), chunk)
    lane = lax.broadcasted_iota(jnp.int32, (1, BLK), 1)
    row2 = jnp.where(lane < 64, chunk[0:1], pltpu.roll(chunk, 64, 1)[1:2])
    blank = jnp.zeros((13, BLK), f32)
    cols = [jnp.concatenate([small[i].astype(f32), row2, blank], 0) for i in range(3)]
    room[BLK:, :] = jnp.concatenate(cols, 1).astype(bf16)
    wait_all(copy_all([(room, q0.at[f]) for f in range(8)], out_sems))


def pack_layer(layer, ids, wi, wf, out, chunks, sems, more=()):
    j = ids[0] * 2 + ids[1]
    rows = pl.ds(pl.multiple_of(j * 64, 64), 64)
    pairs = []
    for f in range(8):
        cols = pl.ds(pl.multiple_of(f * 512 + (j // 2) * BLK, BLK), BLK)
        pairs.append((wi.at[layer, :, cols], chunks.at[f]))
    pairs.append((wf.at[layer, rows, 0:512], out.ref.at[0:64, 512:1024]))
    pairs.append((wf.at[layer, rows, 512:1024], out.ref.at[64:128, 512:1024]))
    wait_all(copy_all(pairs + list(more), sems))
    lane = lax.broadcasted_iota(jnp.int32, (BLK, BLK), 1)
    odd = j % 2 == 1
    for pair in range(4):
        a = chunks[2 * pair].astype(f32)
        b = chunks[2 * pair + 1].astype(f32)
        first = jnp.where(odd, pltpu.roll(a, 64, 1), a)
        second = jnp.where(odd, b, pltpu.roll(b, 64, 1))
        out[:, pair * BLK : pair * BLK + BLK] = jnp.where(lane < 64, first, second).astype(bf16)


def pack_first_kernel(ids, wi, wf, out, chunks, sems):
    pack_layer(0, ids, wi, wf, out, chunks, sems)


def pack_second_kernel(ids, wi, wf, wq, out, chunks, sems):
    j = ids[0] * 2 + ids[1]
    more = []
    for part in range(3):
        cols = pl.ds(pl.multiple_of(part * D + j * BLK, BLK), BLK)
        more.append((wq.at[1, :, cols], out.ref.at[:, D + part * BLK : D + part * BLK + BLK]))
    pack_layer(1, ids, wi, wf, out, chunks, sems, more)


def pass_kernel(layer, ids, x, out, sems):
    wait_all(copy_all([(x.at[layer], out.ref)], sems))


def join_kernel(ids, a, b, out, sems):
    wait_all(copy_all([(a, out.ref.at[0:BLK]), (b, out.ref.at[BLK : 2 * BLK])], sems))


def pair_kernel(ids, own, got, out, sems):
    xl = ids[3]
    wait_all(copy_all([(own.here(), out.at[xl]), (got.here(), out.at[1 - xl])], sems))


def four_kernel(ids, own, got, out, sems):
    xl = ids[3]
    mine, other = own.here(), got.here()
    wait_all(copy_all([(src, out.at[z, at]) for z in range(4) for src, at in ((mine, xl), (other, 1 - xl))], sems))


def params_part(rows_of_f, gain, bias, bfc, bi):
    lane = lax.broadcasted_iota(jnp.int32, (1, BLK), 1)
    for f in range(8):
        cols = slice(f * BLK, f * BLK + BLK)
        rows = rows_of_f[f].astype(f32)
        gain[:, cols] = rows[0:2, 0:BLK]
        bias[:, cols] = rows[0:2, BLK : 2 * BLK]
        bfc[:, cols] = rows[0:2, 2 * BLK :]
    for pair in range(4):
        a = rows_of_f[2 * pair].astype(f32)[2:3, :BLK]
        b = rows_of_f[2 * pair + 1].astype(f32)[2:3, :BLK]
        cols = slice(pair * BLK, pair * BLK + BLK)
        bi[0:1, cols] = jnp.where(lane < 64, a, pltpu.roll(b, 64, 1))
        bi[1:2, cols] = jnp.where(lane < 64, pltpu.roll(a, 64, 1), b)


def qkv_part(normed, w, cosine, sine, q, kv):
    for i in range(HALF // QB):
        rows = slice(i * QB, i * QB + QB)
        out = dot(normed[rows, :], w).astype(bf16).astype(f32)
        cb = cosine[rows, :]
        sb = sine[rows, :]
        kv[rows, :BLK] = turn(out[:, BLK : 2 * BLK], cb, sb).astype(bf16)
        kv[rows, BLK:] = out[:, 2 * BLK :].astype(bf16)
        q[rows, :] = (turn(out[:, :BLK], cb, sb).astype(bf16).astype(f32) * 0.125).astype(bf16)


def take_blocks(ids, blocks, room, sems, at=0):
    part = slice(at, at + BLK)
    return copy_all([(blocks[2 * r + s].at[part], room.at[rows_of(ids, r, s)]) for r in range(4) for s in range(2)], sems)


def qkv_first_kernel(ids, *refs):
    blocks, (wq, cosine, sine), refs = refs[:8], refs[8:11], refs[11:]
    normed, xhat, q, kv, gain, bias, bfc, bi, raw, sems = refs
    copies = take_blocks(ids, blocks, raw, sems)
    w = wq.here()
    params_part([w[f, BLK:, :] for f in range(8)], gain, bias, bfc, bi)
    wait_all(copies)
    for i in range(HALF // QB):
        rows = slice(i * QB, i * QB + QB)
        x, _ = stats(raw[rows, :].astype(f32))
        xhat[rows, :] = x.astype(bf16)
        normed[rows, :] = (x * gain[0:1, :] + bias[0:1, :]).astype(bf16)
    xhat.send()
    normed.send()
    qkv_part(normed, w[:, :BLK, :].reshape(D, 384), cosine, sine, q, kv)


def qkv_kernel(ids, *refs):
    blocks, w, (cosine, sine), (normed, q, kv, wq, sems, wsem) = refs[:8], refs[8:9], refs[9:11], refs[11:]
    copies = copy_all(weight_copies(ids, w, slice(1024, 1408), wq), wsem)
    copies += take_blocks(ids, blocks, normed.ref, sems)
    wait_all(copies)
    normed.send()
    qkv_part(normed, wq[...].reshape(D, 384), cosine, sine, q, kv)


def ff_kernel(layer, ids, normed, bi, *refs):
    w, (active, slope, feed, wi, wf, va, vs, vf, wsems, sems) = refs[:-10], refs[-10:]
    copies = copy_all(weight_copies(ids, w, slice(0, 512), wi), wsems.at[0])
    late = copy_all(weight_copies(ids, w, slice(512, 1024), wf), wsems.at[1])
    normed.here()
    wait_all(copies)
    left = right = None
    sent = []
    for i in range(HALF // 256):
        rows = slice(i * 256, i * 256 + 256)
        pre = dot(normed[rows, :], wi[...].reshape(D, 512)) + bi[layer : layer + 1, :]
        act, der = gelu_both(pre)
        act = act.astype(bf16)
        va[rows, :] = act
        vs[rows, :] = der.astype(bf16)
        if i == 0:
            wait_all(late)
            left, right = wf[:, 0:64, :].reshape(512, 512), wf[:, 64:128, :].reshape(512, 512)
        vf[rows, :512] = dot(act, left).astype(bf16)
        vf[rows, 512:] = dot(act, right).astype(bf16)
        pairs = [(v.at[rows], out.at[rows]) for v, out in ((va, active), (vs, slope), (vf, feed))]
        sent += copy_all(pairs, sems.at[i])
    wait_all(sent)


def ff(ids, layer, normed, w, bi, after=()):
    room = lambda *shape: pltpu.VMEM(shape, bf16)
    return call(
        functools.partial(ff_kernel, layer), "ff", [((HALF, 512), bf16), ((HALF, 512), bf16), ((HALF, D), bf16)],
        (ids, normed, bi, *w), 5,
        [room(8, BLK, 512), room(8, BLK, 512), room(HALF, 512), room(HALF, 512), room(HALF, D),
         pltpu.SemaphoreType.DMA((2, 4)), pltpu.SemaphoreType.DMA((4, 3))],
        raw=range(3, 3 + len(w)), out_raw=(0, 1, 2), limit=62 - 11 * layer, after=after,
    )


def head_cut(x):
    lane = lax.broadcasted_iota(jnp.int32, x.shape, 1)
    zero = jnp.zeros((), x.dtype)
    return [jnp.where(lane < 64, x, zero), jnp.where(lane >= 64, x, zero)]


def seen(i, kk, qseg, kseg, QB):
    q0 = i * QB
    qs = qseg[0:1, q0 : q0 + QB]
    ks = kseg[0:kk, 0:1]
    key = lax.broadcasted_iota(jnp.int32, (kk, QB), 0)
    query = q0 + lax.broadcasted_iota(jnp.int32, (kk, QB), 1)
    return (key <= query) & ((ks == 0) | (ks == qs))


def flip(x):
    return jnp.transpose(x.astype(f32)).astype(bf16)


def attn_own_kernel(ids, q, kv, qseg, acc, m_out, l_out):
    qseg = qseg[...]
    kseg = jnp.transpose(qseg)
    km = head_cut(kv[:, :BLK])
    vt = flip(kv[:, BLK:])
    for i in range(HALF // 512):
        cols = slice(i * 512, (i + 1) * 512)
        kk = (i + 1) * 512
        allowed = seen(i, kk, qseg, kseg, 512)
        for h in range(2):
            rows = slice(h * 64, h * 64 + 64)
            s = jnp.where(allowed, dot_nt(km[h][:kk], q[cols, :]), -1e30)
            m = jnp.max(s, axis=0, keepdims=True)
            p = jnp.exp(s - m)
            l_out[h : h + 1, cols] = jnp.sum(p, axis=0, keepdims=True)
            m_out[h : h + 1, cols] = m
            acc[rows, cols] = dot(vt[rows, :kk], p.astype(bf16))


def split_rows(ids, mine, away, block):
    for r in range(4):
        away[r] = block(rows_of(ids, r, 1)).astype(bf16)
    away.send()
    for r in range(4):
        mine[r] = block(rows_of(ids, r, 0)).astype(bf16)


def attn_full_kernel(ids, q, kv0, acc, m_in, l_in, feed, wo, attn, lse, mine, away, tmp):
    upper = ids[2] == 1
    for ref in (q, kv0, acc, m_in, l_in):
        ref.here()

    @pl.when(upper)
    def _():
        km = head_cut(kv0[:, :BLK])
        vt = flip(kv0[:, BLK:])
        for i in range(HALF // 512):
            cols = slice(i * 512, (i + 1) * 512)
            for h in range(2):
                rows = slice(h * 64, h * 64 + 64)
                s = dot_nt(km[h], q[cols, :])
                m0 = m_in[h : h + 1, cols]
                m = jnp.maximum(m0, jnp.max(s, axis=0, keepdims=True))
                p = jnp.exp(s - m)
                a = jnp.exp(m0 - m)
                l = l_in[h : h + 1, cols] * a + jnp.sum(p, axis=0, keepdims=True)
                o = dot(vt[rows, :], p.astype(bf16))
                tmp[rows, cols] = (acc[rows, cols] * a + o) / l
                lse[h : h + 1, cols] = m + jnp.log(l)

    @pl.when(jnp.logical_not(upper))
    def _():
        for h in range(2):
            rows = slice(h * 64, h * 64 + 64)
            l = l_in[h : h + 1, :]
            tmp[rows, :] = acc[rows, :] / l
            lse[h : h + 1, :] = m_in[h : h + 1, :] + jnp.log(l)

    attn[...] = jnp.transpose(tmp[...]).astype(bf16)
    attn.send()
    lse.send()
    split_rows(ids, mine, away, lambda rows: feed[rows, :].astype(f32) + dot(attn[rows, :], wo[...]))


def mid_kernel(ids, mine, got, total, one, two, three):
    for r, out in ((1, one), (2, two), (3, three)):
        out[...] = (mine[r].astype(f32) + got[r].astype(f32)).astype(bf16)
    total[...] = mine[0].astype(f32) + got[0].astype(f32)


def summed(total, one, two, three):
    return total[...] + one[...].astype(f32) + two[...].astype(f32) + three[...].astype(f32)


def fwd_end_kernel(ids, total, one, two, three, x, gain, bias, bfc, x_new, normed):
    new = x[...].astype(f32) + summed(total, one, two, three) + bfc[0:1, :]
    x_new[...] = new
    xhat, _ = stats(new)
    normed[...] = (xhat * gain[1:2, :] + bias[1:2, :]).astype(bf16)


def last_end_kernel(ids, total, one, two, three, x, bfc, out):
    out[...] = (x[...] + summed(total, one, two, three) + bfc[1:2, :]).astype(bf16)


def grad_in_kernel(at, ids, *refs):
    blocks, (wo, gr, dattn, sems) = refs[:8], refs[8:]
    wait_all(take_blocks(ids, blocks, gr.ref, sems, at))
    gr.send()
    dattn[...] = dot_nt(gr[...], wo[...]).astype(bf16)


def row_delta(attn, do):
    prod = attn[...].astype(f32) * do[...].astype(f32)
    head = lax.broadcasted_iota(jnp.int32, (8, BLK), 0)
    lane = lax.broadcasted_iota(jnp.int32, (8, BLK), 1) // 64
    pickers = jnp.where(head == lane, 1.0, 0.0).astype(f32)
    return lax.dot_general(pickers, prod, NT, precision=lax.Precision.HIGHEST, preferred_element_type=f32)


def grad_block(km, vm, kt, qm, dom, q_blk, do_blk, lse, delta, allowed):
    p = jnp.exp(dot_nt(km, q_blk) - lse)
    if allowed is not None:
        p = jnp.where(allowed, p, 0.0)
    dp = dot_nt(vm, do_blk)
    ds = (p * (dp - delta)).astype(bf16)
    return dot(kt, ds), dot(ds, qm), dot(p.astype(bf16), dom)


def grad_full_kernel(ids, q, kv0, do, attn, lse, dqt, dkv, acck, accv):
    upper = ids[2] == 1
    for ref in (q, kv0, do, attn, lse):
        ref.here()

    @pl.when(upper)
    def _():
        delta = row_delta(attn, do)
        qm, km, vm, dom = [head_cut(x) for x in (q[...], kv0[:, :BLK], kv0[:, BLK:], do[...])]
        kt = flip(kv0[:, :BLK])
        for i in range(HALF // 512):
            cols = slice(i * 512, (i + 1) * 512)
            for h in range(2):
                rows = slice(h * 64, h * 64 + 64)
                dq, dk, dv = grad_block(
                    km[h], vm[h], kt[rows, :], qm[h][cols], dom[h][cols], q[cols, :], do[cols, :],
                    lse[h : h + 1, cols], delta[h : h + 1, cols], None,
                )
                dqt[rows, cols] = dq
                if i == 0 and h == 0:
                    acck[...] = dk
                    accv[...] = dv
                else:
                    acck[...] += dk
                    accv[...] += dv
        dkv[:, :BLK] = acck[...].astype(bf16)
        dkv[:, BLK:] = accv[...].astype(bf16)

    @pl.when(jnp.logical_not(upper))
    def _():
        dqt[...] = jnp.zeros(dqt.shape, f32)
        dkv[...] = jnp.zeros(dkv.shape, bf16)


def grad_own_kernel(ids, q, kv, do, attn, lse, qseg, dqt0, out, tmp, dk_out, dv_out):
    qseg = qseg[...]
    kseg = jnp.transpose(qseg)
    delta = row_delta(attn, do)
    qm, km, vm, dom = [head_cut(x) for x in (q[...], kv[:, :BLK], kv[:, BLK:], do[...])]
    kt = flip(kv[:, :BLK])
    dk_out[...] = jnp.zeros(dk_out.shape, f32)
    dv_out[...] = jnp.zeros(dv_out.shape, f32)
    for i in range(HALF // 256):
        cols = slice(i * 256, (i + 1) * 256)
        kk = (i + 1) * 256
        allowed = seen(i, kk, qseg, kseg, 256)
        for h in range(2):
            rows = slice(h * 64, h * 64 + 64)
            dq, dk, dv = grad_block(
                km[h][:kk], vm[h][:kk], kt[rows, :kk], qm[h][cols], dom[h][cols], q[cols, :], do[cols, :],
                lse[h : h + 1, cols], delta[h : h + 1, cols], allowed,
            )
            tmp[rows, cols] = (dq + dqt0[rows, cols]) * 0.125
            dk_out[:kk, :] += dk
            dv_out[:kk, :] += dv
    out[:, :BLK] = jnp.transpose(tmp[...]).astype(bf16)
    out[:, BLK : 2 * BLK] = dk_out[...].astype(bf16)
    out[:, 2 * BLK :] = dv_out[...].astype(bf16)


def ff_back_outer_kernel(ids, gr, slope, active, attn, normed, *refs):
    w, (part, dbi, out, wi, wf, vd, v, wsems, sems) = refs[:-9], refs[-9:]
    copies = copy_all(weight_copies(ids, w, slice(512, 1024), wf), wsems.at[0])
    late = copy_all(weight_copies(ids, w, slice(0, 512), wi), wsems.at[1])
    gr.here()
    slope.here()
    wait_all(copies)
    left, right = wf[:, 0:64, :].reshape(512, 512), wf[:, 64:128, :].reshape(512, 512)
    total = jnp.zeros((1, 512), f32)
    for i in range(HALF // 512):
        rows = slice(i * 512, i * 512 + 512)
        d = (dot_nt(gr[rows, :512], left) + dot_nt(gr[rows, 512:], right)) * slope[rows, :].astype(f32)
        total = total + jnp.sum(d, axis=0, keepdims=True)
        d = d.astype(bf16)
        vd[rows, :] = d
        if i == 0:
            wait_all(late)
        part[rows, :] = dot_nt(d, wi[...].reshape(D, 512)).astype(bf16)
    part.send()
    dbi[...] = jnp.concatenate([total, jnp.zeros((7, 512), f32)], 0)
    wait_all(outer_rows(out, v, sems, active, gr, attn, normed, vd))


def ff_back_outer(ids, rows, gr, slope, active, attn, normed, w, after):
    room = lambda *shape: pltpu.VMEM(shape, bf16)
    return call(
        ff_back_outer_kernel, "ff_back_outer", [((HALF, D), bf16), ((8, 512), f32), ((8, rows, 512), bf16)],
        (ids, gr, slope, active, attn, normed, *w), 9,
        [room(8, BLK, 512), room(8, BLK, 512), room(HALF, 512), room(8, 288, 512), pltpu.SemaphoreType.DMA((2, 4)),
         pltpu.SemaphoreType.DMA((3, 2))],
        raw=range(6, 6 + len(w)), out_raw=(2,), after=after,
    )


def combine_rows(ids, own, back, cosine, sine, dqkv):
    cb = cosine[...]
    sb = -sine[...]
    dqkv[:, :BLK] = turn(own[:, :BLK].astype(f32), cb, sb).astype(bf16)
    dk = own[:, BLK : 2 * BLK].astype(f32) + back[:, :BLK].astype(f32)
    dqkv[:, BLK : 2 * BLK] = turn(dk, cb, sb).astype(bf16)
    dqkv[:, 2 * BLK :] = (own[:, 2 * BLK :].astype(f32) + back[:, BLK:].astype(f32)).astype(bf16)


def combine_kernel(ids, own, back, cosine, sine, part, w1, normed, _, mine, away, payload, dqkv, out, wq, wsem):
    copies = copy_all(weight_copies(ids, (w1,), slice(1024, 1408), wq), wsem)
    combine_rows(ids, own, back, cosine, sine, dqkv)
    wait_all(copies)
    w = wq[...].reshape(D, 384)
    split_rows(ids, mine, away, lambda rows: part[rows, :].astype(f32) + dot_nt(dqkv[rows, :], w))
    mine.send()
    g_q = outer(normed[...], dqkv[...])
    for f in range(8):
        pack_rows(out, f, g_q)
    wait_all(copy_all([(out, payload.at[:, 288:384])], wsem))


def combine_first_kernel(ids, own, back, cosine, sine, part, wq0, xhat, normed, sums1, dbi0, dbi1, *refs):
    _, mine, away, payload, dqkv, out, sems = refs
    combine_rows(ids, own, back, cosine, sine, dqkv)
    w = wq0[:, :BLK, :].reshape(D, 384)
    gain = jnp.zeros((1, D), f32)
    base = jnp.zeros((1, D), f32)
    for s, to in ((1, away), (0, mine)):
        for r in range(4):
            rows = rows_of(ids, r, s)
            block = part[rows, :].astype(f32) + dot_nt(dqkv[rows, :], w)
            to[r] = block.astype(bf16)
            gain = gain + jnp.sum(block * xhat[rows, :].astype(f32), axis=0, keepdims=True)
            base = base + jnp.sum(block, axis=0, keepdims=True)
        to.send()
    g_q = outer(normed[...], dqkv[...])
    lane = lax.broadcasted_iota(jnp.int32, (1, BLK), 1)
    blank = jnp.zeros((13, 384), f32)
    none = jnp.zeros((1, 256), f32)
    for f in range(8):
        pack_rows(out, f, g_q)
        cols = slice(f * BLK, f * BLK + BLK)
        row0 = jnp.concatenate([gain[:, cols], base[:, cols], sums1[3:4, cols]], 1)
        row1 = jnp.concatenate([sums1[0:1, cols], sums1[1:2, cols], sums1[2:3, cols]], 1)
        half = slice((f // 2) * BLK, (f // 2) * BLK + BLK)
        a = dbi0[0:1, half]
        b = dbi1[0:1, half]
        if f % 2 == 0:
            b = pltpu.roll(b, 64, 1)
        else:
            a = pltpu.roll(a, 64, 1)
        row2 = jnp.concatenate([jnp.where(lane < 64, a, b), none], 1)
        out[f, 96:112, :384] = jnp.concatenate([row0, row1, row2, blank], 0).astype(bf16)
        out[f, 96:112, 384:] = jnp.zeros((16, 128), bf16)
    wait_all(copy_all([(out, payload.at[:, 288:400])], sems))


def norm_back(dn, x, gain_row, g):
    xhat, inv = stats(x[...].astype(f32))
    dx = dn * gain_row
    dx = inv * (dx - jnp.mean(dx, -1, keepdims=True) - xhat * jnp.mean(dx * xhat, -1, keepdims=True))
    return xhat, g[...].astype(f32) + dx


def bwd_end_kernel(ids, total, one, two, three, x, gain, g, g_new, gr, sums):
    dn = summed(total, one, two, three)
    xhat, new = norm_back(dn, x, gain[1:2, :], g)
    g_new[...] = new
    gr[...] = new.astype(bf16)
    col = lambda v: jnp.sum(v, axis=0, keepdims=True)
    top = col(g[...].astype(f32))
    sums[...] = jnp.concatenate([col(dn * xhat), col(dn), top, col(new), jnp.zeros((4, D), f32)], 0)


def bwd_last_kernel(ids, total, one, two, three, x, gain, g, g_new):
    _, new = norm_back(summed(total, one, two, three), x, gain[0:1, :], g)
    g_new[...] = new


def outer(a, b):
    return lax.dot_general(a, b, (((0,), (0,)), ((), ())), preferred_element_type=f32).astype(bf16)


def pack_rows(out, f, g_q):
    for part in range(3):
        for group in range(4):
            piece = g_q[f * 128 + group * 32 : f * 128 + group * 32 + 32, part * BLK : part * BLK + BLK]
            out[f, part * 32 : part * 32 + 32, group * BLK : group * BLK + BLK] = piece


def outer_rows(out, v, sems, active, gr, attn, normed, dpre):
    for half in range(2):
        cols = slice(half * 512, half * 512 + 512)
        g_f = outer(active[...], gr[:, cols])
        g_o = outer(attn[...], gr[:, cols])
        for f in range(8):
            v[f, 128 + 64 * half : 192 + 64 * half, :] = g_f[f * 64 : f * 64 + 64]
            v[f, 256 + 16 * half : 272 + 16 * half, :] = g_o[f * 16 : f * 16 + 16]
    first = copy_all([(v.at[:, 128:288], out.at[:, 128:288])], sems.at[0])
    for half in range(2):
        cols = slice(half * 512, half * 512 + 512)
        g_i = outer(normed[:, cols], dpre[...])
        for k in range(4):
            v[4 * half + k, 0:128, :] = g_i[k * 128 : k * 128 + 128]
        group = slice(4 * half, 4 * half + 4)
        first += copy_all([(v.at[group, 0:128], out.at[group, 0:128])], sems.at[1 + half])
    return first


def fsum_kernel(ids, got, low, piece, room, sems):
    rows = got.shape[1]
    half = rows // 32 * 16
    parts = (slice(0, half), slice(half, rows))
    copies = copy_all([(got.at[:, part], room.at[:, part]) for part in parts], sems)
    for at in range(0, rows, 16):
        if at in (0, half):
            copies[0 if at == 0 else 1].wait()
        part = slice(at, at + 16)
        total = room[0, part, :].astype(f32)
        for f in range(1, 8):
            total = total + room[f, part, :].astype(f32)
        total = total.astype(bf16)
        if 256 <= at < 288:
            piece[at - 256 : at - 240, :] = total
        else:
            to = at if at < 256 else at - 32
            low[to : to + 16, :] = total


def add_rows(terms, start, stop):
    total = terms[0][start:stop, :].astype(f32)
    for term in terms[1:]:
        total = total + term[start:stop, :].astype(f32)
    return total.astype(bf16)


def xsum_top_kernel(ids, low, got, main):
    main[...] = add_rows((low, got), 0, 352)


def xsum_last_kernel(ids, low, got, p0, p0_other, p1, p1_other, main):
    terms = (low, got)
    main[0:112, :] = add_rows(terms, 256, 368)
    main[112:368, :] = add_rows(terms, 0, 256)
    main[368:400, :] = add_rows((p0, p0_other), 0, 32)
    main[400:432, :] = add_rows((p1, p1_other), 0, 32)


def over_groups(ids, name, got, after=()):
    rows = got.shape[1]
    low, piece = call(
        fsum_kernel, name, [((rows - 32, 512), bf16), ((32, 512), bf16)], (ids, got), 3,
        [pltpu.VMEM(got.shape, bf16), dma(2)], raw=(1,), after=after,
    )
    return low, transpose_owner(piece)


def place_in(zero, one, at, y, o_i, o_f):
    lane = lax.broadcasted_iota(jnp.int32, (BLK, BLK), 1)
    start = pl.multiple_of(y * BLK, BLK)
    for half in range(2):
        rows = slice(at + 128 + 64 * half, at + 192 + 64 * half)
        cols = slice(half * 512, half * 512 + 512)
        o_f[pl.ds(start, 64), cols] = zero[rows, :].astype(f32)
        o_f[pl.ds(start + 64, 64), cols] = one[rows, :].astype(f32)
    for pair in range(4):
        cols = slice(pair * BLK, pair * BLK + BLK)
        a, b = zero[at : at + BLK, cols].astype(f32), one[at : at + BLK, cols].astype(f32)
        even = pl.ds(pl.multiple_of(2 * pair * 512 + start, BLK), BLK)
        odd = pl.ds(pl.multiple_of((2 * pair + 1) * 512 + start, BLK), BLK)
        o_i[:, even] = jnp.where(lane < 64, a, pltpu.roll(b, 64, 1))
        o_i[:, odd] = jnp.where(lane < 64, pltpu.roll(a, 64, 1), b)


def place_q(zero, one, at, y, o_q):
    for part in range(3):
        rows = slice(at + part * 32, at + part * 32 + 32)
        start = pl.multiple_of(part * D + 2 * y * BLK, BLK)
        for group in range(4):
            cols = slice(group * BLK, group * BLK + BLK)
            to = slice(group * 32, group * 32 + 32)
            o_q[to, pl.ds(start, BLK)] = zero[rows, cols].astype(f32)
            o_q[to, pl.ds(start + BLK, BLK)] = one[rows, cols].astype(f32)


def fetch_rows(ids, blocks, room, sems):
    pairs = []
    for r in range(4):
        pairs += [(blocks[2 * r], room.at[r, ids[1]]), (blocks[2 * r + 1], room.at[r, 1 - ids[1]])]
    return copy_all(pairs, sems)


def assemble_top_kernel(ids, *refs):
    blocks, (o_i, o_f, o_q, vi, vf, vq, room, sems, out_sems) = refs[:8], refs[8:]
    copies = fetch_rows(ids, blocks, room, sems)
    for r in range(4):
        wait_all(copies[2 * r : 2 * r + 2])
        y = lax.rem(ids[0] + r, 4)
        place_in(room.at[r, 0], room.at[r, 1], 0, y, vi, vf)
        place_q(room.at[r, 0], room.at[r, 1], 256, y, vq)
    wait_all(copy_all([(vi, o_i.at[1]), (vf, o_f.at[1]), (vq, o_q.at[1])], out_sems))


def finish_kernel(ids, *refs):
    blocks, refs = refs[:8], refs[11:]
    o_i, o_f, o_q, o_o, o_g, o_s, o_bf, o_bi, vi, vf, vq, room, sems, out_sems = refs
    copies = fetch_rows(ids, blocks, room, sems)
    total = jnp.zeros((16, 384), f32)
    lane = lax.broadcasted_iota(jnp.int32, (1, BLK), 1)
    for r in range(4):
        wait_all(copies[2 * r : 2 * r + 2])
        y = lax.rem(ids[0] + r, 4)
        place_in(room.at[r, 0], room.at[r, 1], 112, y, vi, vf)
        place_q(room.at[r, 0], room.at[r, 1], 0, y, vq)
    outs = copy_all([(vi, o_i.at[0]), (vf, o_f.at[0]), (vq, o_q.at[0])], out_sems)
    for r in range(4):
        y = lax.rem(ids[0] + r, 4)
        for layer in range(2):
            for half in range(2):
                at = 368 + 32 * layer + 16 * half
                cols = slice(half * 512, half * 512 + 512)
                start = pl.multiple_of(y * 32, 32)
                o_o[layer, pl.ds(start, 16), cols] = room[r, 0, at : at + 16, :].astype(f32)
                o_o[layer, pl.ds(start + 16, 16), cols] = room[r, 1, at : at + 16, :].astype(f32)
        zero, one = room[r, 0, 96:112, :384].astype(f32), room[r, 1, 96:112, :384].astype(f32)
        total = total + zero + one
        a, b = zero[2:3, :BLK], one[2:3, :BLK]
        cols = pl.ds(pl.multiple_of(y * BLK, BLK), BLK)
        o_bi[0:1, cols] = jnp.where(lane < 64, a, pltpu.roll(b, 64, 1))
        o_bi[1:2, cols] = jnp.where(lane < 64, pltpu.roll(a, 64, 1), b)
    o_g[...] = total[0:2, :BLK]
    o_s[...] = total[0:2, BLK : 2 * BLK]
    o_bf[...] = total[0:2, 2 * BLK :]
    wait_all(outs)


def positions_of(group_seg):
    token_index = jnp.arange(group_seg.shape[0], dtype=jnp.int32)
    labels = jnp.arange(CONTS + 1, dtype=jnp.int32)
    member = (group_seg[:, None] == labels[None, :]).astype(jnp.int32)
    counts = jnp.sum(member, axis=0)
    starts = jnp.cumsum(counts) - counts
    own_start = jnp.sum(member * starts[None, :], axis=1)
    return token_index - own_start + jnp.where(group_seg > 0, counts[0], 0)


def rope_tables(positions):
    lane = jnp.arange(BLK, dtype=jnp.int32) % 64
    inverse = 10000.0 ** (-2.0 * (lane // 2).astype(f32) / ROT)
    phase = positions.astype(f32)[:, None] * jnp.where(lane < ROT, inverse, 0.0)[None, :]
    sign = jnp.where(lane % 2 == 0, -1.0, 1.0)
    return jnp.cos(phase), jnp.sin(phase) * sign[None, :]


def scatter(ids, mine, away):
    got = shift(away, "core", 1, 2)
    blk = (BLK, D)
    total, one, two, three = call(
        mid_kernel, "rs_mid", [(blk, f32)] + [(blk, bf16)] * 3, (ids, mine, got), 2, vm=(2,), out_vm=(0, 1, 2, 3), limit=8
    )
    return [total] + spread([one, two, three]), one


def grad_in(ids, g_blocks, wo, at):
    return call(
        functools.partial(grad_in_kernel, at), "grad_in", [((HALF, D), bf16), ((HALF, BLK), bf16)], (ids, *g_blocks, wo), 3,
        [dma(8)], raw=range(1, 9),
    )


def body(tokens, segment, ln_gain, ln_bias, w_qkv, w_out, w_in, b_in, w_fc, b_fc, cotangent):
    xh = lax.axis_index("xh")
    ids = jnp.stack([lax.axis_index("y"), lax.axis_index("core"), xh, lax.axis_index("xl"), lax.axis_index("z")]).astype(jnp.int32)
    own = tokens[0]
    full = (HALF, D)
    blk = (BLK, D)
    head = (HALF, BLK)
    room = lambda shape, kind=f32: pltpu.VMEM(shape, kind)
    chunks = [room((8, BLK, BLK), bf16)]

    group_seg = segment[0]
    positions = positions_of(group_seg)
    seg = lax.dynamic_slice_in_dim(group_seg, xh * HALF, HALF, 0)
    cosine, sine = rope_tables(lax.dynamic_slice_in_dim(positions, xh * HALF, HALF, 0))
    qseg = jnp.broadcast_to(seg[None, :].astype(f32), (8, HALF))

    (both,) = call(
        join_kernel, "join", [((2 * BLK, D), bf16)], (ids, own, cotangent[0]), 1, [dma(2)], raw=(1, 2), limit=62
    )
    (p0,) = call(
        pack_first_kernel, "pack_first", [(blk, bf16)], (ids, w_in, w_fc), 3, chunks + [dma(10)], raw=(1, 2), limit=62, after=(both,),
    )
    other0 = shift(p0, "xl", 1, 2)
    (q0,) = call(
        pack_q_kernel, "pack_q", [((8, 144, 384), bf16)], (ids, w_qkv, ln_gain, ln_bias, b_fc, b_in), 3,
        [room((144, 384), bf16), room((3, 2, BLK), bf16), room((2, 512), bf16), dma(7), dma(8)],
        raw=(1, 2, 3, 4, 5), out_raw=(0,), after=(cosine, other0), limit=62,
    )
    wq0 = lax.all_to_all(q0, FS, 0, 0, tiled=True)
    (p1,) = call(
        pack_second_kernel, "pack_second", [((BLK, 1408), bf16)], (ids, w_in, w_fc, w_qkv), 3, chunks + [dma(13)], raw=(1, 2, 3), limit=62,
        after=(wq0,),
    )
    tok_blocks = gather_blocks(both, lambda *x: gate_all(ids, x, (q0,)))
    w0 = gather_fsdp(ids, p0, other0)

    def attend_own(layer, q, kv, normed, w, before):
        kv0 = lax.ppermute(kv, "xh", [(0, 1)])
        own_part = call(
            attn_own_kernel, "attn_own", [((BLK, HALF), f32), ((2, HALF), f32), ((2, HALF), f32)], (ids, q, kv, qseg), 5
        )
        first = before(own_part[1:2])
        return kv0, ff(ids, layer, normed, w, bi, first), own_part, first

    def attend_full(layer, q, kv0, act, own_part, after):
        active, slope, feed = act
        attn, lse, mine, away = call(
            attn_full_kernel, "attn_full", [(head, bf16), ((2, HALF), f32)] + [((4, BLK, D), bf16)] * 2,
            (ids, q, kv0, *own_part, feed, wo[layer]), 8, [room((BLK, HALF))], after=after,
        )
        return (kv0, active, slope, attn, lse), (mine, away)

    normed0, xhat0, q_0, kv_0, gain, bias, bfc, bi = call(
        qkv_first_kernel, "qkv_first",
        [(full, bf16), (full, bf16), (head, bf16), ((HALF, 256), bf16)] + [((2, D), f32)] * 3 + [((2, 512), f32)],
        (ids, *tok_blocks, wq0, cosine, sine), 6, [room(full, bf16), dma(8)], raw=range(1, 9), out_vm=(4, 5, 6, 7),
        limit=62,
    )

    def fetch_wo(layer, after):
        (out,) = call(
            functools.partial(pass_kernel, layer), "pass_wo", [(blk, bf16)], (ids, w_out), 1, [dma(1)], raw=(1,), after=after,
            limit=62,
        )
        return transpose_owner(out)

    def spread_w1(after):
        return call(
            four_kernel, "four", [((4, 2, BLK, 1408), bf16)], (ids, p1, shift(p1, "xl", 1, 2)), 2, [dma(8)], out_raw=(0,),
            after=after, limit=62,
        )

    kv0, act, own_part, (four,) = attend_own(0, q_0, kv_0, normed0, w0, spread_w1)
    wo = [fetch_wo(0, own_part[1:2])]
    saved0, ends = attend_full(0, q_0, kv0, act, own_part, ())
    w1 = [lax.all_to_all(gate(ids, four, (saved0[3],)), "z", 0, 0, tiled=True).reshape(8, BLK, 1408)]
    terms, sent = scatter(ids, *ends)
    x1, normed_own = call(
        fwd_end_kernel, "fwd_end", [(blk, f32), (blk, bf16)], (ids, *terms, own, gain, bias, bfc), 2,
        vm=range(1, 9), out_vm=(0, 1), limit=8,
    )
    blocks = gather_blocks(normed_own)
    normed1, q_1, kv_1 = call(
        qkv_kernel, "qkv", [(full, bf16), (head, bf16), ((HALF, 256), bf16)], (ids, *blocks, *w1, cosine, sine), 4,
        [room((8, BLK, 384), bf16), dma(8), dma(1)], raw=range(1, 10),
    )
    kv0, act, own_part, _ = attend_own(1, q_1, kv_1, normed1, w1, lambda after: ())
    wo.append(fetch_wo(1, (q_1,)))
    gr_top, dattn_top = grad_in(ids, tok_blocks, wo[1], BLK)
    saved1, ends = attend_full(1, q_1, kv0, act, own_part, ())
    terms, _ = scatter(ids, *ends)
    (mixed,) = call(
        last_end_kernel, "last_end", [(blk, bf16)], (ids, *terms, x1, bfc), 2, vm=range(1, 7), out_vm=(0,), limit=8
    )

    def back(q, kv, normed, w, saved, gr, dattn, rows):
        kv0, active, slope, attn, lse = saved
        dqt0, dkv0 = call(
            grad_full_kernel, "grad_full", [((BLK, HALF), f32), ((HALF, 256), bf16)], (ids, q, kv0, dattn, attn, lse), 8,
            [room(head)] * 2,
        )
        got = lax.ppermute(dkv0, "xh", [(1, 0)])
        part, dbi, payload = ff_back_outer(ids, rows, gr, slope, active, attn, normed, w, (dqt0,))
        pieces = call(
            grad_own_kernel, "grad_own", [((HALF, 384), bf16)], (ids, q, kv, dattn, attn, lse, qseg, dqt0), 5,
            [room((BLK, HALF)), room(head), room(head)],
        )
        return pieces, got, payload, part, dbi

    part_outs = [((4, BLK, D), bf16), ((4, BLK, D), bf16)]
    pieces, got, payload1, part, dbi1 = back(q_1, kv_1, normed1, w1, saved1, gr_top, dattn_top, 384)
    mine, away, payload1 = call(
        combine_kernel, "combine", part_outs + [((8, 384, 512), bf16)],
        (ids, *pieces, got, cosine, sine, part, *w1, normed1, payload1), 6,
        [room((HALF, 384), bf16), room((8, 96, 512), bf16), room((8, BLK, 384), bf16), dma(1)], raw=(6, 8), out_raw=(2,),
        alias={8: 2}, after=(mixed,),
    )
    terms, sent = scatter(ids, mine, away)
    got_a = lax.all_to_all(payload1, FS, 0, 0, tiled=True)
    g1, gr1, sums1 = call(
        bwd_end_kernel, "bwd_end", [(blk, f32), (blk, bf16), ((8, D), f32)], (ids, *terms, x1, gain, cotangent[0]), 2,
        vm=range(1, 8), out_vm=(0, 1, 2), limit=8,
    )
    g_blocks = gather_blocks(gr1)
    gr, dattn = grad_in(ids, g_blocks, wo[0], 0)
    pieces, got, payload, part, dbi0 = back(q_0, kv_0, normed0, w0, saved0, gr, dattn, 400)
    low1, p1 = over_groups(ids, "fsum_top", got_a, pieces[:1])
    (main1,) = call(xsum_top_kernel, "xsum_top", [((352, 512), bf16)], (ids, low1, shift(low1, "xh", 1, 2)), 2)
    mine, away, payload = call(
        combine_first_kernel, "combine_first", part_outs + [((8, 400, 512), bf16)],
        (ids, *pieces, got, cosine, sine, part, wq0, xhat0, normed0, sums1, dbi0, dbi1, payload), 9,
        [room((HALF, 384), bf16), room((8, 112, 512), bf16), dma(1)], raw=(12,), out_raw=(2,), alias={12: 2}, after=(main1,),
    )
    terms, sent = scatter(ids, mine, away)
    (g0,) = call(
        bwd_last_kernel, "bwd_last", [(blk, f32)], (ids, *terms, own, gain, g1), 2, vm=range(1, 8), out_vm=(0,), limit=8
    )
    top_rows = gather_blocks(main1)
    shapes = [((2, BLK, 4096), f32), ((2, 512, D), f32), ((2, BLK, 3 * D), f32)]
    rooms = lambda n: [room(s[0][1:]) for s in shapes] + [room((4, 2, n, 512), bf16), dma(8), dma(3)]
    outs = call(assemble_top_kernel, "assemble_top", shapes, (ids, *top_rows), 5, rooms(352), raw=range(1, 9), out_raw=(0, 1, 2))
    low0, p0 = over_groups(ids, "fsum_first", lax.all_to_all(payload, FS, 0, 0, tiled=True), (g0, outs[2]))
    swap = lambda x: shift(x, "xh", 1, 2)
    (last,) = call(
        xsum_last_kernel, "xsum_last", [((432, 512), bf16)], (ids, low0, swap(low0), p0, swap(p0), p1, swap(p1)), 2,
    )
    last_blocks = gather_blocks(last)
    o_i, o_f, o_q, o_o, o_g, o_s, o_bf, o_bi = call(
        finish_kernel, "finish", shapes + [((2, BLK, D), f32)] + [((2, BLK), f32)] * 3 + [((2, 512), f32)],
        (ids, *last_blocks, *outs), 6, rooms(432), raw=range(1, 12), out_raw=(0, 1, 2),
        alias={9: 0, 10: 1, 11: 2},
    )
    return mixed[None], g0[None], o_g, o_s, o_q, o_o, o_i, o_bi, o_f, o_bf


def solution(mesh):
    fine = Mesh(mesh.devices.reshape(2, 4, 2, 4, 2), AXES)
    seq = ("xh", "y", "core")
    tok = P(FS, seq, None)
    two = P(None, FS)
    three = P(None, FS, None)
    in_specs = (tok, P(FS, None), two, two, three, three, three, two, three, two, tok)
    out_specs = (tok, tok, two, two, three, three, three, two, three, two)
    return jax.shard_map(body, mesh=fine, in_specs=in_specs, out_specs=out_specs, check_vma=False)
```

```python
import functools
import jax
import jax.numpy as jnp
from jax import lax
from jax.experimental import pallas as pl
from jax.experimental.pallas import tpu as pltpu
from jax.sharding import Mesh, PartitionSpec as P

ROT = 32
CONTS = 8
D = 1024
HALF = 1024
BLK = 128
QB = 256
AXES = ("xh", "y", "core", "z", "xl")
FS = ("z", "xl")
f32 = jnp.float32
bf16 = jnp.bfloat16
NT = (((1,), (1,)), ((), ()))
VM = pl.BlockSpec(memory_space=pltpu.VMEM)
SM = pl.BlockSpec(memory_space=pltpu.SMEM)
ANY = pl.BlockSpec(memory_space=pl.ANY)
HBM = pl.BlockSpec(memory_space=pltpu.HBM)
MB = 1024 * 1024


def sds(*args):
    return [jax.ShapeDtypeStruct(s, t) for s, t in args]


class Far:
    def __init__(self, ref, copy):
        self.ref, self.copy = ref, copy

    def here(self):
        if self.copy is not None:
            self.copy.wait()
            self.copy = None
        return self.ref

    def __getitem__(self, index):
        return self.here()[index]

    @property
    def shape(self):
        return self.ref.shape


class Out:
    def __init__(self, ref, copy):
        self.ref, self.copy, self.sent = ref, copy, False

    def __getitem__(self, index):
        return self.ref[index]

    def __setitem__(self, index, value):
        self.ref[index] = value

    @property
    def dtype(self):
        return self.ref.dtype

    @property
    def shape(self):
        return self.ref.shape

    def send(self):
        self.copy.start()
        self.sent = True


COST = 0.001
LIMIT = 51


def call(kernel, name, outs, args, us, scratch=(), limit=None, after=(), raw=(), vm=(), out_raw=(), out_vm=(), alias=None):
    n, m = len(args), len(outs)
    fetched = [i for i in range(1, n) if i not in raw and i not in vm]
    staged = [i for i in range(m) if i not in out_raw and i not in out_vm]

    def run(*refs):
        ins = list(refs[:n])
        results = list(refs[n + len(after) : n + len(after) + m])
        rest = list(refs[n + len(after) + m :])
        own, rest = rest[: len(scratch)], rest[len(scratch) :]
        sems = rest[-1]
        copies = []
        for k, i in enumerate(fetched):
            copy = pltpu.make_async_copy(ins[i], rest[k], sems.at[k])
            copies.append(copy)
            ins[i] = Far(rest[k], copy)
        for copy in copies:
            copy.start()
        for k, i in enumerate(staged):
            ref = rest[len(fetched) + k]
            results[i] = Out(ref, pltpu.make_async_copy(ref, results[i], sems.at[len(fetched) + k]))
        kernel(*ins, *results, *own)
        for i in fetched:
            ins[i].here()
        for i in staged:
            if not results[i].sent:
                results[i].send()
        for i in staged:
            results[i].copy.wait()

    room = [pltpu.VMEM(args[i].shape, args[i].dtype) for i in fetched]
    room += [pltpu.VMEM(outs[i][0], outs[i][1]) for i in staged]
    return pl.pallas_call(
        run,
        out_shape=sds(*outs),
        in_specs=[SM] + [VM if i in vm else HBM for i in range(1, n)] + [ANY] * len(after),
        out_specs=[VM if i in out_vm else HBM for i in range(m)],
        scratch_shapes=list(scratch) + room + [pltpu.SemaphoreType.DMA((max(1, len(room)),))],
        input_output_aliases=alias or {},
        compiler_params=pltpu.CompilerParams(vmem_limit_bytes=(limit or LIMIT) * MB),
        cost_estimate=pl.CostEstimate(flops=int(us * COST * 1e9), bytes_accessed=int(us * COST * 1e6), transcendentals=0),
        name=name,
    )(*args, *after)


def dma(n):
    return pltpu.SemaphoreType.DMA((n,))


def copy_all(pairs, sems):
    copies = [pltpu.make_async_copy(a, b, sems.at[i]) for i, (a, b) in enumerate(pairs)]
    for copy in copies:
        copy.start()
    return copies


def wait_all(copies):
    for copy in copies:
        copy.wait()


def shift(x, axis, by, size):
    return lax.ppermute(x, axis, [(i, (i + by) % size) for i in range(size)])


def gather_blocks(own, hold=None):
    one = shift(own, "y", -1, 4)
    three = shift(own, "y", 1, 4)
    two = shift(own, "y", 2, 4)
    if hold is not None:
        one, two, three = hold(one, two, three)
    blocks = []
    for mine in (own, one, two, three):
        blocks += [mine, shift(mine, "core", 1, 2)]
    return blocks


def spread(low):
    return [shift(low[r - 1], "y", r, 4) for r in (1, 2, 3)]


def transpose_owner(x):
    pairs = [(j * 8 + f, f * 8 + j) for j in range(8) for f in range(8)]
    return lax.ppermute(x, ("y", "core", "z", "xl"), pairs)


def gate(ids, x, after):
    (out,) = call(lambda *refs: None, "gate", [(x.shape, x.dtype)], (ids, x), 1, raw=(1,), out_raw=(0,), after=after, alias={1: 0})
    return out


def gate_all(ids, xs, after):
    n = len(xs)
    return call(
        lambda *refs: None, "gate", [(x.shape, x.dtype) for x in xs], (ids, *xs), 1, raw=range(1, n + 1), out_raw=range(n),
        after=after, alias={i + 1: i for i in range(n)},
    )


def gather_fsdp(ids, x, got, after=()):
    (pair,) = call(
        pair_kernel, "pair", [((2,) + x.shape, bf16)], (ids, x, got), 2, [dma(2)], out_raw=(0,), after=after, limit=62,
    )
    return [pair, shift(pair, "z", -1, 4), shift(pair, "z", 2, 4), shift(pair, "z", 1, 4)]


def weight_copies(ids, pairs, cols, room):
    if len(pairs) == 1:
        return [(pairs[0].at[:, :, cols], room)]
    out = []
    for r in range(4):
        out.append((pairs[r].at[:, :, cols], room.at[pl.ds(2 * lax.rem(ids[4] + r, 4), 2)]))
    return out


def slot(ids, r, s):
    y = lax.rem(ids[0] + r, 4)
    c = ids[1] if s == 0 else 1 - ids[1]
    return y * 2 + c


def rows_of(ids, r, s, n=BLK):
    return pl.ds(pl.multiple_of(slot(ids, r, s) * n, n), n)


def turn(v, cosine, sine):
    lane = lax.broadcasted_iota(jnp.int32, v.shape, 1)
    partner = jnp.where(lane % 2 == 0, pltpu.roll(v, BLK - 1, 1), pltpu.roll(v, 1, 1))
    return v * cosine + partner * sine


def stats(x):
    average = jnp.mean(x, axis=-1, keepdims=True)
    centred = x - average
    variance = jnp.mean(centred * centred, axis=-1, keepdims=True)
    inv = lax.rsqrt(variance + 1e-05)
    return centred * inv, inv


def gelu_both(x):
    a = 0.7978845608028654
    b = 0.044715
    sq = x * x
    t = jnp.tanh(a * x * (1.0 + b * sq))
    half = 0.5 * (1.0 + t)
    slope = half + 0.5 * x * (1.0 - t * t) * a * (1.0 + 3.0 * b * sq)
    return x * half, slope


def dot(a, b):
    return jnp.dot(a, b, preferred_element_type=f32)


def dot_nt(a, b):
    return lax.dot_general(a, b, NT, preferred_element_type=f32)


def pack_q_kernel(ids, wq, gain, bias, bfc, bin_, q0, room, small, binv, sems, out_sems):
    j = ids[0] * 2 + ids[1]
    pairs = []
    for part in range(3):
        cols = pl.ds(pl.multiple_of(part * D + j * BLK, BLK), BLK)
        pairs.append((wq.at[0, :, cols], room.at[0:BLK, part * BLK : part * BLK + BLK]))
    pairs += [(ref, small.at[i]) for i, ref in enumerate((gain, bias, bfc))]
    pairs.append((bin_, binv))
    wait_all(copy_all(pairs, sems))
    chunk = binv[:, pl.ds(pl.multiple_of((j // 2) * BLK, BLK), BLK)].astype(f32)
    chunk = jnp.where(j % 2 == 1, pltpu.roll(chunk, 64, 1), chunk)
    lane = lax.broadcasted_iota(jnp.int32, (1, BLK), 1)
    row2 = jnp.where(lane < 64, chunk[0:1], pltpu.roll(chunk, 64, 1)[1:2])
    blank = jnp.zeros((13, BLK), f32)
    cols = [jnp.concatenate([small[i].astype(f32), row2, blank], 0) for i in range(3)]
    room[BLK:, :] = jnp.concatenate(cols, 1).astype(bf16)
    wait_all(copy_all([(room, q0.at[f]) for f in range(8)], out_sems))


def pack_layer(layer, ids, wi, wf, out, chunks, sems, more=()):
    j = ids[0] * 2 + ids[1]
    rows = pl.ds(pl.multiple_of(j * 64, 64), 64)
    pairs = []
    for f in range(8):
        cols = pl.ds(pl.multiple_of(f * 512 + (j // 2) * BLK, BLK), BLK)
        pairs.append((wi.at[layer, :, cols], chunks.at[f]))
    pairs.append((wf.at[layer, rows, 0:512], out.ref.at[0:64, 512:1024]))
    pairs.append((wf.at[layer, rows, 512:1024], out.ref.at[64:128, 512:1024]))
    wait_all(copy_all(pairs + list(more), sems))
    lane = lax.broadcasted_iota(jnp.int32, (BLK, BLK), 1)
    odd = j % 2 == 1
    for pair in range(4):
        a = chunks[2 * pair].astype(f32)
        b = chunks[2 * pair + 1].astype(f32)
        first = jnp.where(odd, pltpu.roll(a, 64, 1), a)
        second = jnp.where(odd, b, pltpu.roll(b, 64, 1))
        out[:, pair * BLK : pair * BLK + BLK] = jnp.where(lane < 64, first, second).astype(bf16)


def pack_first_kernel(ids, wi, wf, out, chunks, sems):
    pack_layer(0, ids, wi, wf, out, chunks, sems)


def pack_second_kernel(ids, wi, wf, wq, out, chunks, sems):
    j = ids[0] * 2 + ids[1]
    more = []
    for part in range(3):
        cols = pl.ds(pl.multiple_of(part * D + j * BLK, BLK), BLK)
        more.append((wq.at[1, :, cols], out.ref.at[:, D + part * BLK : D + part * BLK + BLK]))
    pack_layer(1, ids, wi, wf, out, chunks, sems, more)


def pass_kernel(layer, ids, x, out, sems):
    wait_all(copy_all([(x.at[layer], out.ref)], sems))


def join_kernel(ids, a, b, out, sems):
    wait_all(copy_all([(a, out.ref.at[0:BLK]), (b, out.ref.at[BLK : 2 * BLK])], sems))


def pair_kernel(ids, own, got, out, sems):
    xl = ids[3]
    wait_all(copy_all([(own.here(), out.at[xl]), (got.here(), out.at[1 - xl])], sems))


def four_kernel(ids, own, got, out, sems):
    xl = ids[3]
    mine, other = own.here(), got.here()
    wait_all(copy_all([(src, out.at[z, at]) for z in range(4) for src, at in ((mine, xl), (other, 1 - xl))], sems))


def params_part(rows_of_f, gain, bias, bfc, bi):
    lane = lax.broadcasted_iota(jnp.int32, (1, BLK), 1)
    for f in range(8):
        cols = slice(f * BLK, f * BLK + BLK)
        rows = rows_of_f[f].astype(f32)
        gain[:, cols] = rows[0:2, 0:BLK]
        bias[:, cols] = rows[0:2, BLK : 2 * BLK]
        bfc[:, cols] = rows[0:2, 2 * BLK :]
    for pair in range(4):
        a = rows_of_f[2 * pair].astype(f32)[2:3, :BLK]
        b = rows_of_f[2 * pair + 1].astype(f32)[2:3, :BLK]
        cols = slice(pair * BLK, pair * BLK + BLK)
        bi[0:1, cols] = jnp.where(lane < 64, a, pltpu.roll(b, 64, 1))
        bi[1:2, cols] = jnp.where(lane < 64, pltpu.roll(a, 64, 1), b)


def qkv_part(normed, w, cosine, sine, q, kv):
    for i in range(HALF // QB):
        rows = slice(i * QB, i * QB + QB)
        out = dot(normed[rows, :], w).astype(bf16).astype(f32)
        cb = cosine[rows, :]
        sb = sine[rows, :]
        kv[rows, :BLK] = turn(out[:, BLK : 2 * BLK], cb, sb).astype(bf16)
        kv[rows, BLK:] = out[:, 2 * BLK :].astype(bf16)
        q[rows, :] = (turn(out[:, :BLK], cb, sb).astype(bf16).astype(f32) * 0.125).astype(bf16)


def take_blocks(ids, blocks, room, sems, at=0):
    part = slice(at, at + BLK)
    return copy_all([(blocks[2 * r + s].at[part], room.at[rows_of(ids, r, s)]) for r in range(4) for s in range(2)], sems)


def qkv_first_kernel(ids, *refs):
    blocks, (wq, cosine, sine), refs = refs[:8], refs[8:11], refs[11:]
    normed, xhat, q, kv, gain, bias, bfc, bi, raw, sems = refs
    copies = take_blocks(ids, blocks, raw, sems)
    w = wq.here()
    params_part([w[f, BLK:, :] for f in range(8)], gain, bias, bfc, bi)
    wait_all(copies)
    for i in range(HALF // QB):
        rows = slice(i * QB, i * QB + QB)
        x, _ = stats(raw[rows, :].astype(f32))
        xhat[rows, :] = x.astype(bf16)
        normed[rows, :] = (x * gain[0:1, :] + bias[0:1, :]).astype(bf16)
    xhat.send()
    normed.send()
    qkv_part(normed, w[:, :BLK, :].reshape(D, 384), cosine, sine, q, kv)


def qkv_kernel(ids, *refs):
    blocks, w, (cosine, sine), (normed, q, kv, wq, sems, wsem) = refs[:8], refs[8:9], refs[9:11], refs[11:]
    copies = copy_all(weight_copies(ids, w, slice(1024, 1408), wq), wsem)
    copies += take_blocks(ids, blocks, normed.ref, sems)
    wait_all(copies)
    normed.send()
    qkv_part(normed, wq[...].reshape(D, 384), cosine, sine, q, kv)


def ff_kernel(layer, ids, far, bi, *refs):
    w, (active, slope, feed, wi, wf, va, vs, vf, wsems, sems, normed) = refs[:-11], refs[-11:]
    copies = copy_all(weight_copies(ids, w, slice(0, 512), wi), wsems.at[0])
    rows = slice(0, QB)
    copies += copy_all([(far.at[rows], normed.at[rows])], wsems.at[2])
    late = copy_all(weight_copies(ids, w, slice(512, 1024), wf), wsems.at[1])
    rows = slice(QB, HALF)
    rest = copy_all([(far.at[rows], normed.at[rows])], wsems.at[3])
    wait_all(copies)
    left = right = None
    sent = []
    for i in range(HALF // QB):
        rows = slice(i * QB, i * QB + QB)
        if i == 1:
            wait_all(rest)
        pre = dot(normed[rows, :], wi[...].reshape(D, 512)) + bi[layer : layer + 1, :]
        act, der = gelu_both(pre)
        act = act.astype(bf16)
        va[rows, :] = act
        vs[rows, :] = der.astype(bf16)
        if i == 0:
            wait_all(late)
            left, right = wf[:, 0:64, :].reshape(512, 512), wf[:, 64:128, :].reshape(512, 512)
        vf[rows, :512] = dot(act, left).astype(bf16)
        vf[rows, 512:] = dot(act, right).astype(bf16)
        pairs = [(v.at[rows], out.at[rows]) for v, out in ((va, active), (vs, slope), (vf, feed))]
        sent += copy_all(pairs, sems.at[i])
    wait_all(sent)


def ff(ids, layer, normed, w, bi, after=()):
    room = lambda *shape: pltpu.VMEM(shape, bf16)
    return call(
        functools.partial(ff_kernel, layer), "ff", [((HALF, 512), bf16), ((HALF, 512), bf16), ((HALF, D), bf16)],
        (ids, normed, bi, *w), 5,
        [room(8, BLK, 512), room(8, BLK, 512), room(HALF, 512), room(HALF, 512), room(HALF, D),
         pltpu.SemaphoreType.DMA((4, 4)), pltpu.SemaphoreType.DMA((4, 3)), room(HALF, D)],
        raw=[1, *range(3, 3 + len(w))], out_raw=(0, 1, 2), limit=62 - 11 * layer, after=after,
    )


def head_cut(x):
    lane = lax.broadcasted_iota(jnp.int32, x.shape, 1)
    zero = jnp.zeros((), x.dtype)
    return [jnp.where(lane < 64, x, zero), jnp.where(lane >= 64, x, zero)]


def seen(i, kk, qseg, kseg, QB):
    q0 = i * QB
    qs = qseg[0:1, q0 : q0 + QB]
    ks = kseg[0:kk, 0:1]
    key = lax.broadcasted_iota(jnp.int32, (kk, QB), 0)
    query = q0 + lax.broadcasted_iota(jnp.int32, (kk, QB), 1)
    return (key <= query) & ((ks == 0) | (ks == qs))


def flip(x):
    return jnp.transpose(x.astype(f32)).astype(bf16)


def attn_own_kernel(ids, q, kv, qseg, acc, m_out, l_out):
    qseg = qseg[...]
    kseg = jnp.transpose(qseg)
    km = head_cut(kv[:, :BLK])
    vt = flip(kv[:, BLK:])
    for i in range(HALF // 512):
        cols = slice(i * 512, (i + 1) * 512)
        kk = (i + 1) * 512
        allowed = seen(i, kk, qseg, kseg, 512)
        for h in range(2):
            rows = slice(h * 64, h * 64 + 64)
            s = jnp.where(allowed, dot_nt(km[h][:kk], q[cols, :]), -1e30)
            m = jnp.max(s, axis=0, keepdims=True)
            p = jnp.exp(s - m)
            l_out[h : h + 1, cols] = jnp.sum(p, axis=0, keepdims=True)
            m_out[h : h + 1, cols] = m
            acc[rows, cols] = dot(vt[rows, :kk], p.astype(bf16))


def split_rows(ids, mine, away, block):
    for r in range(4):
        away[r] = block(rows_of(ids, r, 1)).astype(bf16)
    away.send()
    for r in range(4):
        mine[r] = block(rows_of(ids, r, 0)).astype(bf16)


def attn_full_kernel(ids, q, kv0, acc, m_in, l_in, feed, wo, attn, lse, mine, away, tmp):
    upper = ids[2] == 1
    for ref in (q, kv0, acc, m_in, l_in):
        ref.here()

    @pl.when(upper)
    def _():
        km = head_cut(kv0[:, :BLK])
        vt = flip(kv0[:, BLK:])
        for i in range(HALF // 512):
            cols = slice(i * 512, (i + 1) * 512)
            for h in range(2):
                rows = slice(h * 64, h * 64 + 64)
                s = dot_nt(km[h], q[cols, :])
                m0 = m_in[h : h + 1, cols]
                m = jnp.maximum(m0, jnp.max(s, axis=0, keepdims=True))
                p = jnp.exp(s - m)
                a = jnp.exp(m0 - m)
                l = l_in[h : h + 1, cols] * a + jnp.sum(p, axis=0, keepdims=True)
                o = dot(vt[rows, :], p.astype(bf16))
                tmp[rows, cols] = (acc[rows, cols] * a + o) / l
                lse[h : h + 1, cols] = m + jnp.log(l)

    @pl.when(jnp.logical_not(upper))
    def _():
        for h in range(2):
            rows = slice(h * 64, h * 64 + 64)
            l = l_in[h : h + 1, :]
            tmp[rows, :] = acc[rows, :] / l
            lse[h : h + 1, :] = m_in[h : h + 1, :] + jnp.log(l)

    attn[...] = jnp.transpose(tmp[...]).astype(bf16)
    attn.send()
    lse.send()
    split_rows(ids, mine, away, lambda rows: feed[rows, :].astype(f32) + dot(attn[rows, :], wo[...]))


def mid_kernel(ids, mine, got, total, one, two, three):
    for r, out in ((1, one), (2, two), (3, three)):
        out[...] = (mine[r].astype(f32) + got[r].astype(f32)).astype(bf16)
    total[...] = mine[0].astype(f32) + got[0].astype(f32)


def summed(total, one, two, three):
    return total[...] + one[...].astype(f32) + two[...].astype(f32) + three[...].astype(f32)


def fwd_end_kernel(ids, total, one, two, three, x, gain, bias, bfc, x_new, normed):
    new = x[...].astype(f32) + summed(total, one, two, three) + bfc[0:1, :]
    x_new[...] = new
    xhat, _ = stats(new)
    normed[...] = (xhat * gain[1:2, :] + bias[1:2, :]).astype(bf16)


def last_end_kernel(ids, total, one, two, three, x, bfc, out):
    out[...] = (x[...] + summed(total, one, two, three) + bfc[1:2, :]).astype(bf16)


def grad_in_kernel(at, ids, *refs):
    blocks, (wo, gr, dattn, sems) = refs[:8], refs[8:]
    wait_all(take_blocks(ids, blocks, gr.ref, sems, at))
    gr.send()
    dattn[...] = dot_nt(gr[...], wo[...]).astype(bf16)


def row_delta(attn, do):
    prod = attn[...].astype(f32) * do[...].astype(f32)
    head = lax.broadcasted_iota(jnp.int32, (8, BLK), 0)
    lane = lax.broadcasted_iota(jnp.int32, (8, BLK), 1) // 64
    pickers = jnp.where(head == lane, 1.0, 0.0).astype(f32)
    return lax.dot_general(pickers, prod, NT, precision=lax.Precision.HIGHEST, preferred_element_type=f32)


def grad_block(km, vm, kt, qm, dom, q_blk, do_blk, lse, delta, allowed):
    p = jnp.exp(dot_nt(km, q_blk) - lse)
    if allowed is not None:
        p = jnp.where(allowed, p, 0.0)
    dp = dot_nt(vm, do_blk)
    ds = (p * (dp - delta)).astype(bf16)
    return dot(kt, ds), dot(ds, qm), dot(p.astype(bf16), dom)


def grad_full_kernel(ids, q, kv0, do, attn, lse, dqt, dkv, acck, accv):
    upper = ids[2] == 1
    for ref in (q, kv0, do, attn, lse):
        ref.here()

    @pl.when(upper)
    def _():
        delta = row_delta(attn, do)
        qm, km, vm, dom = [head_cut(x) for x in (q[...], kv0[:, :BLK], kv0[:, BLK:], do[...])]
        kt = flip(kv0[:, :BLK])
        for i in range(HALF // 512):
            cols = slice(i * 512, (i + 1) * 512)
            for h in range(2):
                rows = slice(h * 64, h * 64 + 64)
                dq, dk, dv = grad_block(
                    km[h], vm[h], kt[rows, :], qm[h][cols], dom[h][cols], q[cols, :], do[cols, :],
                    lse[h : h + 1, cols], delta[h : h + 1, cols], None,
                )
                dqt[rows, cols] = dq
                if i == 0 and h == 0:
                    acck[...] = dk
                    accv[...] = dv
                else:
                    acck[...] += dk
                    accv[...] += dv
        dkv[:, :BLK] = acck[...].astype(bf16)
        dkv[:, BLK:] = accv[...].astype(bf16)

    @pl.when(jnp.logical_not(upper))
    def _():
        dqt[...] = jnp.zeros(dqt.shape, f32)
        dkv[...] = jnp.zeros(dkv.shape, bf16)


def grad_own_kernel(ids, q, kv, do, attn, lse, qseg, dqt0, out, tmp, dk_out, dv_out):
    qseg = qseg[...]
    kseg = jnp.transpose(qseg)
    delta = row_delta(attn, do)
    qm, km, vm, dom = [head_cut(x) for x in (q[...], kv[:, :BLK], kv[:, BLK:], do[...])]
    kt = flip(kv[:, :BLK])
    dk_out[...] = jnp.zeros(dk_out.shape, f32)
    dv_out[...] = jnp.zeros(dv_out.shape, f32)
    for i in range(HALF // 256):
        cols = slice(i * 256, (i + 1) * 256)
        kk = (i + 1) * 256
        allowed = seen(i, kk, qseg, kseg, 256)
        for h in range(2):
            rows = slice(h * 64, h * 64 + 64)
            dq, dk, dv = grad_block(
                km[h][:kk], vm[h][:kk], kt[rows, :kk], qm[h][cols], dom[h][cols], q[cols, :], do[cols, :],
                lse[h : h + 1, cols], delta[h : h + 1, cols], allowed,
            )
            tmp[rows, cols] = (dq + dqt0[rows, cols]) * 0.125
            dk_out[:kk, :] += dk
            dv_out[:kk, :] += dv
    out[:, :BLK] = jnp.transpose(tmp[...]).astype(bf16)
    out[:, BLK : 2 * BLK] = dk_out[...].astype(bf16)
    out[:, 2 * BLK :] = dv_out[...].astype(bf16)


def ff_back_outer_kernel(ids, *refs):
    far, w, refs = refs[:5], refs[5:-14], refs[-14:]
    part, dbi, out, wi, wf, vd, v, wsems, sems, gr, slope, active, attn, normed = refs
    rooms = (gr, slope, active, attn, normed)
    copies = copy_all(weight_copies(ids, w, slice(512, 1024), wf), wsems.at[0])
    rows = slice(0, 256)
    first = [(far[0].at[rows], gr.at[rows]), (far[1].at[rows], slope.at[rows])]
    copies += copy_all(first, wsems.at[2])
    late = copy_all(weight_copies(ids, w, slice(0, 512), wi), wsems.at[1])
    rows = slice(256, HALF)
    rest = copy_all([(far[0].at[rows], gr.at[rows]), (far[1].at[rows], slope.at[rows])], wsems.at[3])
    after = copy_all([(far[k], rooms[k]) for k in (2, 3, 4)], wsems.at[4])
    wait_all(copies)
    left, right = wf[:, 0:64, :].reshape(512, 512), wf[:, 64:128, :].reshape(512, 512)
    total = jnp.zeros((1, 512), f32)
    for i in range(HALF // 256):
        if i == 1:
            wait_all(rest)
        rows = slice(i * 256, i * 256 + 256)
        d = (dot_nt(gr[rows, :512], left) + dot_nt(gr[rows, 512:], right)) * slope[rows, :].astype(f32)
        total = total + jnp.sum(d, axis=0, keepdims=True)
        d = d.astype(bf16)
        vd[rows, :] = d
        if i == 0:
            wait_all(late)
        part[rows, :] = dot_nt(d, wi[...].reshape(D, 512)).astype(bf16)
    part.send()
    dbi[...] = jnp.concatenate([total, jnp.zeros((7, 512), f32)], 0)
    wait_all(after)
    wait_all(outer_rows(out, v, sems, active, gr, attn, normed, vd))


def ff_back_outer(ids, rows, gr, slope, active, attn, normed, w, after):
    room = lambda *shape: pltpu.VMEM(shape, bf16)
    return call(
        ff_back_outer_kernel, "ff_back_outer", [((HALF, D), bf16), ((8, 512), f32), ((8, rows, 512), bf16)],
        (ids, gr, slope, active, attn, normed, *w), 9,
        [room(8, BLK, 512), room(8, BLK, 512), room(HALF, 512), room(8, 288, 512), pltpu.SemaphoreType.DMA((5, 4)),
         pltpu.SemaphoreType.DMA((3, 2)), room(HALF, D), room(HALF, 512), room(HALF, 512), room(HALF, BLK), room(HALF, D)],
        raw=range(1, 6 + len(w)), out_raw=(2,), after=after,
    )


def combine_rows(ids, own, back, cosine, sine, dqkv):
    cb = cosine[...]
    sb = -sine[...]
    dqkv[:, :BLK] = turn(own[:, :BLK].astype(f32), cb, sb).astype(bf16)
    dk = own[:, BLK : 2 * BLK].astype(f32) + back[:, :BLK].astype(f32)
    dqkv[:, BLK : 2 * BLK] = turn(dk, cb, sb).astype(bf16)
    dqkv[:, 2 * BLK :] = (own[:, 2 * BLK :].astype(f32) + back[:, BLK:].astype(f32)).astype(bf16)


def combine_kernel(ids, own, back, cosine, sine, part, w1, normed, _, mine, away, payload, dqkv, out, wq, wsem):
    copies = copy_all(weight_copies(ids, (w1,), slice(1024, 1408), wq), wsem)
    combine_rows(ids, own, back, cosine, sine, dqkv)
    wait_all(copies)
    w = wq[...].reshape(D, 384)
    split_rows(ids, mine, away, lambda rows: part[rows, :].astype(f32) + dot_nt(dqkv[rows, :], w))
    mine.send()
    g_q = outer(normed[...], dqkv[...])
    for f in range(8):
        pack_rows(out, f, g_q)
    wait_all(copy_all([(out, payload.at[:, 288:384])], wsem))


def combine_first_kernel(ids, own, back, cosine, sine, wq0, part, xhat, normed, sums1, dbi0, dbi1, *refs):
    _, mine, away, payload, dqkv, out, sems = refs
    combine_rows(ids, own, back, cosine, sine, dqkv)
    w = wq0[:, :BLK, :].reshape(D, 384)
    gain = jnp.zeros((1, D), f32)
    base = jnp.zeros((1, D), f32)
    for s, to in ((1, away), (0, mine)):
        for r in range(4):
            rows = rows_of(ids, r, s)
            block = part[rows, :].astype(f32) + dot_nt(dqkv[rows, :], w)
            to[r] = block.astype(bf16)
            gain = gain + jnp.sum(block * xhat[rows, :].astype(f32), axis=0, keepdims=True)
            base = base + jnp.sum(block, axis=0, keepdims=True)
        to.send()
    g_q = outer(normed[...], dqkv[...])
    lane = lax.broadcasted_iota(jnp.int32, (1, BLK), 1)
    blank = jnp.zeros((13, 384), f32)
    none = jnp.zeros((1, 256), f32)
    for f in range(8):
        pack_rows(out, f, g_q)
        cols = slice(f * BLK, f * BLK + BLK)
        row0 = jnp.concatenate([gain[:, cols], base[:, cols], sums1[3:4, cols]], 1)
        row1 = jnp.concatenate([sums1[0:1, cols], sums1[1:2, cols], sums1[2:3, cols]], 1)
        half = slice((f // 2) * BLK, (f // 2) * BLK + BLK)
        a = dbi0[0:1, half]
        b = dbi1[0:1, half]
        if f % 2 == 0:
            b = pltpu.roll(b, 64, 1)
        else:
            a = pltpu.roll(a, 64, 1)
        row2 = jnp.concatenate([jnp.where(lane < 64, a, b), none], 1)
        out[f, 96:112, :384] = jnp.concatenate([row0, row1, row2, blank], 0).astype(bf16)
        out[f, 96:112, 384:] = jnp.zeros((16, 128), bf16)
    wait_all(copy_all([(out, payload.at[:, 288:400])], sems))


def norm_back(dn, x, gain_row, g):
    xhat, inv = stats(x[...].astype(f32))
    dx = dn * gain_row
    dx = inv * (dx - jnp.mean(dx, -1, keepdims=True) - xhat * jnp.mean(dx * xhat, -1, keepdims=True))
    return xhat, g[...].astype(f32) + dx


def bwd_end_kernel(ids, total, one, two, three, x, gain, g, g_new, gr, sums):
    dn = summed(total, one, two, three)
    xhat, new = norm_back(dn, x, gain[1:2, :], g)
    g_new[...] = new
    gr[...] = new.astype(bf16)
    col = lambda v: jnp.sum(v, axis=0, keepdims=True)
    top = col(g[...].astype(f32))
    sums[...] = jnp.concatenate([col(dn * xhat), col(dn), top, col(new), jnp.zeros((4, D), f32)], 0)


def bwd_last_kernel(ids, total, one, two, three, x, gain, g, g_new):
    _, new = norm_back(summed(total, one, two, three), x, gain[0:1, :], g)
    g_new[...] = new


def outer(a, b):
    return lax.dot_general(a, b, (((0,), (0,)), ((), ())), preferred_element_type=f32).astype(bf16)


def pack_rows(out, f, g_q):
    for part in range(3):
        for group in range(4):
            piece = g_q[f * 128 + group * 32 : f * 128 + group * 32 + 32, part * BLK : part * BLK + BLK]
            out[f, part * 32 : part * 32 + 32, group * BLK : group * BLK + BLK] = piece


def outer_rows(out, v, sems, active, gr, attn, normed, dpre):
    for half in range(2):
        cols = slice(half * 512, half * 512 + 512)
        g_f = outer(active[...], gr[:, cols])
        g_o = outer(attn[...], gr[:, cols])
        for f in range(8):
            v[f, 128 + 64 * half : 192 + 64 * half, :] = g_f[f * 64 : f * 64 + 64]
            v[f, 256 + 16 * half : 272 + 16 * half, :] = g_o[f * 16 : f * 16 + 16]
    first = copy_all([(v.at[:, 128:288], out.at[:, 128:288])], sems.at[0])
    for half in range(2):
        cols = slice(half * 512, half * 512 + 512)
        g_i = outer(normed[:, cols], dpre[...])
        for k in range(4):
            v[4 * half + k, 0:128, :] = g_i[k * 128 : k * 128 + 128]
        group = slice(4 * half, 4 * half + 4)
        first += copy_all([(v.at[group, 0:128], out.at[group, 0:128])], sems.at[1 + half])
    return first


def fsum_kernel(ids, got, *refs):
    more, (low, piece, room, sems) = refs[:-4], refs[-4:]
    rows = got.shape[1]
    half = rows // 32 * 16
    parts = (slice(0, half), slice(half, rows))
    copies = copy_all([(got.at[:, part], room.at[:, part]) for part in parts], sems)
    for at in range(0, rows, 16):
        if at in (0, half):
            copies[0 if at == 0 else 1].wait()
        part = slice(at, at + 16)
        total = room[0, part, :].astype(f32)
        for f in range(1, 8):
            total = total + room[f, part, :].astype(f32)
        total = total.astype(bf16)
        if 256 <= at < 288:
            piece[at - 256 : at - 240, :] = total
        else:
            to = at if at < 256 else at - 32
            low[to : to + 16, :] = total
    for ref in more:
        piece[32:64, :] = ref[...]


def add_rows(terms, start, stop):
    total = terms[0][start:stop, :].astype(f32)
    for term in terms[1:]:
        total = total + term[start:stop, :].astype(f32)
    return total.astype(bf16)


def xsum_top_kernel(ids, low, got, main):
    main[...] = add_rows((low, got), 0, 352)


def xsum_last_kernel(ids, low, got, piece, piece_got, main):
    terms = (low, got)
    main[0:112, :] = add_rows(terms, 256, 368)
    main[112:368, :] = add_rows(terms, 0, 256)
    main[368:432, :] = add_rows((piece, piece_got), 0, 64)


def over_groups(ids, name, got, more=(), after=()):
    rows = got.shape[1]
    return call(
        fsum_kernel, name, [((rows - 32, 512), bf16), ((32 + 32 * len(more), 512), bf16)], (ids, got, *more), 3,
        [pltpu.VMEM(got.shape, bf16), dma(2)], raw=(1,), after=after,
    )


def place_in(zero, one, at, y, o_i, o_f):
    lane = lax.broadcasted_iota(jnp.int32, (BLK, BLK), 1)
    start = pl.multiple_of(y * BLK, BLK)
    for half in range(2):
        rows = slice(at + 128 + 64 * half, at + 192 + 64 * half)
        cols = slice(half * 512, half * 512 + 512)
        o_f[pl.ds(start, 64), cols] = zero[rows, :].astype(f32)
        o_f[pl.ds(start + 64, 64), cols] = one[rows, :].astype(f32)
    for pair in range(4):
        cols = slice(pair * BLK, pair * BLK + BLK)
        a, b = zero[at : at + BLK, cols].astype(f32), one[at : at + BLK, cols].astype(f32)
        even = pl.ds(pl.multiple_of(2 * pair * 512 + start, BLK), BLK)
        odd = pl.ds(pl.multiple_of((2 * pair + 1) * 512 + start, BLK), BLK)
        o_i[:, even] = jnp.where(lane < 64, a, pltpu.roll(b, 64, 1))
        o_i[:, odd] = jnp.where(lane < 64, pltpu.roll(a, 64, 1), b)


def place_q(zero, one, at, y, o_q):
    for part in range(3):
        rows = slice(at + part * 32, at + part * 32 + 32)
        start = pl.multiple_of(part * D + 2 * y * BLK, BLK)
        for group in range(4):
            cols = slice(group * BLK, group * BLK + BLK)
            to = slice(group * 32, group * 32 + 32)
            o_q[to, pl.ds(start, BLK)] = zero[rows, cols].astype(f32)
            o_q[to, pl.ds(start + BLK, BLK)] = one[rows, cols].astype(f32)


def fetch_rows(ids, blocks, room, sems):
    pairs = []
    for r in range(4):
        pairs += [(blocks[2 * r], room.at[r, ids[1]]), (blocks[2 * r + 1], room.at[r, 1 - ids[1]])]
    return copy_all(pairs, sems)


def assemble_top_kernel(ids, *refs):
    blocks, (o_i, o_f, o_q, vi, vf, vq, room, sems, out_sems) = refs[:8], refs[8:]
    copies = fetch_rows(ids, blocks, room, sems)
    for r in range(4):
        wait_all(copies[2 * r : 2 * r + 2])
        y = lax.rem(ids[0] + r, 4)
        place_in(room.at[r, 0], room.at[r, 1], 0, y, vi, vf)
        place_q(room.at[r, 0], room.at[r, 1], 256, y, vq)
    wait_all(copy_all([(vi, o_i.at[1]), (vf, o_f.at[1]), (vq, o_q.at[1])], out_sems))


def finish_kernel(ids, *refs):
    blocks, refs = refs[:8], refs[11:]
    o_i, o_f, o_q, o_o, o_g, o_s, o_bf, o_bi, vi, vf, vq, room, sems, out_sems = refs
    copies = fetch_rows(ids, blocks, room, sems)
    outs = []
    total = jnp.zeros((16, 384), f32)
    lane = lax.broadcasted_iota(jnp.int32, (1, BLK), 1)
    for r in range(4):
        wait_all(copies[2 * r : 2 * r + 2])
        y = lax.rem(ids[0] + r, 4)
        place_in(room.at[r, 0], room.at[r, 1], 112, y, vi, vf)
        rows = pl.ds(pl.multiple_of(y * BLK, BLK), BLK)
        outs += copy_all([(vf.at[rows], o_f.at[0, rows])], out_sems.at[r])
    outs += copy_all([(vi, o_i.at[0])], out_sems.at[4])
    for r in range(4):
        place_q(room.at[r, 0], room.at[r, 1], 0, lax.rem(ids[0] + r, 4), vq)
    outs += copy_all([(vq, o_q.at[0])], out_sems.at[5])
    for r in range(4):
        y = lax.rem(ids[0] + r, 4)
        for layer in range(2):
            for half in range(2):
                at = 368 + 32 * layer + 16 * half
                cols = slice(half * 512, half * 512 + 512)
                start = pl.multiple_of(y * 32, 32)
                o_o[layer, pl.ds(start, 16), cols] = room[r, 0, at : at + 16, :].astype(f32)
                o_o[layer, pl.ds(start + 16, 16), cols] = room[r, 1, at : at + 16, :].astype(f32)
        zero, one = room[r, 0, 96:112, :384].astype(f32), room[r, 1, 96:112, :384].astype(f32)
        total = total + zero + one
        a, b = zero[2:3, :BLK], one[2:3, :BLK]
        cols = pl.ds(pl.multiple_of(y * BLK, BLK), BLK)
        o_bi[0:1, cols] = jnp.where(lane < 64, a, pltpu.roll(b, 64, 1))
        o_bi[1:2, cols] = jnp.where(lane < 64, pltpu.roll(a, 64, 1), b)
    o_g[...] = total[0:2, :BLK]
    o_s[...] = total[0:2, BLK : 2 * BLK]
    o_bf[...] = total[0:2, 2 * BLK :]
    for ref in (o_o, o_g, o_s, o_bf, o_bi):
        ref.send()
    wait_all(outs)


def positions_of(group_seg):
    token_index = jnp.arange(group_seg.shape[0], dtype=jnp.int32)
    labels = jnp.arange(CONTS + 1, dtype=jnp.int32)
    member = (group_seg[:, None] == labels[None, :]).astype(jnp.int32)
    counts = jnp.sum(member, axis=0)
    starts = jnp.cumsum(counts) - counts
    own_start = jnp.sum(member * starts[None, :], axis=1)
    return token_index - own_start + jnp.where(group_seg > 0, counts[0], 0)


def rope_tables(positions):
    lane = jnp.arange(BLK, dtype=jnp.int32) % 64
    inverse = 10000.0 ** (-2.0 * (lane // 2).astype(f32) / ROT)
    phase = positions.astype(f32)[:, None] * jnp.where(lane < ROT, inverse, 0.0)[None, :]
    sign = jnp.where(lane % 2 == 0, -1.0, 1.0)
    return jnp.cos(phase), jnp.sin(phase) * sign[None, :]


def scatter(ids, mine, away):
    got = shift(away, "core", 1, 2)
    blk = (BLK, D)
    total, one, two, three = call(
        mid_kernel, "rs_mid", [(blk, f32)] + [(blk, bf16)] * 3, (ids, mine, got), 2, vm=(2,), out_vm=(0, 1, 2, 3), limit=8
    )
    return [total] + spread([one, two, three]), one


def grad_in(ids, g_blocks, wo, at):
    return call(
        functools.partial(grad_in_kernel, at), "grad_in", [((HALF, D), bf16), ((HALF, BLK), bf16)], (ids, *g_blocks, wo), 3,
        [dma(8)], raw=range(1, 9),
    )


def body(tokens, segment, ln_gain, ln_bias, w_qkv, w_out, w_in, b_in, w_fc, b_fc, cotangent):
    xh = lax.axis_index("xh")
    ids = jnp.stack([lax.axis_index("y"), lax.axis_index("core"), xh, lax.axis_index("xl"), lax.axis_index("z")]).astype(jnp.int32)
    own = tokens[0]
    full = (HALF, D)
    blk = (BLK, D)
    head = (HALF, BLK)
    room = lambda shape, kind=f32: pltpu.VMEM(shape, kind)
    chunks = [room((8, BLK, BLK), bf16)]

    group_seg = segment[0]
    positions = positions_of(group_seg)
    seg = lax.dynamic_slice_in_dim(group_seg, xh * HALF, HALF, 0)
    cosine, sine = rope_tables(lax.dynamic_slice_in_dim(positions, xh * HALF, HALF, 0))
    qseg = jnp.broadcast_to(seg[None, :].astype(f32), (8, HALF))

    (both,) = call(
        join_kernel, "join", [((2 * BLK, D), bf16)], (ids, own, cotangent[0]), 1, [dma(2)], raw=(1, 2), limit=62
    )
    (p0,) = call(
        pack_first_kernel, "pack_first", [(blk, bf16)], (ids, w_in, w_fc), 3, chunks + [dma(10)], raw=(1, 2), limit=62, after=(both,),
    )
    other0 = shift(p0, "xl", 1, 2)
    (q0,) = call(
        pack_q_kernel, "pack_q", [((8, 144, 384), bf16)], (ids, w_qkv, ln_gain, ln_bias, b_fc, b_in), 3,
        [room((144, 384), bf16), room((3, 2, BLK), bf16), room((2, 512), bf16), dma(7), dma(8)],
        raw=(1, 2, 3, 4, 5), out_raw=(0,), after=(cosine, other0), limit=62,
    )
    wq0 = lax.all_to_all(q0, FS, 0, 0, tiled=True)
    (p1,) = call(
        pack_second_kernel, "pack_second", [((BLK, 1408), bf16)], (ids, w_in, w_fc, w_qkv), 3, chunks + [dma(13)], raw=(1, 2, 3), limit=62,
        after=(wq0,),
    )
    tok_blocks = gather_blocks(both, lambda *x: gate_all(ids, x, (q0,)))
    w0 = gather_fsdp(ids, p0, other0)

    def attend_own(layer, q, kv, normed, w, before):
        kv0 = lax.ppermute(kv, "xh", [(0, 1)])
        own_part = call(
            attn_own_kernel, "attn_own", [((BLK, HALF), f32), ((2, HALF), f32), ((2, HALF), f32)], (ids, q, kv, qseg), 5, limit=62 if layer == 0 else None
        )
        first = before(own_part[1:2])
        return kv0, ff(ids, layer, normed, w, bi, first), own_part, first

    def attend_full(layer, q, kv0, act, own_part, after):
        active, slope, feed = act
        attn, lse, mine, away = call(
            attn_full_kernel, "attn_full", [(head, bf16), ((2, HALF), f32)] + [((4, BLK, D), bf16)] * 2,
            (ids, q, kv0, *own_part, feed, wo[layer]), 8, [room((BLK, HALF))], after=after,
        )
        return (kv0, active, slope, attn, lse), (mine, away)

    normed0, xhat0, q_0, kv_0, gain, bias, bfc, bi = call(
        qkv_first_kernel, "qkv_first",
        [(full, bf16), (full, bf16), (head, bf16), ((HALF, 256), bf16)] + [((2, D), f32)] * 3 + [((2, 512), f32)],
        (ids, *tok_blocks, wq0, cosine, sine), 6, [room(full, bf16), dma(8)], raw=range(1, 9), out_vm=(4, 5, 6, 7),
        limit=62,
    )

    def fetch_wo(layer, after):
        (out,) = call(
            functools.partial(pass_kernel, layer), "pass_wo", [(blk, bf16)], (ids, w_out), 1, [dma(1)], raw=(1,), after=after,
            limit=62,
        )
        return transpose_owner(out)

    def spread_w1(after):
        return call(
            four_kernel, "four", [((4, 2, BLK, 1408), bf16)], (ids, p1, shift(p1, "xl", 1, 2)), 2, [dma(8)], out_raw=(0,),
            after=after, limit=62,
        )

    kv0, act, own_part, (four,) = attend_own(0, q_0, kv_0, normed0, w0, spread_w1)
    wo = [fetch_wo(0, own_part[1:2])]
    saved0, ends = attend_full(0, q_0, kv0, act, own_part, ())
    w1 = [lax.all_to_all(gate(ids, four, (saved0[3],)), "z", 0, 0, tiled=True).reshape(8, BLK, 1408)]
    terms, sent = scatter(ids, *ends)
    x1, normed_own = call(
        fwd_end_kernel, "fwd_end", [(blk, f32), (blk, bf16)], (ids, *terms, own, gain, bias, bfc), 2,
        vm=range(1, 9), out_vm=(0, 1), limit=8,
    )
    blocks = gather_blocks(normed_own)
    normed1, q_1, kv_1 = call(
        qkv_kernel, "qkv", [(full, bf16), (head, bf16), ((HALF, 256), bf16)], (ids, *blocks, *w1, cosine, sine), 4,
        [room((8, BLK, 384), bf16), dma(8), dma(1)], raw=range(1, 10),
    )
    kv0, act, own_part, _ = attend_own(1, q_1, kv_1, normed1, w1, lambda after: ())
    wo.append(fetch_wo(1, (q_1,)))
    gr_top, dattn_top = grad_in(ids, tok_blocks, wo[1], BLK)
    saved1, ends = attend_full(1, q_1, kv0, act, own_part, ())
    terms, _ = scatter(ids, *ends)
    (mixed,) = call(
        last_end_kernel, "last_end", [(blk, bf16)], (ids, *terms, x1, bfc), 2, vm=range(1, 7), out_vm=(0,), limit=8
    )

    def back(q, kv, normed, w, saved, gr, dattn, rows):
        kv0, active, slope, attn, lse = saved
        dqt0, dkv0 = call(
            grad_full_kernel, "grad_full", [((BLK, HALF), f32), ((HALF, 256), bf16)], (ids, q, kv0, dattn, attn, lse), 8,
            [room(head)] * 2,
        )
        got = lax.ppermute(dkv0, "xh", [(1, 0)])
        part, dbi, payload = ff_back_outer(ids, rows, gr, slope, active, attn, normed, w, (dqt0,))
        pieces = call(
            grad_own_kernel, "grad_own", [((HALF, 384), bf16)], (ids, q, kv, dattn, attn, lse, qseg, dqt0), 5,
            [room((BLK, HALF)), room(head), room(head)],
        )
        return pieces, got, payload, part, dbi

    part_outs = [((4, BLK, D), bf16), ((4, BLK, D), bf16)]
    pieces, got, payload1, part, dbi1 = back(q_1, kv_1, normed1, w1, saved1, gr_top, dattn_top, 384)
    mine, away, payload1 = call(
        combine_kernel, "combine", part_outs + [((8, 384, 512), bf16)],
        (ids, *pieces, got, cosine, sine, part, *w1, normed1, payload1), 6,
        [room((HALF, 384), bf16), room((8, 96, 512), bf16), room((8, BLK, 384), bf16), dma(1)], raw=(6, 8), out_raw=(2,),
        alias={8: 2}, after=(mixed,),
    )
    terms, sent = scatter(ids, mine, away)
    got_a = lax.all_to_all(payload1, FS, 0, 0, tiled=True)
    g1, gr1, sums1 = call(
        bwd_end_kernel, "bwd_end", [(blk, f32), (blk, bf16), ((8, D), f32)], (ids, *terms, x1, gain, cotangent[0]), 2,
        vm=range(1, 8), out_vm=(0, 1, 2), limit=8,
    )
    g_blocks = gather_blocks(gr1)
    gr, dattn = grad_in(ids, g_blocks, wo[0], 0)
    pieces, got, payload, part, dbi0 = back(q_0, kv_0, normed0, w0, saved0, gr, dattn, 400)
    low1, p1 = over_groups(ids, "fsum_top", got_a, after=pieces[:1])
    (main1,) = call(xsum_top_kernel, "xsum_top", [((352, 512), bf16)], (ids, low1, shift(low1, "xh", 1, 2)), 2)
    mine, away, payload = call(
        combine_first_kernel, "combine_first", part_outs + [((8, 400, 512), bf16)],
        (ids, *pieces, got, cosine, sine, wq0, part, xhat0, normed0, sums1, dbi0, dbi1, payload), 9,
        [room((HALF, 384), bf16), room((8, 112, 512), bf16), dma(1)], raw=(12,), out_raw=(2,), alias={12: 2}, after=(main1,),
    )
    terms, sent = scatter(ids, mine, away)
    (g0,) = call(
        bwd_last_kernel, "bwd_last", [(blk, f32)], (ids, *terms, own, gain, g1), 2, vm=range(1, 8), out_vm=(0,), limit=8
    )
    top_rows = gather_blocks(main1)
    shapes = [((2, BLK, 4096), f32), ((2, 512, D), f32), ((2, BLK, 3 * D), f32)]
    rooms = lambda n: [room(s[0][1:]) for s in shapes] + [room((4, 2, n, 512), bf16), dma(8), dma(3)]
    outs = call(assemble_top_kernel, "assemble_top", shapes, (ids, *top_rows), 5, rooms(352), raw=range(1, 9), out_raw=(0, 1, 2))
    low0, piece = over_groups(ids, "fsum_first", lax.all_to_all(payload, FS, 0, 0, tiled=True), (p1,), (g0, outs[2]))
    piece = transpose_owner(piece)
    swap = lambda x: shift(x, "xh", 1, 2)
    (last,) = call(
        xsum_last_kernel, "xsum_last", [((432, 512), bf16)], (ids, low0, swap(low0), piece, swap(piece)), 2,
    )
    last_blocks = gather_blocks(last)
    o_i, o_f, o_q, o_o, o_g, o_s, o_bf, o_bi = call(
        finish_kernel, "finish", shapes + [((2, BLK, D), f32)] + [((2, BLK), f32)] * 3 + [((2, 512), f32)],
        (ids, *last_blocks, *outs), 6, rooms(432)[:-1] + [pltpu.SemaphoreType.DMA((6, 1))], raw=range(1, 12), out_raw=(0, 1, 2),
        alias={9: 0, 10: 1, 11: 2},
    )
    return mixed[None], g0[None], o_g, o_s, o_q, o_o, o_i, o_bi, o_f, o_bf


def solution(mesh):
    fine = Mesh(mesh.devices.reshape(2, 4, 2, 4, 2), AXES)
    seq = ("xh", "y", "core")
    tok = P(FS, seq, None)
    two = P(None, FS)
    three = P(None, FS, None)
    in_specs = (tok, P(FS, None), two, two, three, three, three, two, three, two, tok)
    out_specs = (tok, tok, two, two, three, three, three, two, three, two)
    return jax.shard_map(body, mesh=fine, in_specs=in_specs, out_specs=out_specs, check_vma=False)
```

```python
import functools
import jax
import jax.numpy as jnp
from jax import lax
from jax.experimental import pallas as pl
from jax.experimental.pallas import tpu as pltpu
from jax.sharding import Mesh, PartitionSpec as P

ROT = 32
CONTS = 8
D = 1024
HALF = 1024
BLK = 128
QB = 256
AXES = ("xh", "y", "core", "z", "xl")
FS = ("z", "xl")
f32 = jnp.float32
bf16 = jnp.bfloat16
NT = (((1,), (1,)), ((), ()))
VM = pl.BlockSpec(memory_space=pltpu.VMEM)
SM = pl.BlockSpec(memory_space=pltpu.SMEM)
ANY = pl.BlockSpec(memory_space=pl.ANY)
HBM = pl.BlockSpec(memory_space=pltpu.HBM)
MB = 1024 * 1024


def sds(*args):
    return [jax.ShapeDtypeStruct(s, t) for s, t in args]


class Far:
    def __init__(self, ref, copy):
        self.ref, self.copy = ref, copy

    def here(self):
        if self.copy is not None:
            self.copy.wait()
            self.copy = None
        return self.ref

    def __getitem__(self, index):
        return self.here()[index]

    @property
    def shape(self):
        return self.ref.shape


class Out:
    def __init__(self, ref, copy):
        self.ref, self.copy, self.sent = ref, copy, False

    def __getitem__(self, index):
        return self.ref[index]

    def __setitem__(self, index, value):
        self.ref[index] = value

    @property
    def dtype(self):
        return self.ref.dtype

    @property
    def shape(self):
        return self.ref.shape

    def send(self):
        self.copy.start()
        self.sent = True


COST = 0.001
LIMIT = 51


def call(kernel, name, outs, args, us, scratch=(), limit=None, after=(), raw=(), vm=(), out_raw=(), out_vm=(), alias=None):
    n, m = len(args), len(outs)
    fetched = [i for i in range(1, n) if i not in raw and i not in vm]
    staged = [i for i in range(m) if i not in out_raw and i not in out_vm]

    def run(*refs):
        ins = list(refs[:n])
        results = list(refs[n + len(after) : n + len(after) + m])
        rest = list(refs[n + len(after) + m :])
        own, rest = rest[: len(scratch)], rest[len(scratch) :]
        sems = rest[-1]
        copies = []
        for k, i in enumerate(fetched):
            copy = pltpu.make_async_copy(ins[i], rest[k], sems.at[k])
            copies.append(copy)
            ins[i] = Far(rest[k], copy)
        for copy in copies:
            copy.start()
        for k, i in enumerate(staged):
            ref = rest[len(fetched) + k]
            results[i] = Out(ref, pltpu.make_async_copy(ref, results[i], sems.at[len(fetched) + k]))
        kernel(*ins, *results, *own)
        for i in fetched:
            ins[i].here()
        for i in staged:
            if not results[i].sent:
                results[i].send()
        for i in staged:
            results[i].copy.wait()

    room = [pltpu.VMEM(args[i].shape, args[i].dtype) for i in fetched]
    room += [pltpu.VMEM(outs[i][0], outs[i][1]) for i in staged]
    return pl.pallas_call(
        run,
        out_shape=sds(*outs),
        in_specs=[SM] + [VM if i in vm else HBM for i in range(1, n)] + [ANY] * len(after),
        out_specs=[VM if i in out_vm else HBM for i in range(m)],
        scratch_shapes=list(scratch) + room + [pltpu.SemaphoreType.DMA((max(1, len(room)),))],
        input_output_aliases=alias or {},
        compiler_params=pltpu.CompilerParams(vmem_limit_bytes=(limit or LIMIT) * MB),
        cost_estimate=pl.CostEstimate(flops=int(us * COST * 1e9), bytes_accessed=int(us * COST * 1e6), transcendentals=0),
        name=name,
    )(*args, *after)


def dma(n):
    return pltpu.SemaphoreType.DMA((n,))


def copy_all(pairs, sems):
    copies = [pltpu.make_async_copy(a, b, sems.at[i]) for i, (a, b) in enumerate(pairs)]
    for copy in copies:
        copy.start()
    return copies


def wait_all(copies):
    for copy in copies:
        copy.wait()


def shift(x, axis, by, size):
    return lax.ppermute(x, axis, [(i, (i + by) % size) for i in range(size)])


def gather_blocks(own, hold=None):
    one = shift(own, "y", -1, 4)
    three = shift(own, "y", 1, 4)
    two = shift(own, "y", 2, 4)
    if hold is not None:
        one, two, three = hold(one, two, three)
    blocks = []
    for mine in (own, one, two, three):
        blocks += [mine, shift(mine, "core", 1, 2)]
    return blocks


def spread(low):
    return [shift(low[r - 1], "y", r, 4) for r in (1, 2, 3)]


def transpose_owner(x):
    pairs = [(j * 8 + f, f * 8 + j) for j in range(8) for f in range(8)]
    return lax.ppermute(x, ("y", "core", "z", "xl"), pairs)


def gate(ids, x, after):
    (out,) = call(lambda *refs: None, "gate", [(x.shape, x.dtype)], (ids, x), 1, raw=(1,), out_raw=(0,), after=after, alias={1: 0})
    return out


def gate_all(ids, xs, after):
    n = len(xs)
    return call(
        lambda *refs: None, "gate", [(x.shape, x.dtype) for x in xs], (ids, *xs), 1, raw=range(1, n + 1), out_raw=range(n),
        after=after, alias={i + 1: i for i in range(n)},
    )


def gather_fsdp(ids, x, got, after=()):
    (pair,) = call(
        pair_kernel, "pair", [((2,) + x.shape, bf16)], (ids, x, got), 2, [dma(2)], out_raw=(0,), after=after, limit=62,
    )
    return [pair, shift(pair, "z", -1, 4), shift(pair, "z", 2, 4), shift(pair, "z", 1, 4)]


def weight_copies(ids, pairs, cols, room):
    if len(pairs) == 1:
        return [(pairs[0].at[:, :, cols], room)]
    out = []
    for r in range(4):
        out.append((pairs[r].at[:, :, cols], room.at[pl.ds(2 * lax.rem(ids[4] + r, 4), 2)]))
    return out


def slot(ids, r, s):
    y = lax.rem(ids[0] + r, 4)
    c = ids[1] if s == 0 else 1 - ids[1]
    return y * 2 + c


def rows_of(ids, r, s, n=BLK):
    return pl.ds(pl.multiple_of(slot(ids, r, s) * n, n), n)


def turn(v, cosine, sine):
    lane = lax.broadcasted_iota(jnp.int32, v.shape, 1)
    partner = jnp.where(lane % 2 == 0, pltpu.roll(v, BLK - 1, 1), pltpu.roll(v, 1, 1))
    return v * cosine + partner * sine


def stats(x):
    average = jnp.mean(x, axis=-1, keepdims=True)
    centred = x - average
    variance = jnp.mean(centred * centred, axis=-1, keepdims=True)
    inv = lax.rsqrt(variance + 1e-05)
    return centred * inv, inv


def gelu_both(x):
    a = 0.7978845608028654
    b = 0.044715
    sq = x * x
    t = jnp.tanh(a * x * (1.0 + b * sq))
    half = 0.5 * (1.0 + t)
    slope = half + 0.5 * x * (1.0 - t * t) * a * (1.0 + 3.0 * b * sq)
    return x * half, slope


def dot(a, b):
    return jnp.dot(a, b, preferred_element_type=f32)


def dot_nt(a, b):
    return lax.dot_general(a, b, NT, preferred_element_type=f32)


def pack_q_kernel(ids, wq, gain, bias, bfc, bin_, q0, room, small, binv, sems, out_sems):
    j = ids[0] * 2 + ids[1]
    pairs = []
    for part in range(3):
        cols = pl.ds(pl.multiple_of(part * D + j * BLK, BLK), BLK)
        pairs.append((wq.at[0, :, cols], room.at[0:BLK, part * BLK : part * BLK + BLK]))
    pairs += [(ref, small.at[i]) for i, ref in enumerate((gain, bias, bfc))]
    pairs.append((bin_, binv))
    wait_all(copy_all(pairs, sems))
    chunk = binv[:, pl.ds(pl.multiple_of((j // 2) * BLK, BLK), BLK)].astype(f32)
    chunk = jnp.where(j % 2 == 1, pltpu.roll(chunk, 64, 1), chunk)
    lane = lax.broadcasted_iota(jnp.int32, (1, BLK), 1)
    row2 = jnp.where(lane < 64, chunk[0:1], pltpu.roll(chunk, 64, 1)[1:2])
    blank = jnp.zeros((13, BLK), f32)
    cols = [jnp.concatenate([small[i].astype(f32), row2, blank], 0) for i in range(3)]
    room[BLK:, :] = jnp.concatenate(cols, 1).astype(bf16)
    wait_all(copy_all([(room, q0.at[f]) for f in range(8)], out_sems))


def pack_layer(layer, ids, wi, wf, out, chunks, sems, more=()):
    j = ids[0] * 2 + ids[1]
    rows = pl.ds(pl.multiple_of(j * 64, 64), 64)
    pairs = []
    for f in range(8):
        cols = pl.ds(pl.multiple_of(f * 512 + (j // 2) * BLK, BLK), BLK)
        pairs.append((wi.at[layer, :, cols], chunks.at[f]))
    pairs.append((wf.at[layer, rows, 0:512], out.ref.at[0:64, 512:1024]))
    pairs.append((wf.at[layer, rows, 512:1024], out.ref.at[64:128, 512:1024]))
    wait_all(copy_all(pairs + list(more), sems))
    lane = lax.broadcasted_iota(jnp.int32, (BLK, BLK), 1)
    odd = j % 2 == 1
    for pair in range(4):
        a = chunks[2 * pair].astype(f32)
        b = chunks[2 * pair + 1].astype(f32)
        first = jnp.where(odd, pltpu.roll(a, 64, 1), a)
        second = jnp.where(odd, b, pltpu.roll(b, 64, 1))
        out[:, pair * BLK : pair * BLK + BLK] = jnp.where(lane < 64, first, second).astype(bf16)


def pack_first_kernel(ids, wi, wf, out, chunks, sems):
    pack_layer(0, ids, wi, wf, out, chunks, sems)


def pack_second_kernel(ids, wi, wf, wq, out, chunks, sems):
    j = ids[0] * 2 + ids[1]
    more = []
    for part in range(3):
        cols = pl.ds(pl.multiple_of(part * D + j * BLK, BLK), BLK)
        more.append((wq.at[1, :, cols], out.ref.at[:, D + part * BLK : D + part * BLK + BLK]))
    pack_layer(1, ids, wi, wf, out, chunks, sems, more)


def pass_kernel(layer, ids, x, out, sems):
    wait_all(copy_all([(x.at[layer], out.ref)], sems))


def join_kernel(ids, a, b, out, sems):
    wait_all(copy_all([(a, out.ref.at[0:BLK]), (b, out.ref.at[BLK : 2 * BLK])], sems))


def pair_kernel(ids, own, got, out, sems):
    xl = ids[3]
    wait_all(copy_all([(own.here(), out.at[xl]), (got.here(), out.at[1 - xl])], sems))


def four_kernel(ids, own, got, out, sems):
    xl = ids[3]
    mine, other = own.here(), got.here()
    wait_all(copy_all([(src, out.at[z, at]) for z in range(4) for src, at in ((mine, xl), (other, 1 - xl))], sems))


def params_part(rows_of_f, gain, bias, bfc, bi):
    lane = lax.broadcasted_iota(jnp.int32, (1, BLK), 1)
    for f in range(8):
        cols = slice(f * BLK, f * BLK + BLK)
        rows = rows_of_f[f].astype(f32)
        gain[:, cols] = rows[0:2, 0:BLK]
        bias[:, cols] = rows[0:2, BLK : 2 * BLK]
        bfc[:, cols] = rows[0:2, 2 * BLK :]
    for pair in range(4):
        a = rows_of_f[2 * pair].astype(f32)[2:3, :BLK]
        b = rows_of_f[2 * pair + 1].astype(f32)[2:3, :BLK]
        cols = slice(pair * BLK, pair * BLK + BLK)
        bi[0:1, cols] = jnp.where(lane < 64, a, pltpu.roll(b, 64, 1))
        bi[1:2, cols] = jnp.where(lane < 64, pltpu.roll(a, 64, 1), b)


def qkv_part(normed, w, cosine, sine, q, kv):
    for i in range(HALF // QB):
        rows = slice(i * QB, i * QB + QB)
        out = dot(normed[rows, :], w).astype(bf16).astype(f32)
        cb = cosine[rows, :]
        sb = sine[rows, :]
        kv[rows, :BLK] = turn(out[:, BLK : 2 * BLK], cb, sb).astype(bf16)
        kv[rows, BLK:] = out[:, 2 * BLK :].astype(bf16)
        q[rows, :] = (turn(out[:, :BLK], cb, sb).astype(bf16).astype(f32) * 0.125).astype(bf16)


def take_blocks(ids, blocks, room, sems, at=0):
    part = slice(at, at + BLK)
    return copy_all([(blocks[2 * r + s].at[part], room.at[rows_of(ids, r, s)]) for r in range(4) for s in range(2)], sems)


def qkv_first_kernel(ids, *refs):
    blocks, (wq, cosine, sine), refs = refs[:8], refs[8:11], refs[11:]
    normed, xhat, q, kv, gain, bias, bfc, bi, raw, sems = refs
    copies = take_blocks(ids, blocks, raw, sems)
    w = wq.here()
    params_part([w[f, BLK:, :] for f in range(8)], gain, bias, bfc, bi)
    wait_all(copies)
    for i in range(HALF // QB):
        rows = slice(i * QB, i * QB + QB)
        x, _ = stats(raw[rows, :].astype(f32))
        xhat[rows, :] = x.astype(bf16)
        normed[rows, :] = (x * gain[0:1, :] + bias[0:1, :]).astype(bf16)
    xhat.send()
    normed.send()
    qkv_part(normed, w[:, :BLK, :].reshape(D, 384), cosine, sine, q, kv)


def qkv_kernel(ids, *refs):
    blocks, w, (cosine, sine), (normed, q, kv, wq, sems, wsem) = refs[:8], refs[8:9], refs[9:11], refs[11:]
    copies = copy_all(weight_copies(ids, w, slice(1024, 1408), wq), wsem)
    copies += take_blocks(ids, blocks, normed.ref, sems)
    wait_all(copies)
    normed.send()
    qkv_part(normed, wq[...].reshape(D, 384), cosine, sine, q, kv)


def ff_kernel(layer, ids, far, bi, *refs):
    w, (active, slope, feed, wi, wf, va, vs, vf, wsems, sems, normed) = refs[:-11], refs[-11:]
    copies = copy_all(weight_copies(ids, w, slice(0, 512), wi), wsems.at[0])
    rows = slice(0, QB)
    copies += copy_all([(far.at[rows], normed.at[rows])], wsems.at[2])
    late = copy_all(weight_copies(ids, w, slice(512, 1024), wf), wsems.at[1])
    rows = slice(QB, HALF)
    rest = copy_all([(far.at[rows], normed.at[rows])], wsems.at[3])
    wait_all(copies)
    left = right = None
    sent = []
    for i in range(HALF // QB):
        rows = slice(i * QB, i * QB + QB)
        if i == 1:
            wait_all(rest)
        pre = dot(normed[rows, :], wi[...].reshape(D, 512)) + bi[layer : layer + 1, :]
        act, der = gelu_both(pre)
        act = act.astype(bf16)
        va[rows, :] = act
        vs[rows, :] = der.astype(bf16)
        if i == 0:
            wait_all(late)
            left, right = wf[:, 0:64, :].reshape(512, 512), wf[:, 64:128, :].reshape(512, 512)
        vf[rows, :512] = dot(act, left).astype(bf16)
        vf[rows, 512:] = dot(act, right).astype(bf16)
        pairs = [(v.at[rows], out.at[rows]) for v, out in ((va, active), (vs, slope), (vf, feed))]
        sent += copy_all(pairs, sems.at[i])
    wait_all(sent)


def ff(ids, layer, normed, w, bi, after=()):
    room = lambda *shape: pltpu.VMEM(shape, bf16)
    return call(
        functools.partial(ff_kernel, layer), "ff", [((HALF, 512), bf16), ((HALF, 512), bf16), ((HALF, D), bf16)],
        (ids, normed, bi, *w), 5,
        [room(8, BLK, 512), room(8, BLK, 512), room(HALF, 512), room(HALF, 512), room(HALF, D),
         pltpu.SemaphoreType.DMA((4, 4)), pltpu.SemaphoreType.DMA((4, 3)), room(HALF, D)],
        raw=[1, *range(3, 3 + len(w))], out_raw=(0, 1, 2), limit=62 - 11 * layer, after=after,
    )


def head_cut(x):
    lane = lax.broadcasted_iota(jnp.int32, x.shape, 1)
    zero = jnp.zeros((), x.dtype)
    return [jnp.where(lane < 64, x, zero), jnp.where(lane >= 64, x, zero)]


def seen(i, kk, qseg, kseg, QB):
    q0 = i * QB
    qs = qseg[0:1, q0 : q0 + QB]
    ks = kseg[0:kk, 0:1]
    key = lax.broadcasted_iota(jnp.int32, (kk, QB), 0)
    query = q0 + lax.broadcasted_iota(jnp.int32, (kk, QB), 1)
    return (key <= query) & ((ks == 0) | (ks == qs))


def flip(x):
    return jnp.transpose(x.astype(f32)).astype(bf16)


def attn_own_kernel(ids, q, kv, qseg, acc, m_out, l_out):
    qseg = qseg[...]
    kseg = jnp.transpose(qseg)
    km = head_cut(kv[:, :BLK])
    vt = flip(kv[:, BLK:])
    for i in range(HALF // 512):
        cols = slice(i * 512, (i + 1) * 512)
        kk = (i + 1) * 512
        allowed = seen(i, kk, qseg, kseg, 512)
        for h in range(2):
            rows = slice(h * 64, h * 64 + 64)
            s = jnp.where(allowed, dot_nt(km[h][:kk], q[cols, :]), -1e30)
            m = jnp.max(s, axis=0, keepdims=True)
            p = jnp.exp(s - m)
            l_out[h : h + 1, cols] = jnp.sum(p, axis=0, keepdims=True)
            m_out[h : h + 1, cols] = m
            acc[rows, cols] = dot(vt[rows, :kk], p.astype(bf16))


def split_rows(ids, mine, away, block):
    for r in range(4):
        away[r] = block(rows_of(ids, r, 1)).astype(bf16)
    away.send()
    for r in range(4):
        mine[r] = block(rows_of(ids, r, 0)).astype(bf16)


def attn_full_kernel(ids, q, kv0, acc, m_in, l_in, feed, wo, attn, lse, mine, away, tmp):
    upper = ids[2] == 1
    for ref in (q, kv0, acc, m_in, l_in):
        ref.here()

    @pl.when(upper)
    def _():
        km = head_cut(kv0[:, :BLK])
        vt = flip(kv0[:, BLK:])
        for i in range(HALF // 512):
            cols = slice(i * 512, (i + 1) * 512)
            for h in range(2):
                rows = slice(h * 64, h * 64 + 64)
                s = dot_nt(km[h], q[cols, :])
                m0 = m_in[h : h + 1, cols]
                m = jnp.maximum(m0, jnp.max(s, axis=0, keepdims=True))
                p = jnp.exp(s - m)
                a = jnp.exp(m0 - m)
                l = l_in[h : h + 1, cols] * a + jnp.sum(p, axis=0, keepdims=True)
                o = dot(vt[rows, :], p.astype(bf16))
                tmp[rows, cols] = (acc[rows, cols] * a + o) / l
                lse[h : h + 1, cols] = m + jnp.log(l)

    @pl.when(jnp.logical_not(upper))
    def _():
        for h in range(2):
            rows = slice(h * 64, h * 64 + 64)
            l = l_in[h : h + 1, :]
            tmp[rows, :] = acc[rows, :] / l
            lse[h : h + 1, :] = m_in[h : h + 1, :] + jnp.log(l)

    attn[...] = jnp.transpose(tmp[...]).astype(bf16)
    attn.send()
    lse.send()
    split_rows(ids, mine, away, lambda rows: feed[rows, :].astype(f32) + dot(attn[rows, :], wo[...]))


def mid_kernel(ids, mine, got, total, one, two, three):
    for r, out in ((1, one), (2, two), (3, three)):
        out[...] = (mine[r].astype(f32) + got[r].astype(f32)).astype(bf16)
    total[...] = mine[0].astype(f32) + got[0].astype(f32)


def summed(total, one, two, three):
    return total[...] + one[...].astype(f32) + two[...].astype(f32) + three[...].astype(f32)


def fwd_end_kernel(ids, total, one, two, three, x, gain, bias, bfc, x_new, normed):
    new = x[...].astype(f32) + summed(total, one, two, three) + bfc[0:1, :]
    x_new[...] = new
    xhat, _ = stats(new)
    normed[...] = (xhat * gain[1:2, :] + bias[1:2, :]).astype(bf16)


def last_end_kernel(ids, total, one, two, three, x, bfc, out):
    out[...] = (x[...] + summed(total, one, two, three) + bfc[1:2, :]).astype(bf16)


def grad_in_kernel(at, ids, *refs):
    blocks, (wo, gr, dattn, sems) = refs[:8], refs[8:]
    wait_all(take_blocks(ids, blocks, gr.ref, sems, at))
    gr.send()
    dattn[...] = dot_nt(gr[...], wo[...]).astype(bf16)


def row_delta(attn, do):
    prod = attn[...].astype(f32) * do[...].astype(f32)
    head = lax.broadcasted_iota(jnp.int32, (8, BLK), 0)
    lane = lax.broadcasted_iota(jnp.int32, (8, BLK), 1) // 64
    pickers = jnp.where(head == lane, 1.0, 0.0).astype(f32)
    return lax.dot_general(pickers, prod, NT, precision=lax.Precision.HIGHEST, preferred_element_type=f32)


def grad_block(km, vm, kt, qm, dom, q_blk, do_blk, lse, delta, allowed):
    p = jnp.exp(dot_nt(km, q_blk) - lse)
    if allowed is not None:
        p = jnp.where(allowed, p, 0.0)
    dp = dot_nt(vm, do_blk)
    ds = (p * (dp - delta)).astype(bf16)
    return dot(kt, ds), dot(ds, qm), dot(p.astype(bf16), dom)


def grad_full_kernel(ids, q, kv0, do, attn, lse, dqt, dkv, acck, accv):
    upper = ids[2] == 1
    for ref in (q, kv0, do, attn, lse):
        ref.here()

    @pl.when(upper)
    def _():
        delta = row_delta(attn, do)
        qm, km, vm, dom = [head_cut(x) for x in (q[...], kv0[:, :BLK], kv0[:, BLK:], do[...])]
        kt = flip(kv0[:, :BLK])
        for i in range(HALF // 512):
            cols = slice(i * 512, (i + 1) * 512)
            for h in range(2):
                rows = slice(h * 64, h * 64 + 64)
                dq, dk, dv = grad_block(
                    km[h], vm[h], kt[rows, :], qm[h][cols], dom[h][cols], q[cols, :], do[cols, :],
                    lse[h : h + 1, cols], delta[h : h + 1, cols], None,
                )
                dqt[rows, cols] = dq
                if i == 0 and h == 0:
                    acck[...] = dk
                    accv[...] = dv
                else:
                    acck[...] += dk
                    accv[...] += dv
        dkv[:, :BLK] = acck[...].astype(bf16)
        dkv[:, BLK:] = accv[...].astype(bf16)

    @pl.when(jnp.logical_not(upper))
    def _():
        dqt[...] = jnp.zeros(dqt.shape, f32)
        dkv[...] = jnp.zeros(dkv.shape, bf16)


def grad_own_kernel(ids, q, kv, do, attn, lse, qseg, dqt0, out, tmp, dk_out, dv_out):
    qseg = qseg[...]
    kseg = jnp.transpose(qseg)
    delta = row_delta(attn, do)
    qm, km, vm, dom = [head_cut(x) for x in (q[...], kv[:, :BLK], kv[:, BLK:], do[...])]
    kt = flip(kv[:, :BLK])
    dk_out[...] = jnp.zeros(dk_out.shape, f32)
    dv_out[...] = jnp.zeros(dv_out.shape, f32)
    for i in range(HALF // 256):
        cols = slice(i * 256, (i + 1) * 256)
        kk = (i + 1) * 256
        allowed = seen(i, kk, qseg, kseg, 256)
        for h in range(2):
            rows = slice(h * 64, h * 64 + 64)
            dq, dk, dv = grad_block(
                km[h][:kk], vm[h][:kk], kt[rows, :kk], qm[h][cols], dom[h][cols], q[cols, :], do[cols, :],
                lse[h : h + 1, cols], delta[h : h + 1, cols], allowed,
            )
            tmp[rows, cols] = (dq + dqt0[rows, cols]) * 0.125
            dk_out[:kk, :] += dk
            dv_out[:kk, :] += dv
    out[:, :BLK] = jnp.transpose(tmp[...]).astype(bf16)
    out[:, BLK : 2 * BLK] = dk_out[...].astype(bf16)
    out[:, 2 * BLK :] = dv_out[...].astype(bf16)


def ff_back_outer_kernel(ids, *refs):
    far, w, refs = refs[:5], refs[5:-14], refs[-14:]
    part, dbi, out, wi, wf, vd, v, wsems, sems, gr, slope, active, attn, normed = refs
    rooms = (gr, slope, active, attn, normed)
    copies = copy_all(weight_copies(ids, w, slice(512, 1024), wf), wsems.at[0])
    rows = slice(0, 256)
    first = [(far[0].at[rows], gr.at[rows]), (far[1].at[rows], slope.at[rows])]
    copies += copy_all(first, wsems.at[2])
    late = copy_all(weight_copies(ids, w, slice(0, 512), wi), wsems.at[1])
    rows = slice(256, HALF)
    rest = copy_all([(far[0].at[rows], gr.at[rows]), (far[1].at[rows], slope.at[rows])], wsems.at[3])
    after = copy_all([(far[k], rooms[k]) for k in (2, 3, 4)], wsems.at[4])
    wait_all(copies)
    left, right = wf[:, 0:64, :].reshape(512, 512), wf[:, 64:128, :].reshape(512, 512)
    total = jnp.zeros((1, 512), f32)
    for i in range(HALF // 256):
        if i == 1:
            wait_all(rest)
        rows = slice(i * 256, i * 256 + 256)
        d = (dot_nt(gr[rows, :512], left) + dot_nt(gr[rows, 512:], right)) * slope[rows, :].astype(f32)
        total = total + jnp.sum(d, axis=0, keepdims=True)
        d = d.astype(bf16)
        vd[rows, :] = d
        if i == 0:
            wait_all(late)
        part[rows, :] = dot_nt(d, wi[...].reshape(D, 512)).astype(bf16)
    part.send()
    dbi[...] = jnp.concatenate([total, jnp.zeros((7, 512), f32)], 0)
    wait_all(after)
    wait_all(outer_rows(out, v, sems, active, gr, attn, normed, vd))


def ff_back_outer(ids, rows, gr, slope, active, attn, normed, w, after):
    room = lambda *shape: pltpu.VMEM(shape, bf16)
    return call(
        ff_back_outer_kernel, "ff_back_outer", [((HALF, D), bf16), ((8, 512), f32), ((8, rows, 512), bf16)],
        (ids, gr, slope, active, attn, normed, *w), 9,
        [room(8, BLK, 512), room(8, BLK, 512), room(HALF, 512), room(8, 288, 512), pltpu.SemaphoreType.DMA((5, 4)),
         pltpu.SemaphoreType.DMA((3, 2)), room(HALF, D), room(HALF, 512), room(HALF, 512), room(HALF, BLK), room(HALF, D)],
        raw=range(1, 6 + len(w)), out_raw=(2,), after=after,
    )


def combine_rows(ids, own, back, cosine, sine, dqkv):
    cb = cosine[...]
    sb = -sine[...]
    dqkv[:, :BLK] = turn(own[:, :BLK].astype(f32), cb, sb).astype(bf16)
    dk = own[:, BLK : 2 * BLK].astype(f32) + back[:, :BLK].astype(f32)
    dqkv[:, BLK : 2 * BLK] = turn(dk, cb, sb).astype(bf16)
    dqkv[:, 2 * BLK :] = (own[:, 2 * BLK :].astype(f32) + back[:, BLK:].astype(f32)).astype(bf16)


def combine_kernel(ids, own, back, cosine, sine, part, w1, far, _, mine, away, payload, dqkv, out, wq, wsem, normed, nsem):
    copies = copy_all(weight_copies(ids, (w1,), slice(1024, 1408), wq), wsem)
    late = copy_all([(far, normed)], nsem)
    combine_rows(ids, own, back, cosine, sine, dqkv)
    wait_all(copies)
    w = wq[...].reshape(D, 384)
    split_rows(ids, mine, away, lambda rows: part[rows, :].astype(f32) + dot_nt(dqkv[rows, :], w))
    mine.send()
    wait_all(late)
    g_q = outer(normed[...], dqkv[...])
    for f in range(8):
        pack_rows(out, f, g_q)
    wait_all(copy_all([(out, payload.at[:, 288:384])], wsem))


def combine_first_kernel(ids, own, back, cosine, sine, wq0, part, xhat, normed, sums1, dbi0, dbi1, *refs):
    _, mine, away, payload, dqkv, out, sems = refs
    combine_rows(ids, own, back, cosine, sine, dqkv)
    w = wq0[:, :BLK, :].reshape(D, 384)
    gain = jnp.zeros((1, D), f32)
    base = jnp.zeros((1, D), f32)
    for s, to in ((1, away), (0, mine)):
        for r in range(4):
            rows = rows_of(ids, r, s)
            block = part[rows, :].astype(f32) + dot_nt(dqkv[rows, :], w)
            to[r] = block.astype(bf16)
            gain = gain + jnp.sum(block * xhat[rows, :].astype(f32), axis=0, keepdims=True)
            base = base + jnp.sum(block, axis=0, keepdims=True)
        to.send()
    g_q = outer(normed[...], dqkv[...])
    lane = lax.broadcasted_iota(jnp.int32, (1, BLK), 1)
    blank = jnp.zeros((13, 384), f32)
    none = jnp.zeros((1, 256), f32)
    for f in range(8):
        pack_rows(out, f, g_q)
        cols = slice(f * BLK, f * BLK + BLK)
        row0 = jnp.concatenate([gain[:, cols], base[:, cols], sums1[3:4, cols]], 1)
        row1 = jnp.concatenate([sums1[0:1, cols], sums1[1:2, cols], sums1[2:3, cols]], 1)
        half = slice((f // 2) * BLK, (f // 2) * BLK + BLK)
        a = dbi0[0:1, half]
        b = dbi1[0:1, half]
        if f % 2 == 0:
            b = pltpu.roll(b, 64, 1)
        else:
            a = pltpu.roll(a, 64, 1)
        row2 = jnp.concatenate([jnp.where(lane < 64, a, b), none], 1)
        out[f, 96:112, :384] = jnp.concatenate([row0, row1, row2, blank], 0).astype(bf16)
        out[f, 96:112, 384:] = jnp.zeros((16, 128), bf16)
    wait_all(copy_all([(out, payload.at[:, 288:400])], sems))


def norm_back(dn, x, gain_row, g):
    xhat, inv = stats(x[...].astype(f32))
    dx = dn * gain_row
    dx = inv * (dx - jnp.mean(dx, -1, keepdims=True) - xhat * jnp.mean(dx * xhat, -1, keepdims=True))
    return xhat, g[...].astype(f32) + dx


def bwd_end_kernel(ids, total, one, two, three, x, gain, g, g_new, gr, sums):
    dn = summed(total, one, two, three)
    xhat, new = norm_back(dn, x, gain[1:2, :], g)
    g_new[...] = new
    gr[...] = new.astype(bf16)
    col = lambda v: jnp.sum(v, axis=0, keepdims=True)
    top = col(g[...].astype(f32))
    sums[...] = jnp.concatenate([col(dn * xhat), col(dn), top, col(new), jnp.zeros((4, D), f32)], 0)


def bwd_last_kernel(ids, total, one, two, three, x, gain, g, g_new):
    _, new = norm_back(summed(total, one, two, three), x, gain[0:1, :], g)
    g_new[...] = new


def outer(a, b):
    return lax.dot_general(a, b, (((0,), (0,)), ((), ())), preferred_element_type=f32).astype(bf16)


def pack_rows(out, f, g_q):
    for part in range(3):
        for group in range(4):
            piece = g_q[f * 128 + group * 32 : f * 128 + group * 32 + 32, part * BLK : part * BLK + BLK]
            out[f, part * 32 : part * 32 + 32, group * BLK : group * BLK + BLK] = piece


def outer_rows(out, v, sems, active, gr, attn, normed, dpre):
    for half in range(2):
        cols = slice(half * 512, half * 512 + 512)
        g_f = outer(active[...], gr[:, cols])
        g_o = outer(attn[...], gr[:, cols])
        for f in range(8):
            v[f, 128 + 64 * half : 192 + 64 * half, :] = g_f[f * 64 : f * 64 + 64]
            v[f, 256 + 16 * half : 272 + 16 * half, :] = g_o[f * 16 : f * 16 + 16]
    first = copy_all([(v.at[:, 128:288], out.at[:, 128:288])], sems.at[0])
    for half in range(2):
        cols = slice(half * 512, half * 512 + 512)
        g_i = outer(normed[:, cols], dpre[...])
        for k in range(4):
            v[4 * half + k, 0:128, :] = g_i[k * 128 : k * 128 + 128]
        group = slice(4 * half, 4 * half + 4)
        first += copy_all([(v.at[group, 0:128], out.at[group, 0:128])], sems.at[1 + half])
    return first


def fsum_kernel(ids, got, *refs):
    more, (low, piece, room, sems) = refs[:-4], refs[-4:]
    rows = got.shape[1]
    half = rows // 32 * 16
    parts = (slice(0, half), slice(half, rows))
    copies = copy_all([(got.at[:, part], room.at[:, part]) for part in parts], sems)
    for at in range(0, rows, 16):
        if at in (0, half):
            copies[0 if at == 0 else 1].wait()
        part = slice(at, at + 16)
        total = room[0, part, :].astype(f32)
        for f in range(1, 8):
            total = total + room[f, part, :].astype(f32)
        total = total.astype(bf16)
        if 256 <= at < 288:
            piece[at - 256 : at - 240, :] = total
        else:
            to = at if at < 256 else at - 32
            low[to : to + 16, :] = total
    for ref in more:
        piece[32:64, :] = ref[...]


def add_rows(terms, start, stop):
    total = terms[0][start:stop, :].astype(f32)
    for term in terms[1:]:
        total = total + term[start:stop, :].astype(f32)
    return total.astype(bf16)


def xsum_top_kernel(ids, low, got, main):
    main[...] = add_rows((low, got), 0, 352)


def xsum_last_kernel(ids, low, got, piece, piece_got, main):
    terms = (low, got)
    main[0:112, :] = add_rows(terms, 256, 368)
    main[112:368, :] = add_rows(terms, 0, 256)
    main[368:432, :] = add_rows((piece, piece_got), 0, 64)


def over_groups(ids, name, got, more=(), after=()):
    rows = got.shape[1]
    return call(
        fsum_kernel, name, [((rows - 32, 512), bf16), ((32 + 32 * len(more), 512), bf16)], (ids, got, *more), 3,
        [pltpu.VMEM(got.shape, bf16), dma(2)], raw=(1,), after=after,
    )


def place_in(zero, one, at, y, o_i, o_f):
    lane = lax.broadcasted_iota(jnp.int32, (BLK, BLK), 1)
    start = pl.multiple_of(y * BLK, BLK)
    for half in range(2):
        rows = slice(at + 128 + 64 * half, at + 192 + 64 * half)
        cols = slice(half * 512, half * 512 + 512)
        o_f[pl.ds(start, 64), cols] = zero[rows, :].astype(f32)
        o_f[pl.ds(start + 64, 64), cols] = one[rows, :].astype(f32)
    for pair in range(4):
        cols = slice(pair * BLK, pair * BLK + BLK)
        a, b = zero[at : at + BLK, cols].astype(f32), one[at : at + BLK, cols].astype(f32)
        even = pl.ds(pl.multiple_of(2 * pair * 512 + start, BLK), BLK)
        odd = pl.ds(pl.multiple_of((2 * pair + 1) * 512 + start, BLK), BLK)
        o_i[:, even] = jnp.where(lane < 64, a, pltpu.roll(b, 64, 1))
        o_i[:, odd] = jnp.where(lane < 64, pltpu.roll(a, 64, 1), b)


def place_q(zero, one, at, y, o_q):
    for part in range(3):
        rows = slice(at + part * 32, at + part * 32 + 32)
        start = pl.multiple_of(part * D + 2 * y * BLK, BLK)
        for group in range(4):
            cols = slice(group * BLK, group * BLK + BLK)
            to = slice(group * 32, group * 32 + 32)
            o_q[to, pl.ds(start, BLK)] = zero[rows, cols].astype(f32)
            o_q[to, pl.ds(start + BLK, BLK)] = one[rows, cols].astype(f32)


def fetch_rows(ids, blocks, room, sems):
    pairs = []
    for r in range(4):
        pairs += [(blocks[2 * r], room.at[r, ids[1]]), (blocks[2 * r + 1], room.at[r, 1 - ids[1]])]
    return copy_all(pairs, sems)


def assemble_top_kernel(ids, *refs):
    blocks, (o_i, o_f, o_q, vi, vf, vq, room, sems, out_sems) = refs[:8], refs[8:]
    copies = fetch_rows(ids, blocks, room, sems)
    for r in range(4):
        wait_all(copies[2 * r : 2 * r + 2])
        y = lax.rem(ids[0] + r, 4)
        place_in(room.at[r, 0], room.at[r, 1], 0, y, vi, vf)
        place_q(room.at[r, 0], room.at[r, 1], 256, y, vq)
    wait_all(copy_all([(vi, o_i.at[1]), (vf, o_f.at[1]), (vq, o_q.at[1])], out_sems))


def finish_kernel(ids, *refs):
    blocks, refs = refs[:8], refs[11:]
    o_i, o_f, o_q, o_o, o_g, o_s, o_bf, o_bi, vi, vf, vq, room, sems, out_sems = refs
    copies = fetch_rows(ids, blocks, room, sems)
    outs = []
    total = jnp.zeros((16, 384), f32)
    lane = lax.broadcasted_iota(jnp.int32, (1, BLK), 1)
    for r in range(4):
        wait_all(copies[2 * r : 2 * r + 2])
        y = lax.rem(ids[0] + r, 4)
        place_in(room.at[r, 0], room.at[r, 1], 112, y, vi, vf)
        rows = pl.ds(pl.multiple_of(y * BLK, BLK), BLK)
        outs += copy_all([(vf.at[rows], o_f.at[0, rows])], out_sems.at[r])
    outs += copy_all([(vi, o_i.at[0])], out_sems.at[4])
    for r in range(4):
        place_q(room.at[r, 0], room.at[r, 1], 0, lax.rem(ids[0] + r, 4), vq)
    outs += copy_all([(vq, o_q.at[0])], out_sems.at[5])
    for r in range(4):
        y = lax.rem(ids[0] + r, 4)
        for layer in range(2):
            for half in range(2):
                at = 368 + 32 * layer + 16 * half
                cols = slice(half * 512, half * 512 + 512)
                start = pl.multiple_of(y * 32, 32)
                o_o[layer, pl.ds(start, 16), cols] = room[r, 0, at : at + 16, :].astype(f32)
                o_o[layer, pl.ds(start + 16, 16), cols] = room[r, 1, at : at + 16, :].astype(f32)
        zero, one = room[r, 0, 96:112, :384].astype(f32), room[r, 1, 96:112, :384].astype(f32)
        total = total + zero + one
        a, b = zero[2:3, :BLK], one[2:3, :BLK]
        cols = pl.ds(pl.multiple_of(y * BLK, BLK), BLK)
        o_bi[0:1, cols] = jnp.where(lane < 64, a, pltpu.roll(b, 64, 1))
        o_bi[1:2, cols] = jnp.where(lane < 64, pltpu.roll(a, 64, 1), b)
    o_g[...] = total[0:2, :BLK]
    o_s[...] = total[0:2, BLK : 2 * BLK]
    o_bf[...] = total[0:2, 2 * BLK :]
    for ref in (o_o, o_g, o_s, o_bf, o_bi):
        ref.send()
    wait_all(outs)


def positions_of(group_seg):
    token_index = jnp.arange(group_seg.shape[0], dtype=jnp.int32)
    labels = jnp.arange(CONTS + 1, dtype=jnp.int32)
    member = (group_seg[:, None] == labels[None, :]).astype(jnp.int32)
    counts = jnp.sum(member, axis=0)
    starts = jnp.cumsum(counts) - counts
    own_start = jnp.sum(member * starts[None, :], axis=1)
    return token_index - own_start + jnp.where(group_seg > 0, counts[0], 0)


def rope_tables(positions):
    lane = jnp.arange(BLK, dtype=jnp.int32) % 64
    inverse = 10000.0 ** (-2.0 * (lane // 2).astype(f32) / ROT)
    phase = positions.astype(f32)[:, None] * jnp.where(lane < ROT, inverse, 0.0)[None, :]
    sign = jnp.where(lane % 2 == 0, -1.0, 1.0)
    return jnp.cos(phase), jnp.sin(phase) * sign[None, :]


def scatter(ids, mine, away):
    got = shift(away, "core", 1, 2)
    blk = (BLK, D)
    total, one, two, three = call(
        mid_kernel, "rs_mid", [(blk, f32)] + [(blk, bf16)] * 3, (ids, mine, got), 2, vm=(2,), out_vm=(0, 1, 2, 3), limit=8
    )
    return [total] + spread([one, two, three]), one


def grad_in(ids, g_blocks, wo, at):
    return call(
        functools.partial(grad_in_kernel, at), "grad_in", [((HALF, D), bf16), ((HALF, BLK), bf16)], (ids, *g_blocks, wo), 3,
        [dma(8)], raw=range(1, 9),
    )


def body(tokens, segment, ln_gain, ln_bias, w_qkv, w_out, w_in, b_in, w_fc, b_fc, cotangent):
    xh = lax.axis_index("xh")
    ids = jnp.stack([lax.axis_index("y"), lax.axis_index("core"), xh, lax.axis_index("xl"), lax.axis_index("z")]).astype(jnp.int32)
    own = tokens[0]
    full = (HALF, D)
    blk = (BLK, D)
    head = (HALF, BLK)
    room = lambda shape, kind=f32: pltpu.VMEM(shape, kind)
    chunks = [room((8, BLK, BLK), bf16)]

    group_seg = segment[0]
    positions = positions_of(group_seg)
    seg = lax.dynamic_slice_in_dim(group_seg, xh * HALF, HALF, 0)
    cosine, sine = rope_tables(lax.dynamic_slice_in_dim(positions, xh * HALF, HALF, 0))
    qseg = jnp.broadcast_to(seg[None, :].astype(f32), (8, HALF))

    both = jnp.concatenate([own, cotangent[0]], 0)
    (p0,) = call(
        pack_first_kernel, "pack_first", [(blk, bf16)], (ids, w_in, w_fc), 3, chunks + [dma(10)], raw=(1, 2), limit=62, after=(both,),
    )
    other0 = shift(p0, "xl", 1, 2)
    (q0,) = call(
        pack_q_kernel, "pack_q", [((8, 144, 384), bf16)], (ids, w_qkv, ln_gain, ln_bias, b_fc, b_in), 3,
        [room((144, 384), bf16), room((3, 2, BLK), bf16), room((2, 512), bf16), dma(7), dma(8)],
        raw=(1, 2, 3, 4, 5), out_raw=(0,), after=(cosine, other0), limit=62,
    )
    wq0 = lax.all_to_all(q0, FS, 0, 0, tiled=True)
    (p1,) = call(
        pack_second_kernel, "pack_second", [((BLK, 1408), bf16)], (ids, w_in, w_fc, w_qkv), 3, chunks + [dma(13)], raw=(1, 2, 3), limit=62,
        after=(wq0,),
    )
    tok_blocks = gather_blocks(both, lambda *x: gate_all(ids, x, (q0,)))
    w0 = gather_fsdp(ids, p0, other0)

    def attend_own(layer, q, kv, normed, w, before):
        kv0 = lax.ppermute(kv, "xh", [(0, 1)])
        own_part = call(
            attn_own_kernel, "attn_own", [((BLK, HALF), f32), ((2, HALF), f32), ((2, HALF), f32)], (ids, q, kv, qseg), 5, limit=62 if layer == 0 else None
        )
        first = before(own_part[1:2])
        return kv0, ff(ids, layer, normed, w, bi, first), own_part, first

    def attend_full(layer, q, kv0, act, own_part, after):
        active, slope, feed = act
        attn, lse, mine, away = call(
            attn_full_kernel, "attn_full", [(head, bf16), ((2, HALF), f32)] + [((4, BLK, D), bf16)] * 2,
            (ids, q, kv0, *own_part, feed, wo[layer]), 8, [room((BLK, HALF))], after=after,
        )
        return (kv0, active, slope, attn, lse), (mine, away)

    normed0, xhat0, q_0, kv_0, gain, bias, bfc, bi = call(
        qkv_first_kernel, "qkv_first",
        [(full, bf16), (full, bf16), (head, bf16), ((HALF, 256), bf16)] + [((2, D), f32)] * 3 + [((2, 512), f32)],
        (ids, *tok_blocks, wq0, cosine, sine), 6, [room(full, bf16), dma(8)], raw=range(1, 9), out_vm=(4, 5, 6, 7),
        limit=62,
    )

    def fetch_wo(layer, after):
        (out,) = call(
            functools.partial(pass_kernel, layer), "pass_wo", [(blk, bf16)], (ids, w_out), 1, [dma(1)], raw=(1,), after=after,
            limit=62,
        )
        return transpose_owner(out)

    def spread_w1(after):
        return call(
            four_kernel, "four", [((4, 2, BLK, 1408), bf16)], (ids, p1, shift(p1, "xl", 1, 2)), 2, [dma(8)], out_raw=(0,),
            after=after, limit=62,
        )

    kv0, act, own_part, (four,) = attend_own(0, q_0, kv_0, normed0, w0, spread_w1)
    wo = [fetch_wo(0, own_part[1:2])]
    saved0, ends = attend_full(0, q_0, kv0, act, own_part, ())
    w1 = [lax.all_to_all(gate(ids, four, (saved0[3],)), "z", 0, 0, tiled=True).reshape(8, BLK, 1408)]
    terms, sent = scatter(ids, *ends)
    x1, normed_own = call(
        fwd_end_kernel, "fwd_end", [(blk, f32), (blk, bf16)], (ids, *terms, own, gain, bias, bfc), 2,
        vm=range(1, 9), out_vm=(0, 1), limit=8,
    )
    blocks = gather_blocks(normed_own)
    normed1, q_1, kv_1 = call(
        qkv_kernel, "qkv", [(full, bf16), (head, bf16), ((HALF, 256), bf16)], (ids, *blocks, *w1, cosine, sine), 4,
        [room((8, BLK, 384), bf16), dma(8), dma(1)], raw=range(1, 10),
    )
    kv0, act, own_part, _ = attend_own(1, q_1, kv_1, normed1, w1, lambda after: ())
    wo.append(fetch_wo(1, (q_1,)))
    gr_top, dattn_top = grad_in(ids, tok_blocks, wo[1], BLK)
    saved1, ends = attend_full(1, q_1, kv0, act, own_part, ())
    terms, _ = scatter(ids, *ends)
    (mixed,) = call(
        last_end_kernel, "last_end", [(blk, bf16)], (ids, *terms, x1, bfc), 2, vm=range(1, 7), out_vm=(0,), limit=8
    )

    def back(q, kv, normed, w, saved, gr, dattn, rows):
        kv0, active, slope, attn, lse = saved
        dqt0, dkv0 = call(
            grad_full_kernel, "grad_full", [((BLK, HALF), f32), ((HALF, 256), bf16)], (ids, q, kv0, dattn, attn, lse), 8,
            [room(head)] * 2,
        )
        got = lax.ppermute(dkv0, "xh", [(1, 0)])
        part, dbi, payload = ff_back_outer(ids, rows, gr, slope, active, attn, normed, w, (dqt0,))
        pieces = call(
            grad_own_kernel, "grad_own", [((HALF, 384), bf16)], (ids, q, kv, dattn, attn, lse, qseg, dqt0), 5,
            [room((BLK, HALF)), room(head), room(head)],
        )
        return pieces, got, payload, part, dbi

    part_outs = [((4, BLK, D), bf16), ((4, BLK, D), bf16)]
    pieces, got, payload1, part, dbi1 = back(q_1, kv_1, normed1, w1, saved1, gr_top, dattn_top, 384)
    mine, away, payload1 = call(
        combine_kernel, "combine", part_outs + [((8, 384, 512), bf16)],
        (ids, *pieces, got, cosine, sine, part, *w1, normed1, payload1), 6,
        [room((HALF, 384), bf16), room((8, 96, 512), bf16), room((8, BLK, 384), bf16), dma(1), room(full, bf16),
         dma(1)], raw=(6, 7, 8), out_raw=(2,),
        alias={8: 2}, after=(mixed,),
    )
    terms, sent = scatter(ids, mine, away)
    got_a = lax.all_to_all(payload1, FS, 0, 0, tiled=True)
    g1, gr1, sums1 = call(
        bwd_end_kernel, "bwd_end", [(blk, f32), (blk, bf16), ((8, D), f32)], (ids, *terms, x1, gain, cotangent[0]), 2,
        vm=range(1, 8), out_vm=(0, 1, 2), limit=8,
    )
    g_blocks = gather_blocks(gr1)
    gr, dattn = grad_in(ids, g_blocks, wo[0], 0)
    pieces, got, payload, part, dbi0 = back(q_0, kv_0, normed0, w0, saved0, gr, dattn, 400)
    low1, p1 = over_groups(ids, "fsum_top", got_a, after=pieces[:1])
    (main1,) = call(xsum_top_kernel, "xsum_top", [((352, 512), bf16)], (ids, low1, shift(low1, "xh", 1, 2)), 2)
    mine, away, payload = call(
        combine_first_kernel, "combine_first", part_outs + [((8, 400, 512), bf16)],
        (ids, *pieces, got, cosine, sine, wq0, part, xhat0, normed0, sums1, dbi0, dbi1, payload), 9,
        [room((HALF, 384), bf16), room((8, 112, 512), bf16), dma(1)], raw=(12,), out_raw=(2,), alias={12: 2}, after=(main1,),
    )
    terms, sent = scatter(ids, mine, away)
    (g0,) = call(
        bwd_last_kernel, "bwd_last", [(blk, f32)], (ids, *terms, own, gain, g1), 2, vm=range(1, 8), out_vm=(0,), limit=8
    )
    top_rows = gather_blocks(main1)
    shapes = [((2, BLK, 4096), f32), ((2, 512, D), f32), ((2, BLK, 3 * D), f32)]
    rooms = lambda n: [room(s[0][1:]) for s in shapes] + [room((4, 2, n, 512), bf16), dma(8), dma(3)]
    outs = call(assemble_top_kernel, "assemble_top", shapes, (ids, *top_rows), 5, rooms(352), raw=range(1, 9), out_raw=(0, 1, 2))
    low0, piece = over_groups(ids, "fsum_first", lax.all_to_all(payload, FS, 0, 0, tiled=True), (p1,), (g0, outs[2]))
    piece = transpose_owner(piece)
    swap = lambda x: shift(x, "xh", 1, 2)
    (last,) = call(
        xsum_last_kernel, "xsum_last", [((432, 512), bf16)], (ids, low0, swap(low0), piece, swap(piece)), 2,
    )
    last_blocks = gather_blocks(last)
    o_i, o_f, o_q, o_o, o_g, o_s, o_bf, o_bi = call(
        finish_kernel, "finish", shapes + [((2, BLK, D), f32)] + [((2, BLK), f32)] * 3 + [((2, 512), f32)],
        (ids, *last_blocks, *outs), 6, rooms(432)[:-1] + [pltpu.SemaphoreType.DMA((6, 1))], raw=range(1, 12), out_raw=(0, 1, 2),
        alias={9: 0, 10: 1, 11: 2},
    )
    return mixed[None], g0[None], o_g, o_s, o_q, o_o, o_i, o_bi, o_f, o_bf


def solution(mesh):
    fine = Mesh(mesh.devices.reshape(2, 4, 2, 4, 2), AXES)
    seq = ("xh", "y", "core")
    tok = P(FS, seq, None)
    two = P(None, FS)
    three = P(None, FS, None)
    in_specs = (tok, P(FS, None), two, two, three, three, three, two, three, two, tok)
    out_specs = (tok, tok, two, two, three, three, three, two, three, two)
    return jax.shard_map(body, mesh=fine, in_specs=in_specs, out_specs=out_specs, check_vma=False)
```

```python
import functools
import jax
import jax.numpy as jnp
from jax import lax
from jax.experimental import pallas as pl
from jax.experimental.pallas import tpu as pltpu
from jax.sharding import Mesh, PartitionSpec as P

ROT = 32
CONTS = 8
D = 1024
HALF = 1024
BLK = 128
QB = 256
AXES = ("xh", "y", "core", "z", "xl")
FS = ("z", "xl")
f32 = jnp.float32
bf16 = jnp.bfloat16
NT = (((1,), (1,)), ((), ()))
VM = pl.BlockSpec(memory_space=pltpu.VMEM)
SM = pl.BlockSpec(memory_space=pltpu.SMEM)
ANY = pl.BlockSpec(memory_space=pl.ANY)
HBM = pl.BlockSpec(memory_space=pltpu.HBM)
MB = 1024 * 1024


def sds(*args):
    return [jax.ShapeDtypeStruct(s, t) for s, t in args]


class Far:
    def __init__(self, ref, copy):
        self.ref, self.copy = ref, copy

    def here(self):
        if self.copy is not None:
            self.copy.wait()
            self.copy = None
        return self.ref

    def __getitem__(self, index):
        return self.here()[index]

    @property
    def shape(self):
        return self.ref.shape


class Out:
    def __init__(self, ref, copy):
        self.ref, self.copy, self.sent = ref, copy, False

    def __getitem__(self, index):
        return self.ref[index]

    def __setitem__(self, index, value):
        self.ref[index] = value

    @property
    def dtype(self):
        return self.ref.dtype

    @property
    def shape(self):
        return self.ref.shape

    def send(self):
        self.copy.start()
        self.sent = True


COST = 0.001
LIMIT = 51


def call(kernel, name, outs, args, us, scratch=(), limit=None, after=(), raw=(), vm=(), out_raw=(), out_vm=(), alias=None):
    n, m = len(args), len(outs)
    fetched = [i for i in range(1, n) if i not in raw and i not in vm]
    staged = [i for i in range(m) if i not in out_raw and i not in out_vm]

    def run(*refs):
        ins = list(refs[:n])
        results = list(refs[n + len(after) : n + len(after) + m])
        rest = list(refs[n + len(after) + m :])
        own, rest = rest[: len(scratch)], rest[len(scratch) :]
        sems = rest[-1]
        copies = []
        for k, i in enumerate(fetched):
            copy = pltpu.make_async_copy(ins[i], rest[k], sems.at[k])
            copies.append(copy)
            ins[i] = Far(rest[k], copy)
        for copy in copies:
            copy.start()
        for k, i in enumerate(staged):
            ref = rest[len(fetched) + k]
            results[i] = Out(ref, pltpu.make_async_copy(ref, results[i], sems.at[len(fetched) + k]))
        kernel(*ins, *results, *own)
        for i in fetched:
            ins[i].here()
        for i in staged:
            if not results[i].sent:
                results[i].send()
        for i in staged:
            results[i].copy.wait()

    room = [pltpu.VMEM(args[i].shape, args[i].dtype) for i in fetched]
    room += [pltpu.VMEM(outs[i][0], outs[i][1]) for i in staged]
    return pl.pallas_call(
        run,
        out_shape=sds(*outs),
        in_specs=[SM] + [VM if i in vm else HBM for i in range(1, n)] + [ANY] * len(after),
        out_specs=[VM if i in out_vm else HBM for i in range(m)],
        scratch_shapes=list(scratch) + room + [pltpu.SemaphoreType.DMA((max(1, len(room)),))],
        input_output_aliases=alias or {},
        compiler_params=pltpu.CompilerParams(vmem_limit_bytes=(limit or LIMIT) * MB),
        cost_estimate=pl.CostEstimate(flops=int(us * COST * 1e9), bytes_accessed=int(us * COST * 1e6), transcendentals=0),
        name=name,
    )(*args, *after)


def dma(n):
    return pltpu.SemaphoreType.DMA((n,))


def copy_all(pairs, sems):
    copies = [pltpu.make_async_copy(a, b, sems.at[i]) for i, (a, b) in enumerate(pairs)]
    for copy in copies:
        copy.start()
    return copies


def wait_all(copies):
    for copy in copies:
        copy.wait()


def shift(x, axis, by, size):
    return lax.ppermute(x, axis, [(i, (i + by) % size) for i in range(size)])


def gather_blocks(own, hold=None):
    one = shift(own, "y", -1, 4)
    three = shift(own, "y", 1, 4)
    two = shift(own, "y", 2, 4)
    if hold is not None:
        one, two, three = hold(one, two, three)
    blocks = []
    for mine in (own, one, two, three):
        blocks += [mine, shift(mine, "core", 1, 2)]
    return blocks


def spread(low):
    return [shift(low[r - 1], "y", r, 4) for r in (1, 2, 3)]


def transpose_owner(x):
    pairs = [(j * 8 + f, f * 8 + j) for j in range(8) for f in range(8)]
    return lax.ppermute(x, ("y", "core", "z", "xl"), pairs)


def gate(ids, x, after):
    (out,) = call(lambda *refs: None, "gate", [(x.shape, x.dtype)], (ids, x), 1, raw=(1,), out_raw=(0,), after=after, alias={1: 0})
    return out


def gate_all(ids, xs, after):
    n = len(xs)
    return call(
        lambda *refs: None, "gate", [(x.shape, x.dtype) for x in xs], (ids, *xs), 1, raw=range(1, n + 1), out_raw=range(n),
        after=after, alias={i + 1: i for i in range(n)},
    )


def gather_fsdp(ids, x, got, after=()):
    (pair,) = call(
        pair_kernel, "pair", [((2,) + x.shape, bf16)], (ids, x, got), 2, [dma(2)], out_raw=(0,), after=after, limit=62,
    )
    return [pair, shift(pair, "z", -1, 4), shift(pair, "z", 2, 4), shift(pair, "z", 1, 4)]


def weight_copies(ids, pairs, cols, room):
    if len(pairs) == 1:
        return [(pairs[0].at[:, :, cols], room)]
    out = []
    for r in range(4):
        out.append((pairs[r].at[:, :, cols], room.at[pl.ds(2 * lax.rem(ids[4] + r, 4), 2)]))
    return out


def slot(ids, r, s):
    y = lax.rem(ids[0] + r, 4)
    c = ids[1] if s == 0 else 1 - ids[1]
    return y * 2 + c


def rows_of(ids, r, s, n=BLK):
    return pl.ds(pl.multiple_of(slot(ids, r, s) * n, n), n)


def turn(v, cosine, sine):
    lane = lax.broadcasted_iota(jnp.int32, v.shape, 1)
    partner = jnp.where(lane % 2 == 0, pltpu.roll(v, BLK - 1, 1), pltpu.roll(v, 1, 1))
    return v * cosine + partner * sine


def stats(x):
    average = jnp.mean(x, axis=-1, keepdims=True)
    centred = x - average
    variance = jnp.mean(centred * centred, axis=-1, keepdims=True)
    inv = lax.rsqrt(variance + 1e-05)
    return centred * inv, inv


def gelu_both(x):
    a = 0.7978845608028654
    b = 0.044715
    sq = x * x
    t = jnp.tanh(a * x * (1.0 + b * sq))
    half = 0.5 * (1.0 + t)
    slope = half + 0.5 * x * (1.0 - t * t) * a * (1.0 + 3.0 * b * sq)
    return x * half, slope


def dot(a, b):
    return jnp.dot(a, b, preferred_element_type=f32)


def dot_nt(a, b):
    return lax.dot_general(a, b, NT, preferred_element_type=f32)


def pack_q_kernel(ids, wq, gain, bias, bfc, bin_, q0, room, small, binv, sems, out_sems):
    j = ids[0] * 2 + ids[1]
    pairs = []
    for part in range(3):
        cols = pl.ds(pl.multiple_of(part * D + j * BLK, BLK), BLK)
        pairs.append((wq.at[0, :, cols], room.at[0:BLK, part * BLK : part * BLK + BLK]))
    pairs += [(ref, small.at[i]) for i, ref in enumerate((gain, bias, bfc))]
    pairs.append((bin_, binv))
    wait_all(copy_all(pairs, sems))
    chunk = binv[:, pl.ds(pl.multiple_of((j // 2) * BLK, BLK), BLK)].astype(f32)
    chunk = jnp.where(j % 2 == 1, pltpu.roll(chunk, 64, 1), chunk)
    lane = lax.broadcasted_iota(jnp.int32, (1, BLK), 1)
    row2 = jnp.where(lane < 64, chunk[0:1], pltpu.roll(chunk, 64, 1)[1:2])
    blank = jnp.zeros((13, BLK), f32)
    cols = [jnp.concatenate([small[i].astype(f32), row2, blank], 0) for i in range(3)]
    room[BLK:, :] = jnp.concatenate(cols, 1).astype(bf16)
    wait_all(copy_all([(room, q0.at[f]) for f in range(8)], out_sems))


def pack_layer(layer, ids, wi, wf, out, chunks, sems, more=()):
    j = ids[0] * 2 + ids[1]
    rows = pl.ds(pl.multiple_of(j * 64, 64), 64)
    pairs = []
    for f in range(8):
        cols = pl.ds(pl.multiple_of(f * 512 + (j // 2) * BLK, BLK), BLK)
        pairs.append((wi.at[layer, :, cols], chunks.at[f]))
    pairs.append((wf.at[layer, rows, 0:512], out.ref.at[0:64, 512:1024]))
    pairs.append((wf.at[layer, rows, 512:1024], out.ref.at[64:128, 512:1024]))
    wait_all(copy_all(pairs + list(more), sems))
    lane = lax.broadcasted_iota(jnp.int32, (BLK, BLK), 1)
    odd = j % 2 == 1
    for pair in range(4):
        a = chunks[2 * pair].astype(f32)
        b = chunks[2 * pair + 1].astype(f32)
        first = jnp.where(odd, pltpu.roll(a, 64, 1), a)
        second = jnp.where(odd, b, pltpu.roll(b, 64, 1))
        out[:, pair * BLK : pair * BLK + BLK] = jnp.where(lane < 64, first, second).astype(bf16)


def pack_first_kernel(ids, wi, wf, out, chunks, sems):
    pack_layer(0, ids, wi, wf, out, chunks, sems)


def pack_second_kernel(ids, wi, wf, wq, out, chunks, sems):
    j = ids[0] * 2 + ids[1]
    more = []
    for part in range(3):
        cols = pl.ds(pl.multiple_of(part * D + j * BLK, BLK), BLK)
        more.append((wq.at[1, :, cols], out.ref.at[:, D + part * BLK : D + part * BLK + BLK]))
    pack_layer(1, ids, wi, wf, out, chunks, sems, more)


def pass_kernel(layer, ids, x, out, sems):
    wait_all(copy_all([(x.at[layer], out.ref)], sems))


def join_kernel(ids, a, b, out, sems):
    wait_all(copy_all([(a, out.ref.at[0:BLK]), (b, out.ref.at[BLK : 2 * BLK])], sems))


def pair_kernel(ids, own, got, out, sems):
    xl = ids[3]
    wait_all(copy_all([(own.here(), out.at[xl]), (got.here(), out.at[1 - xl])], sems))


def four_kernel(ids, own, got, out, sems):
    xl = ids[3]
    mine, other = own.here(), got.here()
    wait_all(copy_all([(src, out.at[z, at]) for z in range(4) for src, at in ((mine, xl), (other, 1 - xl))], sems))


def params_part(rows_of_f, gain, bias, bfc, bi):
    lane = lax.broadcasted_iota(jnp.int32, (1, BLK), 1)
    for f in range(8):
        cols = slice(f * BLK, f * BLK + BLK)
        rows = rows_of_f[f].astype(f32)
        gain[:, cols] = rows[0:2, 0:BLK]
        bias[:, cols] = rows[0:2, BLK : 2 * BLK]
        bfc[:, cols] = rows[0:2, 2 * BLK :]
    for pair in range(4):
        a = rows_of_f[2 * pair].astype(f32)[2:3, :BLK]
        b = rows_of_f[2 * pair + 1].astype(f32)[2:3, :BLK]
        cols = slice(pair * BLK, pair * BLK + BLK)
        bi[0:1, cols] = jnp.where(lane < 64, a, pltpu.roll(b, 64, 1))
        bi[1:2, cols] = jnp.where(lane < 64, pltpu.roll(a, 64, 1), b)


def qkv_part(normed, w, cosine, sine, q, kv):
    for i in range(HALF // QB):
        rows = slice(i * QB, i * QB + QB)
        out = dot(normed[rows, :], w).astype(bf16).astype(f32)
        cb = cosine[rows, :]
        sb = sine[rows, :]
        kv[rows, :BLK] = turn(out[:, BLK : 2 * BLK], cb, sb).astype(bf16)
        kv[rows, BLK:] = out[:, 2 * BLK :].astype(bf16)
        q[rows, :] = (turn(out[:, :BLK], cb, sb).astype(bf16).astype(f32) * 0.125).astype(bf16)


def take_blocks(ids, blocks, room, sems, at=0):
    part = slice(at, at + BLK)
    return copy_all([(blocks[2 * r + s].at[part], room.at[rows_of(ids, r, s)]) for r in range(4) for s in range(2)], sems)


def qkv_first_kernel(ids, *refs):
    blocks, (wq, cosine, sine), refs = refs[:8], refs[8:11], refs[11:]
    normed, xhat, q, kv, gain, bias, bfc, bi, raw, sems = refs
    copies = take_blocks(ids, blocks, raw, sems)
    w = wq.here()
    params_part([w[f, BLK:, :] for f in range(8)], gain, bias, bfc, bi)
    for k in range(8):
        copies[k].wait()
        rows = rows_of(ids, k // 2, k % 2)
        x, _ = stats(raw[rows, :].astype(f32))
        xhat[rows, :] = x.astype(bf16)
        normed[rows, :] = (x * gain[0:1, :] + bias[0:1, :]).astype(bf16)
    xhat.send()
    normed.send()
    qkv_part(normed, w[:, :BLK, :].reshape(D, 384), cosine, sine, q, kv)


def qkv_kernel(ids, *refs):
    blocks, w, (cosine, sine), (normed, q, kv, wq, sems, wsem) = refs[:8], refs[8:9], refs[9:11], refs[11:]
    copies = copy_all(weight_copies(ids, w, slice(1024, 1408), wq), wsem)
    copies += take_blocks(ids, blocks, normed.ref, sems)
    wait_all(copies)
    normed.send()
    qkv_part(normed, wq[...].reshape(D, 384), cosine, sine, q, kv)


def ff_kernel(layer, ids, far, bi, *refs):
    w, (active, slope, feed, wi, wf, va, vs, vf, wsems, sems, normed) = refs[:-11], refs[-11:]
    copies = copy_all(weight_copies(ids, w, slice(0, 512), wi), wsems.at[0])
    rows = slice(0, QB)
    copies += copy_all([(far.at[rows], normed.at[rows])], wsems.at[2])
    late = copy_all(weight_copies(ids, w, slice(512, 1024), wf), wsems.at[1])
    rows = slice(QB, HALF)
    rest = copy_all([(far.at[rows], normed.at[rows])], wsems.at[3])
    wait_all(copies)
    left = right = None
    sent = []
    for i in range(HALF // QB):
        rows = slice(i * QB, i * QB + QB)
        if i == 1:
            wait_all(rest)
        pre = dot(normed[rows, :], wi[...].reshape(D, 512)) + bi[layer : layer + 1, :]
        act, der = gelu_both(pre)
        act = act.astype(bf16)
        va[rows, :] = act
        vs[rows, :] = der.astype(bf16)
        if i == 0:
            wait_all(late)
            left, right = wf[:, 0:64, :].reshape(512, 512), wf[:, 64:128, :].reshape(512, 512)
        vf[rows, :512] = dot(act, left).astype(bf16)
        vf[rows, 512:] = dot(act, right).astype(bf16)
        pairs = [(v.at[rows], out.at[rows]) for v, out in ((va, active), (vs, slope), (vf, feed))]
        sent += copy_all(pairs, sems.at[i])
    wait_all(sent)


def ff(ids, layer, normed, w, bi, after=()):
    room = lambda *shape: pltpu.VMEM(shape, bf16)
    return call(
        functools.partial(ff_kernel, layer), "ff", [((HALF, 512), bf16), ((HALF, 512), bf16), ((HALF, D), bf16)],
        (ids, normed, bi, *w), 5,
        [room(8, BLK, 512), room(8, BLK, 512), room(HALF, 512), room(HALF, 512), room(HALF, D),
         pltpu.SemaphoreType.DMA((4, 4)), pltpu.SemaphoreType.DMA((4, 3)), room(HALF, D)],
        raw=[1, *range(3, 3 + len(w))], out_raw=(0, 1, 2), limit=62 - 11 * layer, after=after,
    )


def head_cut(x):
    lane = lax.broadcasted_iota(jnp.int32, x.shape, 1)
    zero = jnp.zeros((), x.dtype)
    return [jnp.where(lane < 64, x, zero), jnp.where(lane >= 64, x, zero)]


def seen(i, kk, qseg, kseg, QB):
    q0 = i * QB
    qs = qseg[0:1, q0 : q0 + QB]
    ks = kseg[0:kk, 0:1]
    key = lax.broadcasted_iota(jnp.int32, (kk, QB), 0)
    query = q0 + lax.broadcasted_iota(jnp.int32, (kk, QB), 1)
    return (key <= query) & ((ks == 0) | (ks == qs))


def flip(x):
    return jnp.transpose(x.astype(f32)).astype(bf16)


def attn_own_kernel(ids, q, kv, qseg, acc, m_out, l_out):
    qseg = qseg[...]
    kseg = jnp.transpose(qseg)
    km = head_cut(kv[:, :BLK])
    vt = flip(kv[:, BLK:])
    for i in range(HALF // 512):
        cols = slice(i * 512, (i + 1) * 512)
        kk = (i + 1) * 512
        allowed = seen(i, kk, qseg, kseg, 512)
        for h in range(2):
            rows = slice(h * 64, h * 64 + 64)
            s = jnp.where(allowed, dot_nt(km[h][:kk], q[cols, :]), -1e30)
            m = jnp.max(s, axis=0, keepdims=True)
            p = jnp.exp(s - m)
            l_out[h : h + 1, cols] = jnp.sum(p, axis=0, keepdims=True)
            m_out[h : h + 1, cols] = m
            acc[rows, cols] = dot(vt[rows, :kk], p.astype(bf16))


def split_rows(ids, mine, away, block):
    for r in range(4):
        away[r] = block(rows_of(ids, r, 1)).astype(bf16)
    away.send()
    for r in range(4):
        mine[r] = block(rows_of(ids, r, 0)).astype(bf16)


def attn_full_kernel(ids, q, kv0, acc, m_in, l_in, feed, wo, attn, lse, mine, away, tmp):
    upper = ids[2] == 1
    for ref in (q, kv0, acc, m_in, l_in):
        ref.here()

    @pl.when(upper)
    def _():
        km = head_cut(kv0[:, :BLK])
        vt = flip(kv0[:, BLK:])
        for i in range(HALF // 512):
            cols = slice(i * 512, (i + 1) * 512)
            for h in range(2):
                rows = slice(h * 64, h * 64 + 64)
                s = dot_nt(km[h], q[cols, :])
                m0 = m_in[h : h + 1, cols]
                m = jnp.maximum(m0, jnp.max(s, axis=0, keepdims=True))
                p = jnp.exp(s - m)
                a = jnp.exp(m0 - m)
                l = l_in[h : h + 1, cols] * a + jnp.sum(p, axis=0, keepdims=True)
                o = dot(vt[rows, :], p.astype(bf16))
                tmp[rows, cols] = (acc[rows, cols] * a + o) / l
                lse[h : h + 1, cols] = m + jnp.log(l)

    @pl.when(jnp.logical_not(upper))
    def _():
        for h in range(2):
            rows = slice(h * 64, h * 64 + 64)
            l = l_in[h : h + 1, :]
            tmp[rows, :] = acc[rows, :] / l
            lse[h : h + 1, :] = m_in[h : h + 1, :] + jnp.log(l)

    attn[...] = jnp.transpose(tmp[...]).astype(bf16)
    attn.send()
    lse.send()
    split_rows(ids, mine, away, lambda rows: feed[rows, :].astype(f32) + dot(attn[rows, :], wo[...]))


def mid_kernel(ids, mine, got, total, one, two, three):
    for r, out in ((1, one), (2, two), (3, three)):
        out[...] = (mine[r].astype(f32) + got[r].astype(f32)).astype(bf16)
    total[...] = mine[0].astype(f32) + got[0].astype(f32)


def summed(total, one, two, three):
    return total[...] + one[...].astype(f32) + two[...].astype(f32) + three[...].astype(f32)


def fwd_end_kernel(ids, total, one, two, three, x, gain, bias, bfc, x_new, normed):
    new = x[...].astype(f32) + summed(total, one, two, three) + bfc[0:1, :]
    x_new[...] = new
    xhat, _ = stats(new)
    normed[...] = (xhat * gain[1:2, :] + bias[1:2, :]).astype(bf16)


def last_end_kernel(ids, total, one, two, three, x, bfc, out):
    out[...] = (x[...] + summed(total, one, two, three) + bfc[1:2, :]).astype(bf16)


def grad_in_kernel(at, ids, *refs):
    blocks, (wo, gr, dattn, sems) = refs[:8], refs[8:]
    wait_all(take_blocks(ids, blocks, gr.ref, sems, at))
    gr.send()
    dattn[...] = dot_nt(gr[...], wo[...]).astype(bf16)


def row_delta(attn, do):
    prod = attn[...].astype(f32) * do[...].astype(f32)
    head = lax.broadcasted_iota(jnp.int32, (8, BLK), 0)
    lane = lax.broadcasted_iota(jnp.int32, (8, BLK), 1) // 64
    pickers = jnp.where(head == lane, 1.0, 0.0).astype(f32)
    return lax.dot_general(pickers, prod, NT, precision=lax.Precision.HIGHEST, preferred_element_type=f32)


def grad_block(km, vm, kt, qm, dom, q_blk, do_blk, lse, delta, allowed):
    p = jnp.exp(dot_nt(km, q_blk) - lse)
    if allowed is not None:
        p = jnp.where(allowed, p, 0.0)
    dp = dot_nt(vm, do_blk)
    ds = (p * (dp - delta)).astype(bf16)
    return dot(kt, ds), dot(ds, qm), dot(p.astype(bf16), dom)


def grad_full_kernel(ids, q, kv0, do, attn, lse, dqt, dkv, acck, accv):
    upper = ids[2] == 1
    for ref in (q, kv0, do, attn, lse):
        ref.here()

    @pl.when(upper)
    def _():
        delta = row_delta(attn, do)
        qm, km, vm, dom = [head_cut(x) for x in (q[...], kv0[:, :BLK], kv0[:, BLK:], do[...])]
        kt = flip(kv0[:, :BLK])
        for i in range(HALF // 512):
            cols = slice(i * 512, (i + 1) * 512)
            for h in range(2):
                rows = slice(h * 64, h * 64 + 64)
                dq, dk, dv = grad_block(
                    km[h], vm[h], kt[rows, :], qm[h][cols], dom[h][cols], q[cols, :], do[cols, :],
                    lse[h : h + 1, cols], delta[h : h + 1, cols], None,
                )
                dqt[rows, cols] = dq
                if i == 0 and h == 0:
                    acck[...] = dk
                    accv[...] = dv
                else:
                    acck[...] += dk
                    accv[...] += dv
        dkv[:, :BLK] = acck[...].astype(bf16)
        dkv[:, BLK:] = accv[...].astype(bf16)

    @pl.when(jnp.logical_not(upper))
    def _():
        dqt[...] = jnp.zeros(dqt.shape, f32)
        dkv[...] = jnp.zeros(dkv.shape, bf16)


def grad_own_kernel(ids, q, kv, do, attn, lse, qseg, dqt0, out, tmp, dk_out, dv_out):
    qseg = qseg[...]
    kseg = jnp.transpose(qseg)
    delta = row_delta(attn, do)
    qm, km, vm, dom = [head_cut(x) for x in (q[...], kv[:, :BLK], kv[:, BLK:], do[...])]
    kt = flip(kv[:, :BLK])
    dk_out[...] = jnp.zeros(dk_out.shape, f32)
    dv_out[...] = jnp.zeros(dv_out.shape, f32)
    for i in range(HALF // 256):
        cols = slice(i * 256, (i + 1) * 256)
        kk = (i + 1) * 256
        allowed = seen(i, kk, qseg, kseg, 256)
        for h in range(2):
            rows = slice(h * 64, h * 64 + 64)
            dq, dk, dv = grad_block(
                km[h][:kk], vm[h][:kk], kt[rows, :kk], qm[h][cols], dom[h][cols], q[cols, :], do[cols, :],
                lse[h : h + 1, cols], delta[h : h + 1, cols], allowed,
            )
            tmp[rows, cols] = (dq + dqt0[rows, cols]) * 0.125
            dk_out[:kk, :] += dk
            dv_out[:kk, :] += dv
    out[:, :BLK] = jnp.transpose(tmp[...]).astype(bf16)
    out[:, BLK : 2 * BLK] = dk_out[...].astype(bf16)
    out[:, 2 * BLK :] = dv_out[...].astype(bf16)


def ff_back_outer_kernel(ids, *refs):
    far, w, refs = refs[:5], refs[5:-14], refs[-14:]
    part, dbi, out, wi, wf, vd, v, wsems, sems, gr, slope, active, attn, normed = refs
    rooms = (gr, slope, active, attn, normed)
    copies = copy_all(weight_copies(ids, w, slice(512, 1024), wf), wsems.at[0])
    rows = slice(0, 256)
    first = [(far[0].at[rows], gr.at[rows]), (far[1].at[rows], slope.at[rows])]
    copies += copy_all(first, wsems.at[2])
    late = copy_all(weight_copies(ids, w, slice(0, 512), wi), wsems.at[1])
    rows = slice(256, HALF)
    rest = copy_all([(far[0].at[rows], gr.at[rows]), (far[1].at[rows], slope.at[rows])], wsems.at[3])
    after = copy_all([(far[k], rooms[k]) for k in (2, 3, 4)], wsems.at[4])
    wait_all(copies)
    left, right = wf[:, 0:64, :].reshape(512, 512), wf[:, 64:128, :].reshape(512, 512)
    total = jnp.zeros((1, 512), f32)
    for i in range(HALF // 256):
        if i == 1:
            wait_all(rest)
        rows = slice(i * 256, i * 256 + 256)
        d = (dot_nt(gr[rows, :512], left) + dot_nt(gr[rows, 512:], right)) * slope[rows, :].astype(f32)
        total = total + jnp.sum(d, axis=0, keepdims=True)
        d = d.astype(bf16)
        vd[rows, :] = d
        if i == 0:
            wait_all(late)
        part[rows, :] = dot_nt(d, wi[...].reshape(D, 512)).astype(bf16)
    part.send()
    dbi[...] = jnp.concatenate([total, jnp.zeros((7, 512), f32)], 0)
    wait_all(after)
    wait_all(outer_rows(out, v, sems, active, gr, attn, normed, vd))


def ff_back_outer(ids, rows, gr, slope, active, attn, normed, w, after):
    room = lambda *shape: pltpu.VMEM(shape, bf16)
    return call(
        ff_back_outer_kernel, "ff_back_outer", [((HALF, D), bf16), ((8, 512), f32), ((8, rows, 512), bf16)],
        (ids, gr, slope, active, attn, normed, *w), 9,
        [room(8, BLK, 512), room(8, BLK, 512), room(HALF, 512), room(8, 288, 512), pltpu.SemaphoreType.DMA((5, 4)),
         pltpu.SemaphoreType.DMA((3, 2)), room(HALF, D), room(HALF, 512), room(HALF, 512), room(HALF, BLK), room(HALF, D)],
        raw=range(1, 6 + len(w)), out_raw=(2,), after=after,
    )


def combine_rows(ids, own, back, cosine, sine, dqkv):
    cb = cosine[...]
    sb = -sine[...]
    dqkv[:, :BLK] = turn(own[:, :BLK].astype(f32), cb, sb).astype(bf16)
    dk = own[:, BLK : 2 * BLK].astype(f32) + back[:, :BLK].astype(f32)
    dqkv[:, BLK : 2 * BLK] = turn(dk, cb, sb).astype(bf16)
    dqkv[:, 2 * BLK :] = (own[:, 2 * BLK :].astype(f32) + back[:, BLK:].astype(f32)).astype(bf16)


def combine_kernel(ids, own, back, cosine, sine, part, w1, far, _, mine, away, payload, dqkv, out, wq, wsem, normed, nsem):
    copies = copy_all(weight_copies(ids, (w1,), slice(1024, 1408), wq), wsem)
    late = copy_all([(far, normed)], nsem)
    combine_rows(ids, own, back, cosine, sine, dqkv)
    wait_all(copies)
    w = wq[...].reshape(D, 384)
    split_rows(ids, mine, away, lambda rows: part[rows, :].astype(f32) + dot_nt(dqkv[rows, :], w))
    mine.send()
    wait_all(late)
    g_q = outer(normed[...], dqkv[...])
    for f in range(8):
        pack_rows(out, f, g_q)
    wait_all(copy_all([(out, payload.at[:, 288:384])], wsem))


def combine_first_kernel(ids, own, back, cosine, sine, wq0, part, xhat, normed, sums1, dbi0, dbi1, *refs):
    _, mine, away, payload, dqkv, out, sems = refs
    combine_rows(ids, own, back, cosine, sine, dqkv)
    w = wq0[:, :BLK, :].reshape(D, 384)
    gain = jnp.zeros((1, D), f32)
    base = jnp.zeros((1, D), f32)
    for s, to in ((1, away), (0, mine)):
        for r in range(4):
            rows = rows_of(ids, r, s)
            block = part[rows, :].astype(f32) + dot_nt(dqkv[rows, :], w)
            to[r] = block.astype(bf16)
            gain = gain + jnp.sum(block * xhat[rows, :].astype(f32), axis=0, keepdims=True)
            base = base + jnp.sum(block, axis=0, keepdims=True)
        to.send()
    g_q = outer(normed[...], dqkv[...])
    lane = lax.broadcasted_iota(jnp.int32, (1, BLK), 1)
    blank = jnp.zeros((13, 384), f32)
    none = jnp.zeros((1, 256), f32)
    for f in range(8):
        pack_rows(out, f, g_q)
        cols = slice(f * BLK, f * BLK + BLK)
        row0 = jnp.concatenate([gain[:, cols], base[:, cols], sums1[3:4, cols]], 1)
        row1 = jnp.concatenate([sums1[0:1, cols], sums1[1:2, cols], sums1[2:3, cols]], 1)
        half = slice((f // 2) * BLK, (f // 2) * BLK + BLK)
        a = dbi0[0:1, half]
        b = dbi1[0:1, half]
        if f % 2 == 0:
            b = pltpu.roll(b, 64, 1)
        else:
            a = pltpu.roll(a, 64, 1)
        row2 = jnp.concatenate([jnp.where(lane < 64, a, b), none], 1)
        out[f, 96:112, :384] = jnp.concatenate([row0, row1, row2, blank], 0).astype(bf16)
        out[f, 96:112, 384:] = jnp.zeros((16, 128), bf16)
    wait_all(copy_all([(out, payload.at[:, 288:400])], sems))


def norm_back(dn, x, gain_row, g):
    xhat, inv = stats(x[...].astype(f32))
    dx = dn * gain_row
    dx = inv * (dx - jnp.mean(dx, -1, keepdims=True) - xhat * jnp.mean(dx * xhat, -1, keepdims=True))
    return xhat, g[...].astype(f32) + dx


def bwd_end_kernel(ids, total, one, two, three, x, gain, g, g_new, gr, sums):
    dn = summed(total, one, two, three)
    xhat, new = norm_back(dn, x, gain[1:2, :], g)
    g_new[...] = new
    gr[...] = new.astype(bf16)
    col = lambda v: jnp.sum(v, axis=0, keepdims=True)
    top = col(g[...].astype(f32))
    sums[...] = jnp.concatenate([col(dn * xhat), col(dn), top, col(new), jnp.zeros((4, D), f32)], 0)


def bwd_last_kernel(ids, total, one, two, three, x, gain, g, g_new):
    _, new = norm_back(summed(total, one, two, three), x, gain[0:1, :], g)
    g_new[...] = new


def outer(a, b):
    return lax.dot_general(a, b, (((0,), (0,)), ((), ())), preferred_element_type=f32).astype(bf16)


def pack_rows(out, f, g_q):
    for part in range(3):
        for group in range(4):
            piece = g_q[f * 128 + group * 32 : f * 128 + group * 32 + 32, part * BLK : part * BLK + BLK]
            out[f, part * 32 : part * 32 + 32, group * BLK : group * BLK + BLK] = piece


def outer_rows(out, v, sems, active, gr, attn, normed, dpre):
    for half in range(2):
        cols = slice(half * 512, half * 512 + 512)
        g_f = outer(active[...], gr[:, cols])
        g_o = outer(attn[...], gr[:, cols])
        for f in range(8):
            v[f, 128 + 64 * half : 192 + 64 * half, :] = g_f[f * 64 : f * 64 + 64]
            v[f, 256 + 16 * half : 272 + 16 * half, :] = g_o[f * 16 : f * 16 + 16]
    first = copy_all([(v.at[:, 128:288], out.at[:, 128:288])], sems.at[0])
    for half in range(2):
        cols = slice(half * 512, half * 512 + 512)
        g_i = outer(normed[:, cols], dpre[...])
        for k in range(4):
            v[4 * half + k, 0:128, :] = g_i[k * 128 : k * 128 + 128]
        group = slice(4 * half, 4 * half + 4)
        first += copy_all([(v.at[group, 0:128], out.at[group, 0:128])], sems.at[1 + half])
    return first


def fsum_kernel(ids, got, *refs):
    more, (low, piece, room, sems) = refs[:-4], refs[-4:]
    rows = got.shape[1]
    half = rows // 32 * 16
    parts = (slice(0, half), slice(half, rows))
    copies = copy_all([(got.at[:, part], room.at[:, part]) for part in parts], sems)
    for at in range(0, rows, 16):
        if at in (0, half):
            copies[0 if at == 0 else 1].wait()
        part = slice(at, at + 16)
        total = room[0, part, :].astype(f32)
        for f in range(1, 8):
            total = total + room[f, part, :].astype(f32)
        total = total.astype(bf16)
        if 256 <= at < 288:
            piece[at - 256 : at - 240, :] = total
        else:
            to = at if at < 256 else at - 32
            low[to : to + 16, :] = total
    for ref in more:
        piece[32:64, :] = ref[...]


def add_rows(terms, start, stop):
    total = terms[0][start:stop, :].astype(f32)
    for term in terms[1:]:
        total = total + term[start:stop, :].astype(f32)
    return total.astype(bf16)


def xsum_top_kernel(ids, low, got, main):
    main[...] = add_rows((low, got), 0, 352)


def xsum_last_kernel(ids, low, got, piece, piece_got, main):
    terms = (low, got)
    main[0:112, :] = add_rows(terms, 256, 368)
    main[112:368, :] = add_rows(terms, 0, 256)
    main[368:432, :] = add_rows((piece, piece_got), 0, 64)


def over_groups(ids, name, got, more=(), after=()):
    rows = got.shape[1]
    return call(
        fsum_kernel, name, [((rows - 32, 512), bf16), ((32 + 32 * len(more), 512), bf16)], (ids, got, *more), 3,
        [pltpu.VMEM(got.shape, bf16), dma(2)], raw=(1,), after=after,
    )


def place_in(zero, one, at, y, o_i, o_f):
    lane = lax.broadcasted_iota(jnp.int32, (BLK, BLK), 1)
    start = pl.multiple_of(y * BLK, BLK)
    for half in range(2):
        rows = slice(at + 128 + 64 * half, at + 192 + 64 * half)
        cols = slice(half * 512, half * 512 + 512)
        o_f[pl.ds(start, 64), cols] = zero[rows, :].astype(f32)
        o_f[pl.ds(start + 64, 64), cols] = one[rows, :].astype(f32)
    for pair in range(4):
        cols = slice(pair * BLK, pair * BLK + BLK)
        a, b = zero[at : at + BLK, cols].astype(f32), one[at : at + BLK, cols].astype(f32)
        even = pl.ds(pl.multiple_of(2 * pair * 512 + start, BLK), BLK)
        odd = pl.ds(pl.multiple_of((2 * pair + 1) * 512 + start, BLK), BLK)
        o_i[:, even] = jnp.where(lane < 64, a, pltpu.roll(b, 64, 1))
        o_i[:, odd] = jnp.where(lane < 64, pltpu.roll(a, 64, 1), b)


def place_q(zero, one, at, y, o_q):
    for part in range(3):
        rows = slice(at + part * 32, at + part * 32 + 32)
        start = pl.multiple_of(part * D + 2 * y * BLK, BLK)
        for group in range(4):
            cols = slice(group * BLK, group * BLK + BLK)
            to = slice(group * 32, group * 32 + 32)
            o_q[to, pl.ds(start, BLK)] = zero[rows, cols].astype(f32)
            o_q[to, pl.ds(start + BLK, BLK)] = one[rows, cols].astype(f32)


def fetch_rows(ids, blocks, room, sems):
    pairs = []
    for r in range(4):
        pairs += [(blocks[2 * r], room.at[r, ids[1]]), (blocks[2 * r + 1], room.at[r, 1 - ids[1]])]
    return copy_all(pairs, sems)


def assemble_top_kernel(ids, *refs):
    blocks, (o_i, o_f, o_q, vi, vf, vq, room, sems, out_sems) = refs[:8], refs[8:]
    copies = fetch_rows(ids, blocks, room, sems)
    for r in range(4):
        wait_all(copies[2 * r : 2 * r + 2])
        y = lax.rem(ids[0] + r, 4)
        place_in(room.at[r, 0], room.at[r, 1], 0, y, vi, vf)
        place_q(room.at[r, 0], room.at[r, 1], 256, y, vq)
    wait_all(copy_all([(vi, o_i.at[1]), (vf, o_f.at[1]), (vq, o_q.at[1])], out_sems))


def finish_kernel(ids, *refs):
    blocks, refs = refs[:8], refs[11:]
    o_i, o_f, o_q, o_o, o_g, o_s, o_bf, o_bi, vi, vf, vq, room, sems, out_sems = refs
    copies = fetch_rows(ids, blocks, room, sems)
    outs = []
    total = jnp.zeros((16, 384), f32)
    lane = lax.broadcasted_iota(jnp.int32, (1, BLK), 1)
    for r in range(4):
        wait_all(copies[2 * r : 2 * r + 2])
        y = lax.rem(ids[0] + r, 4)
        place_in(room.at[r, 0], room.at[r, 1], 112, y, vi, vf)
        rows = pl.ds(pl.multiple_of(y * BLK, BLK), BLK)
        outs += copy_all([(vf.at[rows], o_f.at[0, rows])], out_sems.at[r])
    outs += copy_all([(vi, o_i.at[0])], out_sems.at[4])
    for r in range(4):
        place_q(room.at[r, 0], room.at[r, 1], 0, lax.rem(ids[0] + r, 4), vq)
    outs += copy_all([(vq, o_q.at[0])], out_sems.at[5])
    for r in range(4):
        y = lax.rem(ids[0] + r, 4)
        for layer in range(2):
            for half in range(2):
                at = 368 + 32 * layer + 16 * half
                cols = slice(half * 512, half * 512 + 512)
                start = pl.multiple_of(y * 32, 32)
                o_o[layer, pl.ds(start, 16), cols] = room[r, 0, at : at + 16, :].astype(f32)
                o_o[layer, pl.ds(start + 16, 16), cols] = room[r, 1, at : at + 16, :].astype(f32)
        zero, one = room[r, 0, 96:112, :384].astype(f32), room[r, 1, 96:112, :384].astype(f32)
        total = total + zero + one
        a, b = zero[2:3, :BLK], one[2:3, :BLK]
        cols = pl.ds(pl.multiple_of(y * BLK, BLK), BLK)
        o_bi[0:1, cols] = jnp.where(lane < 64, a, pltpu.roll(b, 64, 1))
        o_bi[1:2, cols] = jnp.where(lane < 64, pltpu.roll(a, 64, 1), b)
    o_g[...] = total[0:2, :BLK]
    o_s[...] = total[0:2, BLK : 2 * BLK]
    o_bf[...] = total[0:2, 2 * BLK :]
    for ref in (o_o, o_g, o_s, o_bf, o_bi):
        ref.send()
    wait_all(outs)


def positions_of(group_seg):
    token_index = jnp.arange(group_seg.shape[0], dtype=jnp.int32)
    labels = jnp.arange(CONTS + 1, dtype=jnp.int32)
    member = (group_seg[:, None] == labels[None, :]).astype(jnp.int32)
    counts = jnp.sum(member, axis=0)
    starts = jnp.cumsum(counts) - counts
    own_start = jnp.sum(member * starts[None, :], axis=1)
    return token_index - own_start + jnp.where(group_seg > 0, counts[0], 0)


def rope_tables(positions):
    lane = jnp.arange(BLK, dtype=jnp.int32) % 64
    inverse = 10000.0 ** (-2.0 * (lane // 2).astype(f32) / ROT)
    phase = positions.astype(f32)[:, None] * jnp.where(lane < ROT, inverse, 0.0)[None, :]
    sign = jnp.where(lane % 2 == 0, -1.0, 1.0)
    return jnp.cos(phase), jnp.sin(phase) * sign[None, :]


def scatter(ids, mine, away):
    got = shift(away, "core", 1, 2)
    blk = (BLK, D)
    total, one, two, three = call(
        mid_kernel, "rs_mid", [(blk, f32)] + [(blk, bf16)] * 3, (ids, mine, got), 2, vm=(2,), out_vm=(0, 1, 2, 3), limit=8
    )
    return [total] + spread([one, two, three]), one


def grad_in(ids, g_blocks, wo, at):
    return call(
        functools.partial(grad_in_kernel, at), "grad_in", [((HALF, D), bf16), ((HALF, BLK), bf16)], (ids, *g_blocks, wo), 3,
        [dma(8)], raw=range(1, 9),
    )


def body(tokens, segment, ln_gain, ln_bias, w_qkv, w_out, w_in, b_in, w_fc, b_fc, cotangent):
    xh = lax.axis_index("xh")
    ids = jnp.stack([lax.axis_index("y"), lax.axis_index("core"), xh, lax.axis_index("xl"), lax.axis_index("z")]).astype(jnp.int32)
    own = tokens[0]
    full = (HALF, D)
    blk = (BLK, D)
    head = (HALF, BLK)
    room = lambda shape, kind=f32: pltpu.VMEM(shape, kind)
    chunks = [room((8, BLK, BLK), bf16)]

    group_seg = segment[0]
    positions = positions_of(group_seg)
    seg = lax.dynamic_slice_in_dim(group_seg, xh * HALF, HALF, 0)
    cosine, sine = rope_tables(lax.dynamic_slice_in_dim(positions, xh * HALF, HALF, 0))
    qseg = jnp.broadcast_to(seg[None, :].astype(f32), (8, HALF))

    both = jnp.concatenate([own, cotangent[0]], 0)
    (p0,) = call(
        pack_first_kernel, "pack_first", [(blk, bf16)], (ids, w_in, w_fc), 3, chunks + [dma(10)], raw=(1, 2), limit=62, after=(both,),
    )
    other0 = shift(p0, "xl", 1, 2)
    (q0,) = call(
        pack_q_kernel, "pack_q", [((8, 144, 384), bf16)], (ids, w_qkv, ln_gain, ln_bias, b_fc, b_in), 3,
        [room((144, 384), bf16), room((3, 2, BLK), bf16), room((2, 512), bf16), dma(7), dma(8)],
        raw=(1, 2, 3, 4, 5), out_raw=(0,), after=(cosine, other0), limit=62,
    )
    wq0 = lax.all_to_all(q0, FS, 0, 0, tiled=True)
    (p1,) = call(
        pack_second_kernel, "pack_second", [((BLK, 1408), bf16)], (ids, w_in, w_fc, w_qkv), 3, chunks + [dma(13)], raw=(1, 2, 3), limit=62,
        after=(wq0,),
    )
    tok_blocks = gather_blocks(both, lambda *x: gate_all(ids, x, (q0,)))
    w0 = gather_fsdp(ids, p0, other0)

    def attend_own(layer, q, kv, normed, w, before):
        kv0 = lax.ppermute(kv, "xh", [(0, 1)])
        own_part = call(
            attn_own_kernel, "attn_own", [((BLK, HALF), f32), ((2, HALF), f32), ((2, HALF), f32)], (ids, q, kv, qseg), 5, limit=62 if layer == 0 else None
        )
        first = before(own_part[1:2])
        return kv0, ff(ids, layer, normed, w, bi, first), own_part, first

    def attend_full(layer, q, kv0, act, own_part, after):
        active, slope, feed = act
        attn, lse, mine, away = call(
            attn_full_kernel, "attn_full", [(head, bf16), ((2, HALF), f32)] + [((4, BLK, D), bf16)] * 2,
            (ids, q, kv0, *own_part, feed, wo[layer]), 8, [room((BLK, HALF))], after=after,
        )
        return (kv0, active, slope, attn, lse), (mine, away)

    normed0, xhat0, q_0, kv_0, gain, bias, bfc, bi = call(
        qkv_first_kernel, "qkv_first",
        [(full, bf16), (full, bf16), (head, bf16), ((HALF, 256), bf16)] + [((2, D), f32)] * 3 + [((2, 512), f32)],
        (ids, *tok_blocks, wq0, cosine, sine), 6, [room(full, bf16), dma(8)], raw=range(1, 9), out_vm=(4, 5, 6, 7),
        limit=62,
    )

    def fetch_wo(layer, after):
        (out,) = call(
            functools.partial(pass_kernel, layer), "pass_wo", [(blk, bf16)], (ids, w_out), 1, [dma(1)], raw=(1,), after=after,
            limit=62,
        )
        return transpose_owner(out)

    def spread_w1(after):
        return call(
            four_kernel, "four", [((4, 2, BLK, 1408), bf16)], (ids, p1, shift(p1, "xl", 1, 2)), 2, [dma(8)], out_raw=(0,),
            after=after, limit=62,
        )

    kv0, act, own_part, (four,) = attend_own(0, q_0, kv_0, normed0, w0, spread_w1)
    wo = [fetch_wo(0, own_part[1:2])]
    saved0, ends = attend_full(0, q_0, kv0, act, own_part, ())
    w1 = [lax.all_to_all(gate(ids, four, (saved0[3],)), "z", 0, 0, tiled=True).reshape(8, BLK, 1408)]
    terms, sent = scatter(ids, *ends)
    x1, normed_own = call(
        fwd_end_kernel, "fwd_end", [(blk, f32), (blk, bf16)], (ids, *terms, own, gain, bias, bfc), 2,
        vm=range(1, 9), out_vm=(0, 1), limit=8,
    )
    blocks = gather_blocks(normed_own)
    normed1, q_1, kv_1 = call(
        qkv_kernel, "qkv", [(full, bf16), (head, bf16), ((HALF, 256), bf16)], (ids, *blocks, *w1, cosine, sine), 4,
        [room((8, BLK, 384), bf16), dma(8), dma(1)], raw=range(1, 10),
    )
    kv0, act, own_part, _ = attend_own(1, q_1, kv_1, normed1, w1, lambda after: ())
    wo.append(fetch_wo(1, (q_1,)))
    gr_top, dattn_top = grad_in(ids, tok_blocks, wo[1], BLK)
    saved1, ends = attend_full(1, q_1, kv0, act, own_part, ())
    terms, _ = scatter(ids, *ends)
    (mixed,) = call(
        last_end_kernel, "last_end", [(blk, bf16)], (ids, *terms, x1, bfc), 2, vm=range(1, 7), out_vm=(0,), limit=8
    )

    def back(q, kv, normed, w, saved, gr, dattn, rows):
        kv0, active, slope, attn, lse = saved
        dqt0, dkv0 = call(
            grad_full_kernel, "grad_full", [((BLK, HALF), f32), ((HALF, 256), bf16)], (ids, q, kv0, dattn, attn, lse), 8,
            [room(head)] * 2,
        )
        got = lax.ppermute(dkv0, "xh", [(1, 0)])
        part, dbi, payload = ff_back_outer(ids, rows, gr, slope, active, attn, normed, w, (dqt0,))
        pieces = call(
            grad_own_kernel, "grad_own", [((HALF, 384), bf16)], (ids, q, kv, dattn, attn, lse, qseg, dqt0), 5,
            [room((BLK, HALF)), room(head), room(head)],
        )
        return pieces, got, payload, part, dbi

    part_outs = [((4, BLK, D), bf16), ((4, BLK, D), bf16)]
    pieces, got, payload1, part, dbi1 = back(q_1, kv_1, normed1, w1, saved1, gr_top, dattn_top, 384)
    mine, away, payload1 = call(
        combine_kernel, "combine", part_outs + [((8, 384, 512), bf16)],
        (ids, *pieces, got, cosine, sine, part, *w1, normed1, payload1), 6,
        [room((HALF, 384), bf16), room((8, 96, 512), bf16), room((8, BLK, 384), bf16), dma(1), room(full, bf16),
         dma(1)], raw=(6, 7, 8), out_raw=(2,),
        alias={8: 2}, after=(mixed,),
    )
    terms, sent = scatter(ids, mine, away)
    got_a = lax.all_to_all(payload1, FS, 0, 0, tiled=True)
    g1, gr1, sums1 = call(
        bwd_end_kernel, "bwd_end", [(blk, f32), (blk, bf16), ((8, D), f32)], (ids, *terms, x1, gain, cotangent[0]), 2,
        vm=range(1, 8), out_vm=(0, 1, 2), limit=8,
    )
    g_blocks = gather_blocks(gr1)
    gr, dattn = grad_in(ids, g_blocks, wo[0], 0)
    pieces, got, payload, part, dbi0 = back(q_0, kv_0, normed0, w0, saved0, gr, dattn, 400)
    low1, p1 = over_groups(ids, "fsum_top", got_a, after=pieces[:1])
    (main1,) = call(xsum_top_kernel, "xsum_top", [((352, 512), bf16)], (ids, low1, shift(low1, "xh", 1, 2)), 2)
    mine, away, payload = call(
        combine_first_kernel, "combine_first", part_outs + [((8, 400, 512), bf16)],
        (ids, *pieces, got, cosine, sine, wq0, part, xhat0, normed0, sums1, dbi0, dbi1, payload), 9,
        [room((HALF, 384), bf16), room((8, 112, 512), bf16), dma(1)], raw=(12,), out_raw=(2,), alias={12: 2}, after=(main1,),
    )
    terms, sent = scatter(ids, mine, away)
    (g0,) = call(
        bwd_last_kernel, "bwd_last", [(blk, f32)], (ids, *terms, own, gain, g1), 2, vm=range(1, 8), out_vm=(0,), limit=8
    )
    top_rows = gather_blocks(main1)
    shapes = [((2, BLK, 4096), f32), ((2, 512, D), f32), ((2, BLK, 3 * D), f32)]
    rooms = lambda n: [room(s[0][1:]) for s in shapes] + [room((4, 2, n, 512), bf16), dma(8), dma(3)]
    outs = call(assemble_top_kernel, "assemble_top", shapes, (ids, *top_rows), 5, rooms(352), raw=range(1, 9), out_raw=(0, 1, 2))
    low0, piece = over_groups(ids, "fsum_first", lax.all_to_all(payload, FS, 0, 0, tiled=True), (p1,), (g0, outs[2]))
    piece = transpose_owner(piece)
    swap = lambda x: shift(x, "xh", 1, 2)
    (last,) = call(
        xsum_last_kernel, "xsum_last", [((432, 512), bf16)], (ids, low0, swap(low0), piece, swap(piece)), 2,
    )
    last_blocks = gather_blocks(last)
    o_i, o_f, o_q, o_o, o_g, o_s, o_bf, o_bi = call(
        finish_kernel, "finish", shapes + [((2, BLK, D), f32)] + [((2, BLK), f32)] * 3 + [((2, 512), f32)],
        (ids, *last_blocks, *outs), 6, rooms(432)[:-1] + [pltpu.SemaphoreType.DMA((6, 1))], raw=range(1, 12), out_raw=(0, 1, 2),
        alias={9: 0, 10: 1, 11: 2},
    )
    return mixed[None], g0[None], o_g, o_s, o_q, o_o, o_i, o_bi, o_f, o_bf


def solution(mesh):
    fine = Mesh(mesh.devices.reshape(2, 4, 2, 4, 2), AXES)
    seq = ("xh", "y", "core")
    tok = P(FS, seq, None)
    two = P(None, FS)
    three = P(None, FS, None)
    in_specs = (tok, P(FS, None), two, two, three, three, three, two, three, two, tok)
    out_specs = (tok, tok, two, two, three, three, three, two, three, two)
    return jax.shard_map(body, mesh=fine, in_specs=in_specs, out_specs=out_specs, check_vma=False)
```

```python
import functools
import jax
import jax.numpy as jnp
from jax import lax
from jax.experimental import pallas as pl
from jax.experimental.pallas import tpu as pltpu
from jax.sharding import Mesh, PartitionSpec as P

ROT = 32
CONTS = 8
D = 1024
HALF = 1024
BLK = 128
QB = 256
AXES = ("xh", "y", "core", "z", "xl")
FS = ("z", "xl")
f32 = jnp.float32
bf16 = jnp.bfloat16
NT = (((1,), (1,)), ((), ()))
VM = pl.BlockSpec(memory_space=pltpu.VMEM)
SM = pl.BlockSpec(memory_space=pltpu.SMEM)
ANY = pl.BlockSpec(memory_space=pl.ANY)
HBM = pl.BlockSpec(memory_space=pltpu.HBM)
MB = 1024 * 1024


def sds(*args):
    return [jax.ShapeDtypeStruct(s, t) for s, t in args]


class Far:
    def __init__(self, ref, copy):
        self.ref, self.copy = ref, copy

    def here(self):
        if self.copy is not None:
            self.copy.wait()
            self.copy = None
        return self.ref

    def __getitem__(self, index):
        return self.here()[index]

    @property
    def shape(self):
        return self.ref.shape


class Out:
    def __init__(self, ref, copy):
        self.ref, self.copy, self.sent = ref, copy, False

    def __getitem__(self, index):
        return self.ref[index]

    def __setitem__(self, index, value):
        self.ref[index] = value

    @property
    def dtype(self):
        return self.ref.dtype

    @property
    def shape(self):
        return self.ref.shape

    def send(self):
        self.copy.start()
        self.sent = True


COST = 0.001
LIMIT = 51


def call(kernel, name, outs, args, us, scratch=(), limit=None, after=(), raw=(), vm=(), out_raw=(), out_vm=(), alias=None):
    n, m = len(args), len(outs)
    fetched = [i for i in range(1, n) if i not in raw and i not in vm]
    staged = [i for i in range(m) if i not in out_raw and i not in out_vm]

    def run(*refs):
        ins = list(refs[:n])
        results = list(refs[n + len(after) : n + len(after) + m])
        rest = list(refs[n + len(after) + m :])
        own, rest = rest[: len(scratch)], rest[len(scratch) :]
        sems = rest[-1]
        copies = []
        for k, i in enumerate(fetched):
            copy = pltpu.make_async_copy(ins[i], rest[k], sems.at[k])
            copies.append(copy)
            ins[i] = Far(rest[k], copy)
        for copy in copies:
            copy.start()
        for k, i in enumerate(staged):
            ref = rest[len(fetched) + k]
            results[i] = Out(ref, pltpu.make_async_copy(ref, results[i], sems.at[len(fetched) + k]))
        kernel(*ins, *results, *own)
        for i in fetched:
            ins[i].here()
        for i in staged:
            if not results[i].sent:
                results[i].send()
        for i in staged:
            results[i].copy.wait()

    room = [pltpu.VMEM(args[i].shape, args[i].dtype) for i in fetched]
    room += [pltpu.VMEM(outs[i][0], outs[i][1]) for i in staged]
    return pl.pallas_call(
        run,
        out_shape=sds(*outs),
        in_specs=[SM] + [VM if i in vm else HBM for i in range(1, n)] + [ANY] * len(after),
        out_specs=[VM if i in out_vm else HBM for i in range(m)],
        scratch_shapes=list(scratch) + room + [pltpu.SemaphoreType.DMA((max(1, len(room)),))],
        input_output_aliases=alias or {},
        compiler_params=pltpu.CompilerParams(vmem_limit_bytes=(limit or LIMIT) * MB),
        cost_estimate=pl.CostEstimate(flops=int(us * COST * 1e9), bytes_accessed=int(us * COST * 1e6), transcendentals=0),
        name=name,
    )(*args, *after)


def dma(n):
    return pltpu.SemaphoreType.DMA((n,))


def copy_all(pairs, sems):
    copies = [pltpu.make_async_copy(a, b, sems.at[i]) for i, (a, b) in enumerate(pairs)]
    for copy in copies:
        copy.start()
    return copies


def wait_all(copies):
    for copy in copies:
        copy.wait()


def shift(x, axis, by, size):
    return lax.ppermute(x, axis, [(i, (i + by) % size) for i in range(size)])


def gather_blocks(own, hold=None):
    one = shift(own, "y", -1, 4)
    three = shift(own, "y", 1, 4)
    two = shift(own, "y", 2, 4)
    if hold is not None:
        one, two, three = hold(one, two, three)
    blocks = []
    for mine in (own, one, two, three):
        blocks += [mine, shift(mine, "core", 1, 2)]
    return blocks


def spread(low):
    return [shift(low[r - 1], "y", r, 4) for r in (1, 2, 3)]


def transpose_owner(x):
    pairs = [(j * 8 + f, f * 8 + j) for j in range(8) for f in range(8)]
    return lax.ppermute(x, ("y", "core", "z", "xl"), pairs)


def gate(ids, x, after):
    (out,) = call(lambda *refs: None, "gate", [(x.shape, x.dtype)], (ids, x), 1, raw=(1,), out_raw=(0,), after=after, alias={1: 0})
    return out


def gate_all(ids, xs, after):
    n = len(xs)
    return call(
        lambda *refs: None, "gate", [(x.shape, x.dtype) for x in xs], (ids, *xs), 1, raw=range(1, n + 1), out_raw=range(n),
        after=after, alias={i + 1: i for i in range(n)},
    )


def gather_fsdp(ids, x, got, after=()):
    (pair,) = call(
        pair_kernel, "pair", [((2,) + x.shape, bf16)], (ids, x, got), 2, [dma(2)], out_raw=(0,), after=after, limit=62,
    )
    return [pair, shift(pair, "z", -1, 4), shift(pair, "z", 2, 4), shift(pair, "z", 1, 4)]


def weight_copies(ids, pairs, cols, room):
    if len(pairs) == 1:
        return [(pairs[0].at[:, :, cols], room)]
    out = []
    for r in range(4):
        out.append((pairs[r].at[:, :, cols], room.at[pl.ds(2 * lax.rem(ids[4] + r, 4), 2)]))
    return out


def slot(ids, r, s):
    y = lax.rem(ids[0] + r, 4)
    c = ids[1] if s == 0 else 1 - ids[1]
    return y * 2 + c


def rows_of(ids, r, s, n=BLK):
    return pl.ds(pl.multiple_of(slot(ids, r, s) * n, n), n)


def turn(v, cosine, sine):
    lane = lax.broadcasted_iota(jnp.int32, v.shape, 1)
    partner = jnp.where(lane % 2 == 0, pltpu.roll(v, BLK - 1, 1), pltpu.roll(v, 1, 1))
    return v * cosine + partner * sine


def stats(x):
    average = jnp.mean(x, axis=-1, keepdims=True)
    centred = x - average
    variance = jnp.mean(centred * centred, axis=-1, keepdims=True)
    inv = lax.rsqrt(variance + 1e-05)
    return centred * inv, inv


def gelu_both(x):
    a = 0.7978845608028654
    b = 0.044715
    sq = x * x
    t = jnp.tanh(a * x * (1.0 + b * sq))
    half = 0.5 * (1.0 + t)
    slope = half + 0.5 * x * (1.0 - t * t) * a * (1.0 + 3.0 * b * sq)
    return x * half, slope


def dot(a, b):
    return jnp.dot(a, b, preferred_element_type=f32)


def dot_nt(a, b):
    return lax.dot_general(a, b, NT, preferred_element_type=f32)


def pack_q_kernel(ids, wq, gain, bias, bfc, bin_, q0, room, small, binv, sems, out_sems):
    j = ids[0] * 2 + ids[1]
    pairs = []
    for part in range(3):
        cols = pl.ds(pl.multiple_of(part * D + j * BLK, BLK), BLK)
        pairs.append((wq.at[0, :, cols], room.at[0:BLK, part * BLK : part * BLK + BLK]))
    pairs += [(ref, small.at[i]) for i, ref in enumerate((gain, bias, bfc))]
    pairs.append((bin_, binv))
    wait_all(copy_all(pairs, sems))
    chunk = binv[:, pl.ds(pl.multiple_of((j // 2) * BLK, BLK), BLK)].astype(f32)
    chunk = jnp.where(j % 2 == 1, pltpu.roll(chunk, 64, 1), chunk)
    lane = lax.broadcasted_iota(jnp.int32, (1, BLK), 1)
    row2 = jnp.where(lane < 64, chunk[0:1], pltpu.roll(chunk, 64, 1)[1:2])
    blank = jnp.zeros((13, BLK), f32)
    cols = [jnp.concatenate([small[i].astype(f32), row2, blank], 0) for i in range(3)]
    room[BLK:, :] = jnp.concatenate(cols, 1).astype(bf16)
    wait_all(copy_all([(room, q0.at[f]) for f in range(8)], out_sems))


def pack_layer(layer, ids, wi, wf, out, chunks, sems, more=()):
    j = ids[0] * 2 + ids[1]
    rows = pl.ds(pl.multiple_of(j * 64, 64), 64)
    pairs = []
    for f in range(8):
        cols = pl.ds(pl.multiple_of(f * 512 + (j // 2) * BLK, BLK), BLK)
        pairs.append((wi.at[layer, :, cols], chunks.at[f]))
    pairs.append((wf.at[layer, rows, 0:512], out.ref.at[0:64, 512:1024]))
    pairs.append((wf.at[layer, rows, 512:1024], out.ref.at[64:128, 512:1024]))
    wait_all(copy_all(pairs + list(more), sems))
    lane = lax.broadcasted_iota(jnp.int32, (BLK, BLK), 1)
    odd = j % 2 == 1
    for pair in range(4):
        a = chunks[2 * pair].astype(f32)
        b = chunks[2 * pair + 1].astype(f32)
        first = jnp.where(odd, pltpu.roll(a, 64, 1), a)
        second = jnp.where(odd, b, pltpu.roll(b, 64, 1))
        out[:, pair * BLK : pair * BLK + BLK] = jnp.where(lane < 64, first, second).astype(bf16)


def pack_first_kernel(ids, wi, wf, out, chunks, sems):
    pack_layer(0, ids, wi, wf, out, chunks, sems)


def pack_second_kernel(ids, wi, wf, wq, out, chunks, sems):
    j = ids[0] * 2 + ids[1]
    more = []
    for part in range(3):
        cols = pl.ds(pl.multiple_of(part * D + j * BLK, BLK), BLK)
        more.append((wq.at[1, :, cols], out.ref.at[:, D + part * BLK : D + part * BLK + BLK]))
    pack_layer(1, ids, wi, wf, out, chunks, sems, more)


def pass_kernel(layer, ids, x, out, sems):
    wait_all(copy_all([(x.at[layer], out.ref)], sems))


def join_kernel(ids, a, b, out, sems):
    wait_all(copy_all([(a, out.ref.at[0:BLK]), (b, out.ref.at[BLK : 2 * BLK])], sems))


def pair_kernel(ids, own, got, out, sems):
    xl = ids[3]
    wait_all(copy_all([(own.here(), out.at[xl]), (got.here(), out.at[1 - xl])], sems))


def four_kernel(ids, own, got, out, sems):
    xl = ids[3]
    mine, other = own.here(), got.here()
    wait_all(copy_all([(src, out.at[z, at]) for z in range(4) for src, at in ((mine, xl), (other, 1 - xl))], sems))


def params_part(rows_of_f, gain, bias, bfc, bi):
    lane = lax.broadcasted_iota(jnp.int32, (1, BLK), 1)
    for f in range(8):
        cols = slice(f * BLK, f * BLK + BLK)
        rows = rows_of_f[f].astype(f32)
        gain[:, cols] = rows[0:2, 0:BLK]
        bias[:, cols] = rows[0:2, BLK : 2 * BLK]
        bfc[:, cols] = rows[0:2, 2 * BLK :]
    for pair in range(4):
        a = rows_of_f[2 * pair].astype(f32)[2:3, :BLK]
        b = rows_of_f[2 * pair + 1].astype(f32)[2:3, :BLK]
        cols = slice(pair * BLK, pair * BLK + BLK)
        bi[0:1, cols] = jnp.where(lane < 64, a, pltpu.roll(b, 64, 1))
        bi[1:2, cols] = jnp.where(lane < 64, pltpu.roll(a, 64, 1), b)


def qkv_part(normed, w, cosine, sine, q, kv):
    for i in range(HALF // QB):
        rows = slice(i * QB, i * QB + QB)
        out = dot(normed[rows, :], w).astype(bf16).astype(f32)
        cb = cosine[rows, :]
        sb = sine[rows, :]
        kv[rows, :BLK] = turn(out[:, BLK : 2 * BLK], cb, sb).astype(bf16)
        kv[rows, BLK:] = out[:, 2 * BLK :].astype(bf16)
        q[rows, :] = (turn(out[:, :BLK], cb, sb).astype(bf16).astype(f32) * 0.125).astype(bf16)


def take_blocks(ids, blocks, room, sems, at=0):
    part = slice(at, at + BLK)
    return copy_all([(blocks[2 * r + s].at[part], room.at[rows_of(ids, r, s)]) for r in range(4) for s in range(2)], sems)


def qkv_first_kernel(ids, *refs):
    blocks, (wq, cosine, sine), refs = refs[:8], refs[8:11], refs[11:]
    normed, xhat, q, kv, gain, bias, bfc, bi, raw, sems = refs
    copies = take_blocks(ids, blocks, raw, sems)
    w = wq.here()
    params_part([w[f, BLK:, :] for f in range(8)], gain, bias, bfc, bi)
    wait_all(copies)
    for i in range(HALF // QB):
        rows = slice(i * QB, i * QB + QB)
        x, _ = stats(raw[rows, :].astype(f32))
        xhat[rows, :] = x.astype(bf16)
        normed[rows, :] = (x * gain[0:1, :] + bias[0:1, :]).astype(bf16)
    xhat.send()
    normed.send()
    qkv_part(normed, w[:, :BLK, :].reshape(D, 384), cosine, sine, q, kv)


def qkv_kernel(ids, *refs):
    blocks, w, (cosine, sine), (normed, q, kv, wq, sems, wsem) = refs[:8], refs[8:9], refs[9:11], refs[11:]
    copies = copy_all(weight_copies(ids, w, slice(1024, 1408), wq), wsem)
    copies += take_blocks(ids, blocks, normed.ref, sems)
    wait_all(copies)
    normed.send()
    qkv_part(normed, wq[...].reshape(D, 384), cosine, sine, q, kv)


def ff_kernel(layer, ids, far, bi, *refs):
    w, (active, slope, feed, wi, wf, va, vs, vf, wsems, sems, normed) = refs[:-11], refs[-11:]
    copies = copy_all(weight_copies(ids, w, slice(0, 512), wi), wsems.at[0])
    rows = slice(0, QB)
    copies += copy_all([(far.at[rows], normed.at[rows])], wsems.at[2])
    late = copy_all(weight_copies(ids, w, slice(512, 1024), wf), wsems.at[1])
    rows = slice(QB, HALF)
    rest = copy_all([(far.at[rows], normed.at[rows])], wsems.at[3])
    wait_all(copies)
    left = right = None
    sent = []
    for i in range(HALF // QB):
        rows = slice(i * QB, i * QB + QB)
        if i == 1:
            wait_all(rest)
        pre = dot(normed[rows, :], wi[...].reshape(D, 512)) + bi[layer : layer + 1, :]
        act, der = gelu_both(pre)
        act = act.astype(bf16)
        va[rows, :] = act
        vs[rows, :] = der.astype(bf16)
        if i == 0:
            wait_all(late)
            left, right = wf[:, 0:64, :].reshape(512, 512), wf[:, 64:128, :].reshape(512, 512)
        vf[rows, :512] = dot(act, left).astype(bf16)
        vf[rows, 512:] = dot(act, right).astype(bf16)
        pairs = [(v.at[rows], out.at[rows]) for v, out in ((va, active), (vs, slope), (vf, feed))]
        sent += copy_all(pairs, sems.at[i])
    wait_all(sent)


def ff(ids, layer, normed, w, bi, after=()):
    room = lambda *shape: pltpu.VMEM(shape, bf16)
    return call(
        functools.partial(ff_kernel, layer), "ff", [((HALF, 512), bf16), ((HALF, 512), bf16), ((HALF, D), bf16)],
        (ids, normed, bi, *w), 5,
        [room(8, BLK, 512), room(8, BLK, 512), room(HALF, 512), room(HALF, 512), room(HALF, D),
         pltpu.SemaphoreType.DMA((4, 4)), pltpu.SemaphoreType.DMA((4, 3)), room(HALF, D)],
        raw=[1, *range(3, 3 + len(w))], out_raw=(0, 1, 2), limit=62 - 11 * layer, after=after,
    )


def head_cut(x):
    lane = lax.broadcasted_iota(jnp.int32, x.shape, 1)
    zero = jnp.zeros((), x.dtype)
    return [jnp.where(lane < 64, x, zero), jnp.where(lane >= 64, x, zero)]


def seen(i, kk, qseg, kseg, QB):
    q0 = i * QB
    qs = qseg[0:1, q0 : q0 + QB]
    ks = kseg[0:kk, 0:1]
    key = lax.broadcasted_iota(jnp.int32, (kk, QB), 0)
    query = q0 + lax.broadcasted_iota(jnp.int32, (kk, QB), 1)
    return (key <= query) & ((ks == 0) | (ks == qs))


def flip(x):
    return jnp.transpose(x.astype(f32)).astype(bf16)


def attn_own_kernel(ids, q, kv, qseg, acc, m_out, l_out):
    qseg = qseg[...]
    kseg = jnp.transpose(qseg)
    km = head_cut(kv[:, :BLK])
    vt = flip(kv[:, BLK:])
    for i in range(HALF // 512):
        cols = slice(i * 512, (i + 1) * 512)
        kk = (i + 1) * 512
        allowed = seen(i, kk, qseg, kseg, 512)
        for h in range(2):
            rows = slice(h * 64, h * 64 + 64)
            s = jnp.where(allowed, dot_nt(km[h][:kk], q[cols, :]), -1e30)
            m = jnp.max(s, axis=0, keepdims=True)
            p = jnp.exp(s - m)
            l_out[h : h + 1, cols] = jnp.sum(p, axis=0, keepdims=True)
            m_out[h : h + 1, cols] = m
            acc[rows, cols] = dot(vt[rows, :kk], p.astype(bf16))


def split_rows(ids, mine, away, block):
    for r in range(4):
        away[r] = block(rows_of(ids, r, 1)).astype(bf16)
    away.send()
    for r in range(4):
        mine[r] = block(rows_of(ids, r, 0)).astype(bf16)


def attn_full_kernel(ids, q, kv0, acc, m_in, l_in, feed, wo, attn, lse, mine, away, tmp):
    upper = ids[2] == 1
    for ref in (q, kv0, acc, m_in, l_in):
        ref.here()

    @pl.when(upper)
    def _():
        km = head_cut(kv0[:, :BLK])
        vt = flip(kv0[:, BLK:])
        for i in range(HALF // 512):
            cols = slice(i * 512, (i + 1) * 512)
            for h in range(2):
                rows = slice(h * 64, h * 64 + 64)
                s = dot_nt(km[h], q[cols, :])
                m0 = m_in[h : h + 1, cols]
                m = jnp.maximum(m0, jnp.max(s, axis=0, keepdims=True))
                p = jnp.exp(s - m)
                a = jnp.exp(m0 - m)
                l = l_in[h : h + 1, cols] * a + jnp.sum(p, axis=0, keepdims=True)
                o = dot(vt[rows, :], p.astype(bf16))
                tmp[rows, cols] = (acc[rows, cols] * a + o) / l
                lse[h : h + 1, cols] = m + jnp.log(l)

    @pl.when(jnp.logical_not(upper))
    def _():
        for h in range(2):
            rows = slice(h * 64, h * 64 + 64)
            l = l_in[h : h + 1, :]
            tmp[rows, :] = acc[rows, :] / l
            lse[h : h + 1, :] = m_in[h : h + 1, :] + jnp.log(l)

    attn[...] = jnp.transpose(tmp[...]).astype(bf16)
    attn.send()
    lse.send()
    split_rows(ids, mine, away, lambda rows: feed[rows, :].astype(f32) + dot(attn[rows, :], wo[...]))


def mid_kernel(ids, mine, got, total, one, two, three):
    for r, out in ((1, one), (2, two), (3, three)):
        out[...] = (mine[r].astype(f32) + got[r].astype(f32)).astype(bf16)
    total[...] = mine[0].astype(f32) + got[0].astype(f32)


def summed(total, one, two, three):
    return total[...] + one[...].astype(f32) + two[...].astype(f32) + three[...].astype(f32)


def fwd_end_kernel(ids, total, one, two, three, x, gain, bias, bfc, x_new, normed):
    new = x[...].astype(f32) + summed(total, one, two, three) + bfc[0:1, :]
    x_new[...] = new
    xhat, _ = stats(new)
    normed[...] = (xhat * gain[1:2, :] + bias[1:2, :]).astype(bf16)


def last_end_kernel(ids, total, one, two, three, x, bfc, out):
    out[...] = (x[...] + summed(total, one, two, three) + bfc[1:2, :]).astype(bf16)


def grad_in_kernel(at, ids, *refs):
    blocks, (wo, gr, dattn, sems) = refs[:8], refs[8:]
    wait_all(take_blocks(ids, blocks, gr.ref, sems, at))
    gr.send()
    dattn[...] = dot_nt(gr[...], wo[...]).astype(bf16)


def row_delta(attn, do):
    prod = attn[...].astype(f32) * do[...].astype(f32)
    head = lax.broadcasted_iota(jnp.int32, (8, BLK), 0)
    lane = lax.broadcasted_iota(jnp.int32, (8, BLK), 1) // 64
    pickers = jnp.where(head == lane, 1.0, 0.0).astype(f32)
    return lax.dot_general(pickers, prod, NT, precision=lax.Precision.HIGHEST, preferred_element_type=f32)


def grad_block(km, vm, kt, qm, dom, q_blk, do_blk, lse, delta, allowed):
    p = jnp.exp(dot_nt(km, q_blk) - lse)
    if allowed is not None:
        p = jnp.where(allowed, p, 0.0)
    dp = dot_nt(vm, do_blk)
    ds = (p * (dp - delta)).astype(bf16)
    return dot(kt, ds), dot(ds, qm), dot(p.astype(bf16), dom)


def grad_full_kernel(ids, q, kv0, do, attn, lse, dqt, dkv, acck, accv):
    upper = ids[2] == 1
    for ref in (q, kv0, do, attn, lse):
        ref.here()

    @pl.when(upper)
    def _():
        delta = row_delta(attn, do)
        qm, km, vm, dom = [head_cut(x) for x in (q[...], kv0[:, :BLK], kv0[:, BLK:], do[...])]
        kt = flip(kv0[:, :BLK])
        for i in range(HALF // 512):
            cols = slice(i * 512, (i + 1) * 512)
            for h in range(2):
                rows = slice(h * 64, h * 64 + 64)
                dq, dk, dv = grad_block(
                    km[h], vm[h], kt[rows, :], qm[h][cols], dom[h][cols], q[cols, :], do[cols, :],
                    lse[h : h + 1, cols], delta[h : h + 1, cols], None,
                )
                dqt[rows, cols] = dq
                if i == 0 and h == 0:
                    acck[...] = dk
                    accv[...] = dv
                else:
                    acck[...] += dk
                    accv[...] += dv
        dkv[:, :BLK] = acck[...].astype(bf16)
        dkv[:, BLK:] = accv[...].astype(bf16)

    @pl.when(jnp.logical_not(upper))
    def _():
        dqt[...] = jnp.zeros(dqt.shape, f32)
        dkv[...] = jnp.zeros(dkv.shape, bf16)


def grad_own_kernel(ids, q, kv, do, attn, lse, qseg, dqt0, out, tmp, dk_out, dv_out):
    qseg = qseg[...]
    kseg = jnp.transpose(qseg)
    delta = row_delta(attn, do)
    qm, km, vm, dom = [head_cut(x) for x in (q[...], kv[:, :BLK], kv[:, BLK:], do[...])]
    kt = flip(kv[:, :BLK])
    dk_out[...] = jnp.zeros(dk_out.shape, f32)
    dv_out[...] = jnp.zeros(dv_out.shape, f32)
    for i in range(HALF // 256):
        cols = slice(i * 256, (i + 1) * 256)
        kk = (i + 1) * 256
        allowed = seen(i, kk, qseg, kseg, 256)
        for h in range(2):
            rows = slice(h * 64, h * 64 + 64)
            dq, dk, dv = grad_block(
                km[h][:kk], vm[h][:kk], kt[rows, :kk], qm[h][cols], dom[h][cols], q[cols, :], do[cols, :],
                lse[h : h + 1, cols], delta[h : h + 1, cols], allowed,
            )
            tmp[rows, cols] = (dq + dqt0[rows, cols]) * 0.125
            dk_out[:kk, :] += dk
            dv_out[:kk, :] += dv
    out[:, :BLK] = jnp.transpose(tmp[...]).astype(bf16)
    out[:, BLK : 2 * BLK] = dk_out[...].astype(bf16)
    out[:, 2 * BLK :] = dv_out[...].astype(bf16)


def ff_back_outer_kernel(ids, *refs):
    far, w, refs = refs[:5], refs[5:-14], refs[-14:]
    part, dbi, out, wi, wf, vd, v, wsems, sems, gr, slope, active, attn, normed = refs
    rooms = (gr, slope, active, attn, normed)
    copies = copy_all(weight_copies(ids, w, slice(512, 1024), wf), wsems.at[0])
    rows = slice(0, 256)
    first = [(far[0].at[rows], gr.at[rows]), (far[1].at[rows], slope.at[rows])]
    copies += copy_all(first, wsems.at[2])
    late = copy_all(weight_copies(ids, w, slice(0, 512), wi), wsems.at[1])
    rows = slice(256, HALF)
    rest = copy_all([(far[0].at[rows], gr.at[rows]), (far[1].at[rows], slope.at[rows])], wsems.at[3])
    after = copy_all([(far[k], rooms[k]) for k in (2, 3, 4)], wsems.at[4])
    wait_all(copies)
    left, right = wf[:, 0:64, :].reshape(512, 512), wf[:, 64:128, :].reshape(512, 512)
    total = jnp.zeros((1, 512), f32)
    for i in range(HALF // 256):
        if i == 1:
            wait_all(rest)
        rows = slice(i * 256, i * 256 + 256)
        d = (dot_nt(gr[rows, :512], left) + dot_nt(gr[rows, 512:], right)) * slope[rows, :].astype(f32)
        total = total + jnp.sum(d, axis=0, keepdims=True)
        d = d.astype(bf16)
        vd[rows, :] = d
        if i == 0:
            wait_all(late)
        part[rows, :] = dot_nt(d, wi[...].reshape(D, 512)).astype(bf16)
    part.send()
    dbi[...] = jnp.concatenate([total, jnp.zeros((7, 512), f32)], 0)
    wait_all(after)
    wait_all(outer_rows(out, v, sems, active, gr, attn, normed, vd))


def ff_back_outer(ids, rows, gr, slope, active, attn, normed, w, after):
    room = lambda *shape: pltpu.VMEM(shape, bf16)
    return call(
        ff_back_outer_kernel, "ff_back_outer", [((HALF, D), bf16), ((8, 512), f32), ((8, rows, 512), bf16)],
        (ids, gr, slope, active, attn, normed, *w), 9,
        [room(8, BLK, 512), room(8, BLK, 512), room(HALF, 512), room(8, 288, 512), pltpu.SemaphoreType.DMA((5, 4)),
         pltpu.SemaphoreType.DMA((3, 2)), room(HALF, D), room(HALF, 512), room(HALF, 512), room(HALF, BLK), room(HALF, D)],
        raw=range(1, 6 + len(w)), out_raw=(2,), after=after,
    )


def combine_rows(ids, own, back, cosine, sine, dqkv):
    cb = cosine[...]
    sb = -sine[...]
    dqkv[:, :BLK] = turn(own[:, :BLK].astype(f32), cb, sb).astype(bf16)
    dk = own[:, BLK : 2 * BLK].astype(f32) + back[:, :BLK].astype(f32)
    dqkv[:, BLK : 2 * BLK] = turn(dk, cb, sb).astype(bf16)
    dqkv[:, 2 * BLK :] = (own[:, 2 * BLK :].astype(f32) + back[:, BLK:].astype(f32)).astype(bf16)


def combine_kernel(ids, own, back, cosine, sine, part, w1, far, _, mine, away, payload, dqkv, out, wq, wsem, normed, nsem):
    copies = copy_all(weight_copies(ids, (w1,), slice(1024, 1408), wq), wsem)
    late = copy_all([(far, normed)], nsem)
    combine_rows(ids, own, back, cosine, sine, dqkv)
    wait_all(copies)
    w = wq[...].reshape(D, 384)
    split_rows(ids, mine, away, lambda rows: part[rows, :].astype(f32) + dot_nt(dqkv[rows, :], w))
    mine.send()
    wait_all(late)
    g_q = outer(normed[...], dqkv[...])
    for f in range(8):
        pack_rows(out, f, g_q)
    wait_all(copy_all([(out, payload.at[:, 288:384])], wsem))


def combine_first_kernel(ids, own, back, cosine, sine, wq0, part, xhat, normed, sums1, dbi0, dbi1, *refs):
    _, mine, away, payload, dqkv, out, sems = refs
    combine_rows(ids, own, back, cosine, sine, dqkv)
    w = wq0[:, :BLK, :].reshape(D, 384)
    gain = jnp.zeros((1, D), f32)
    base = jnp.zeros((1, D), f32)
    for s, to in ((1, away), (0, mine)):
        for r in range(4):
            rows = rows_of(ids, r, s)
            block = part[rows, :].astype(f32) + dot_nt(dqkv[rows, :], w)
            to[r] = block.astype(bf16)
            gain = gain + jnp.sum(block * xhat[rows, :].astype(f32), axis=0, keepdims=True)
            base = base + jnp.sum(block, axis=0, keepdims=True)
        to.send()
    g_q = outer(normed[...], dqkv[...])
    lane = lax.broadcasted_iota(jnp.int32, (1, BLK), 1)
    blank = jnp.zeros((13, 384), f32)
    none = jnp.zeros((1, 256), f32)
    for f in range(8):
        pack_rows(out, f, g_q)
        cols = slice(f * BLK, f * BLK + BLK)
        row0 = jnp.concatenate([gain[:, cols], base[:, cols], sums1[3:4, cols]], 1)
        row1 = jnp.concatenate([sums1[0:1, cols], sums1[1:2, cols], sums1[2:3, cols]], 1)
        half = slice((f // 2) * BLK, (f // 2) * BLK + BLK)
        a = dbi0[0:1, half]
        b = dbi1[0:1, half]
        if f % 2 == 0:
            b = pltpu.roll(b, 64, 1)
        else:
            a = pltpu.roll(a, 64, 1)
        row2 = jnp.concatenate([jnp.where(lane < 64, a, b), none], 1)
        out[f, 96:112, :384] = jnp.concatenate([row0, row1, row2, blank], 0).astype(bf16)
        out[f, 96:112, 384:] = jnp.zeros((16, 128), bf16)
    wait_all(copy_all([(out, payload.at[:, 288:400])], sems))


def norm_back(dn, x, gain_row, g):
    xhat, inv = stats(x[...].astype(f32))
    dx = dn * gain_row
    dx = inv * (dx - jnp.mean(dx, -1, keepdims=True) - xhat * jnp.mean(dx * xhat, -1, keepdims=True))
    return xhat, g[...].astype(f32) + dx


def bwd_end_kernel(ids, total, one, two, three, x, gain, g, g_new, gr, sums):
    dn = summed(total, one, two, three)
    xhat, new = norm_back(dn, x, gain[1:2, :], g)
    g_new[...] = new
    gr[...] = new.astype(bf16)
    col = lambda v: jnp.sum(v, axis=0, keepdims=True)
    top = col(g[...].astype(f32))
    sums[...] = jnp.concatenate([col(dn * xhat), col(dn), top, col(new), jnp.zeros((4, D), f32)], 0)


def bwd_last_kernel(ids, total, one, two, three, x, gain, g, g_new):
    _, new = norm_back(summed(total, one, two, three), x, gain[0:1, :], g)
    g_new[...] = new


def outer(a, b):
    return lax.dot_general(a, b, (((0,), (0,)), ((), ())), preferred_element_type=f32).astype(bf16)


def pack_rows(out, f, g_q):
    for part in range(3):
        for group in range(4):
            piece = g_q[f * 128 + group * 32 : f * 128 + group * 32 + 32, part * BLK : part * BLK + BLK]
            out[f, part * 32 : part * 32 + 32, group * BLK : group * BLK + BLK] = piece


def outer_rows(out, v, sems, active, gr, attn, normed, dpre):
    for half in range(2):
        cols = slice(half * 512, half * 512 + 512)
        g_f = outer(active[...], gr[:, cols])
        g_o = outer(attn[...], gr[:, cols])
        for f in range(8):
            v[f, 128 + 64 * half : 192 + 64 * half, :] = g_f[f * 64 : f * 64 + 64]
            v[f, 256 + 16 * half : 272 + 16 * half, :] = g_o[f * 16 : f * 16 + 16]
    first = copy_all([(v.at[:, 128:288], out.at[:, 128:288])], sems.at[0])
    for half in range(2):
        cols = slice(half * 512, half * 512 + 512)
        g_i = outer(normed[:, cols], dpre[...])
        for k in range(4):
            v[4 * half + k, 0:128, :] = g_i[k * 128 : k * 128 + 128]
        group = slice(4 * half, 4 * half + 4)
        first += copy_all([(v.at[group, 0:128], out.at[group, 0:128])], sems.at[1 + half])
    return first


def fsum_kernel(ids, got, *refs):
    more, (low, piece, room, sems) = refs[:-4], refs[-4:]
    rows = got.shape[1]
    half = rows // 32 * 16
    parts = (slice(0, half), slice(half, rows))
    copies = copy_all([(got.at[:, part], room.at[:, part]) for part in parts], sems)
    for at in range(0, rows, 16):
        if at in (0, half):
            copies[0 if at == 0 else 1].wait()
        part = slice(at, at + 16)
        total = room[0, part, :].astype(f32)
        for f in range(1, 8):
            total = total + room[f, part, :].astype(f32)
        total = total.astype(bf16)
        if 256 <= at < 288:
            piece[at - 256 : at - 240, :] = total
        else:
            to = at if at < 256 else at - 32
            low[to : to + 16, :] = total
    for ref in more:
        piece[32:64, :] = ref[...]


def add_rows(terms, start, stop):
    total = terms[0][start:stop, :].astype(f32)
    for term in terms[1:]:
        total = total + term[start:stop, :].astype(f32)
    return total.astype(bf16)


def xsum_top_kernel(ids, low, got, main):
    main[...] = add_rows((low, got), 0, 352)


def xsum_last_kernel(ids, low, got, piece, piece_got, main):
    terms = (low, got)
    main[0:112, :] = add_rows(terms, 256, 368)
    main[112:368, :] = add_rows(terms, 0, 256)
    main[368:432, :] = add_rows((piece, piece_got), 0, 64)


def over_groups(ids, name, got, more=(), after=()):
    rows = got.shape[1]
    return call(
        fsum_kernel, name, [((rows - 32, 512), bf16), ((32 + 32 * len(more), 512), bf16)], (ids, got, *more), 3,
        [pltpu.VMEM(got.shape, bf16), dma(2)], raw=(1,), after=after,
    )


def place_in(zero, one, at, y, o_i, o_f):
    lane = lax.broadcasted_iota(jnp.int32, (BLK, BLK), 1)
    start = pl.multiple_of(y * BLK, BLK)
    for half in range(2):
        rows = slice(at + 128 + 64 * half, at + 192 + 64 * half)
        cols = slice(half * 512, half * 512 + 512)
        o_f[pl.ds(start, 64), cols] = zero[rows, :].astype(f32)
        o_f[pl.ds(start + 64, 64), cols] = one[rows, :].astype(f32)
    for pair in range(4):
        cols = slice(pair * BLK, pair * BLK + BLK)
        a, b = zero[at : at + BLK, cols].astype(f32), one[at : at + BLK, cols].astype(f32)
        even = pl.ds(pl.multiple_of(2 * pair * 512 + start, BLK), BLK)
        odd = pl.ds(pl.multiple_of((2 * pair + 1) * 512 + start, BLK), BLK)
        o_i[:, even] = jnp.where(lane < 64, a, pltpu.roll(b, 64, 1))
        o_i[:, odd] = jnp.where(lane < 64, pltpu.roll(a, 64, 1), b)


def place_q(zero, one, at, y, o_q):
    for part in range(3):
        rows = slice(at + part * 32, at + part * 32 + 32)
        start = pl.multiple_of(part * D + 2 * y * BLK, BLK)
        for group in range(4):
            cols = slice(group * BLK, group * BLK + BLK)
            to = slice(group * 32, group * 32 + 32)
            o_q[to, pl.ds(start, BLK)] = zero[rows, cols].astype(f32)
            o_q[to, pl.ds(start + BLK, BLK)] = one[rows, cols].astype(f32)


def fetch_rows(ids, blocks, room, sems):
    pairs = []
    for r in range(4):
        pairs += [(blocks[2 * r], room.at[r, ids[1]]), (blocks[2 * r + 1], room.at[r, 1 - ids[1]])]
    return copy_all(pairs, sems)


def assemble_top_kernel(ids, *refs):
    blocks, (o_i, o_f, o_q, vi, vf, vq, room, sems, out_sems) = refs[:8], refs[8:]
    copies = fetch_rows(ids, blocks, room, sems)
    for r in range(4):
        wait_all(copies[2 * r : 2 * r + 2])
        y = lax.rem(ids[0] + r, 4)
        place_in(room.at[r, 0], room.at[r, 1], 0, y, vi, vf)
        place_q(room.at[r, 0], room.at[r, 1], 256, y, vq)
    wait_all(copy_all([(vi, o_i.at[1]), (vf, o_f.at[1]), (vq, o_q.at[1])], out_sems))


def finish_kernel(ids, *refs):
    blocks, refs = refs[:8], refs[11:]
    o_i, o_f, o_q, o_o, o_g, o_s, o_bf, o_bi, vi, vf, vq, room, sems, out_sems = refs
    copies = fetch_rows(ids, blocks, room, sems)
    outs = []
    total = jnp.zeros((16, 384), f32)
    lane = lax.broadcasted_iota(jnp.int32, (1, BLK), 1)
    for r in range(4):
        wait_all(copies[2 * r : 2 * r + 2])
        y = lax.rem(ids[0] + r, 4)
        place_in(room.at[r, 0], room.at[r, 1], 112, y, vi, vf)
        rows = pl.ds(pl.multiple_of(y * BLK, BLK), BLK)
        outs += copy_all([(vf.at[rows], o_f.at[0, rows])], out_sems.at[r])
    outs += copy_all([(vi, o_i.at[0])], out_sems.at[4])
    for r in range(4):
        place_q(room.at[r, 0], room.at[r, 1], 0, lax.rem(ids[0] + r, 4), vq)
    outs += copy_all([(vq, o_q.at[0])], out_sems.at[5])
    for r in range(4):
        y = lax.rem(ids[0] + r, 4)
        for layer in range(2):
            for half in range(2):
                at = 368 + 32 * layer + 16 * half
                cols = slice(half * 512, half * 512 + 512)
                start = pl.multiple_of(y * 32, 32)
                o_o[layer, pl.ds(start, 16), cols] = room[r, 0, at : at + 16, :].astype(f32)
                o_o[layer, pl.ds(start + 16, 16), cols] = room[r, 1, at : at + 16, :].astype(f32)
        zero, one = room[r, 0, 96:112, :384].astype(f32), room[r, 1, 96:112, :384].astype(f32)
        total = total + zero + one
        a, b = zero[2:3, :BLK], one[2:3, :BLK]
        cols = pl.ds(pl.multiple_of(y * BLK, BLK), BLK)
        o_bi[0:1, cols] = jnp.where(lane < 64, a, pltpu.roll(b, 64, 1))
        o_bi[1:2, cols] = jnp.where(lane < 64, pltpu.roll(a, 64, 1), b)
    o_g[...] = total[0:2, :BLK]
    o_s[...] = total[0:2, BLK : 2 * BLK]
    o_bf[...] = total[0:2, 2 * BLK :]
    for ref in (o_o, o_g, o_s, o_bf, o_bi):
        ref.send()
    wait_all(outs)


def positions_of(group_seg):
    token_index = jnp.arange(group_seg.shape[0], dtype=jnp.int32)
    labels = jnp.arange(CONTS + 1, dtype=jnp.int32)
    member = (group_seg[:, None] == labels[None, :]).astype(jnp.int32)
    counts = jnp.sum(member, axis=0)
    starts = jnp.cumsum(counts) - counts
    own_start = jnp.sum(member * starts[None, :], axis=1)
    return token_index - own_start + jnp.where(group_seg > 0, counts[0], 0)


def rope_tables(positions):
    lane = jnp.arange(BLK, dtype=jnp.int32) % 64
    inverse = 10000.0 ** (-2.0 * (lane // 2).astype(f32) / ROT)
    phase = positions.astype(f32)[:, None] * jnp.where(lane < ROT, inverse, 0.0)[None, :]
    sign = jnp.where(lane % 2 == 0, -1.0, 1.0)
    return jnp.cos(phase), jnp.sin(phase) * sign[None, :]


def scatter(ids, mine, away):
    got = shift(away, "core", 1, 2)
    blk = (BLK, D)
    total, one, two, three = call(
        mid_kernel, "rs_mid", [(blk, f32)] + [(blk, bf16)] * 3, (ids, mine, got), 2, vm=(2,), out_vm=(0, 1, 2, 3), limit=8
    )
    return [total] + spread([one, two, three]), one


def grad_in(ids, g_blocks, wo, at):
    return call(
        functools.partial(grad_in_kernel, at), "grad_in", [((HALF, D), bf16), ((HALF, BLK), bf16)], (ids, *g_blocks, wo), 3,
        [dma(8)], raw=range(1, 9),
    )


def body(tokens, segment, ln_gain, ln_bias, w_qkv, w_out, w_in, b_in, w_fc, b_fc, cotangent):
    xh = lax.axis_index("xh")
    ids = jnp.stack([lax.axis_index("y"), lax.axis_index("core"), xh, lax.axis_index("xl"), lax.axis_index("z")]).astype(jnp.int32)
    own = tokens[0]
    full = (HALF, D)
    blk = (BLK, D)
    head = (HALF, BLK)
    room = lambda shape, kind=f32: pltpu.VMEM(shape, kind)
    chunks = [room((8, BLK, BLK), bf16)]

    group_seg = segment[0]
    positions = positions_of(group_seg)
    seg = lax.dynamic_slice_in_dim(group_seg, xh * HALF, HALF, 0)
    cosine, sine = rope_tables(lax.dynamic_slice_in_dim(positions, xh * HALF, HALF, 0))
    qseg = jnp.broadcast_to(seg[None, :].astype(f32), (8, HALF))

    both = jnp.concatenate([own, cotangent[0]], 0)
    (p0,) = call(
        pack_first_kernel, "pack_first", [(blk, bf16)], (ids, w_in, w_fc), 3, chunks + [dma(10)], raw=(1, 2), limit=62, after=(both,),
    )
    other0 = shift(p0, "xl", 1, 2)
    (q0,) = call(
        pack_q_kernel, "pack_q", [((8, 144, 384), bf16)], (ids, w_qkv, ln_gain, ln_bias, b_fc, b_in), 3,
        [room((144, 384), bf16), room((3, 2, BLK), bf16), room((2, 512), bf16), dma(7), dma(8)],
        raw=(1, 2, 3, 4, 5), out_raw=(0,), after=(other0,), limit=62,
    )
    wq0 = lax.all_to_all(q0, FS, 0, 0, tiled=True)
    (p1,) = call(
        pack_second_kernel, "pack_second", [((BLK, 1408), bf16)], (ids, w_in, w_fc, w_qkv), 3, chunks + [dma(13)], raw=(1, 2, 3), limit=62,
        after=(wq0,),
    )
    tok_blocks = gather_blocks(both, lambda *x: gate_all(ids, x, (q0,)))
    w0 = gather_fsdp(ids, p0, other0)

    def attend_own(layer, q, kv, normed, w, before):
        kv0 = lax.ppermute(kv, "xh", [(0, 1)])
        own_part = call(
            attn_own_kernel, "attn_own", [((BLK, HALF), f32), ((2, HALF), f32), ((2, HALF), f32)], (ids, q, kv, qseg), 5, limit=62 if layer == 0 else None
        )
        first = before(own_part[1:2])
        return kv0, ff(ids, layer, normed, w, bi, first), own_part, first

    def attend_full(layer, q, kv0, act, own_part, after):
        active, slope, feed = act
        attn, lse, mine, away = call(
            attn_full_kernel, "attn_full", [(head, bf16), ((2, HALF), f32)] + [((4, BLK, D), bf16)] * 2,
            (ids, q, kv0, *own_part, feed, wo[layer]), 8, [room((BLK, HALF))], after=after,
        )
        return (kv0, active, slope, attn, lse), (mine, away)

    normed0, xhat0, q_0, kv_0, gain, bias, bfc, bi = call(
        qkv_first_kernel, "qkv_first",
        [(full, bf16), (full, bf16), (head, bf16), ((HALF, 256), bf16)] + [((2, D), f32)] * 3 + [((2, 512), f32)],
        (ids, *tok_blocks, wq0, cosine, sine), 6, [room(full, bf16), dma(8)], raw=range(1, 9), out_vm=(4, 5, 6, 7),
        limit=62,
    )

    def fetch_wo(layer, after):
        (out,) = call(
            functools.partial(pass_kernel, layer), "pass_wo", [(blk, bf16)], (ids, w_out), 1, [dma(1)], raw=(1,), after=after,
            limit=62,
        )
        return transpose_owner(out)

    def spread_w1(after):
        return call(
            four_kernel, "four", [((4, 2, BLK, 1408), bf16)], (ids, p1, shift(p1, "xl", 1, 2)), 2, [dma(8)], out_raw=(0,),
            after=after, limit=62,
        )

    kv0, act, own_part, (four,) = attend_own(0, q_0, kv_0, normed0, w0, spread_w1)
    wo = [fetch_wo(0, own_part[1:2])]
    saved0, ends = attend_full(0, q_0, kv0, act, own_part, ())
    w1 = [lax.all_to_all(gate(ids, four, (saved0[3],)), "z", 0, 0, tiled=True).reshape(8, BLK, 1408)]
    terms, sent = scatter(ids, *ends)
    x1, normed_own = call(
        fwd_end_kernel, "fwd_end", [(blk, f32), (blk, bf16)], (ids, *terms, own, gain, bias, bfc), 2,
        vm=range(1, 9), out_vm=(0, 1), limit=8,
    )
    blocks = gather_blocks(normed_own)
    normed1, q_1, kv_1 = call(
        qkv_kernel, "qkv", [(full, bf16), (head, bf16), ((HALF, 256), bf16)], (ids, *blocks, *w1, cosine, sine), 4,
        [room((8, BLK, 384), bf16), dma(8), dma(1)], raw=range(1, 10),
    )
    kv0, act, own_part, _ = attend_own(1, q_1, kv_1, normed1, w1, lambda after: ())
    wo.append(fetch_wo(1, (q_1,)))
    gr_top, dattn_top = grad_in(ids, tok_blocks, wo[1], BLK)
    saved1, ends = attend_full(1, q_1, kv0, act, own_part, ())
    terms, _ = scatter(ids, *ends)
    (mixed,) = call(
        last_end_kernel, "last_end", [(blk, bf16)], (ids, *terms, x1, bfc), 2, vm=range(1, 7), out_vm=(0,), limit=8
    )

    def back(q, kv, normed, w, saved, gr, dattn, rows):
        kv0, active, slope, attn, lse = saved
        dqt0, dkv0 = call(
            grad_full_kernel, "grad_full", [((BLK, HALF), f32), ((HALF, 256), bf16)], (ids, q, kv0, dattn, attn, lse), 8,
            [room(head)] * 2,
        )
        got = lax.ppermute(dkv0, "xh", [(1, 0)])
        part, dbi, payload = ff_back_outer(ids, rows, gr, slope, active, attn, normed, w, (dqt0,))
        pieces = call(
            grad_own_kernel, "grad_own", [((HALF, 384), bf16)], (ids, q, kv, dattn, attn, lse, qseg, dqt0), 5,
            [room((BLK, HALF)), room(head), room(head)],
        )
        return pieces, got, payload, part, dbi

    part_outs = [((4, BLK, D), bf16), ((4, BLK, D), bf16)]
    pieces, got, payload1, part, dbi1 = back(q_1, kv_1, normed1, w1, saved1, gr_top, dattn_top, 384)
    mine, away, payload1 = call(
        combine_kernel, "combine", part_outs + [((8, 384, 512), bf16)],
        (ids, *pieces, got, cosine, sine, part, *w1, normed1, payload1), 6,
        [room((HALF, 384), bf16), room((8, 96, 512), bf16), room((8, BLK, 384), bf16), dma(1), room(full, bf16),
         dma(1)], raw=(6, 7, 8), out_raw=(2,),
        alias={8: 2}, after=(mixed,),
    )
    terms, sent = scatter(ids, mine, away)
    got_a = lax.all_to_all(payload1, FS, 0, 0, tiled=True)
    g1, gr1, sums1 = call(
        bwd_end_kernel, "bwd_end", [(blk, f32), (blk, bf16), ((8, D), f32)], (ids, *terms, x1, gain, cotangent[0]), 2,
        vm=range(1, 8), out_vm=(0, 1, 2), limit=8,
    )
    g_blocks = gather_blocks(gr1)
    gr, dattn = grad_in(ids, g_blocks, wo[0], 0)
    pieces, got, payload, part, dbi0 = back(q_0, kv_0, normed0, w0, saved0, gr, dattn, 400)
    low1, p1 = over_groups(ids, "fsum_top", got_a, after=pieces[:1])
    (main1,) = call(xsum_top_kernel, "xsum_top", [((352, 512), bf16)], (ids, low1, shift(low1, "xh", 1, 2)), 2)
    mine, away, payload = call(
        combine_first_kernel, "combine_first", part_outs + [((8, 400, 512), bf16)],
        (ids, *pieces, got, cosine, sine, wq0, part, xhat0, normed0, sums1, dbi0, dbi1, payload), 9,
        [room((HALF, 384), bf16), room((8, 112, 512), bf16), dma(1)], raw=(12,), out_raw=(2,), alias={12: 2}, after=(main1,),
    )
    terms, sent = scatter(ids, mine, away)
    (g0,) = call(
        bwd_last_kernel, "bwd_last", [(blk, f32)], (ids, *terms, own, gain, g1), 2, vm=range(1, 8), out_vm=(0,), limit=8
    )
    top_rows = gather_blocks(main1)
    shapes = [((2, BLK, 4096), f32), ((2, 512, D), f32), ((2, BLK, 3 * D), f32)]
    rooms = lambda n: [room(s[0][1:]) for s in shapes] + [room((4, 2, n, 512), bf16), dma(8), dma(3)]
    outs = call(assemble_top_kernel, "assemble_top", shapes, (ids, *top_rows), 5, rooms(352), raw=range(1, 9), out_raw=(0, 1, 2))
    low0, piece = over_groups(ids, "fsum_first", lax.all_to_all(payload, FS, 0, 0, tiled=True), (p1,), (g0, outs[2]))
    piece = transpose_owner(piece)
    swap = lambda x: shift(x, "xh", 1, 2)
    (last,) = call(
        xsum_last_kernel, "xsum_last", [((432, 512), bf16)], (ids, low0, swap(low0), piece, swap(piece)), 2,
    )
    last_blocks = gather_blocks(last)
    o_i, o_f, o_q, o_o, o_g, o_s, o_bf, o_bi = call(
        finish_kernel, "finish", shapes + [((2, BLK, D), f32)] + [((2, BLK), f32)] * 3 + [((2, 512), f32)],
        (ids, *last_blocks, *outs), 6, rooms(432)[:-1] + [pltpu.SemaphoreType.DMA((6, 1))], raw=range(1, 12), out_raw=(0, 1, 2),
        alias={9: 0, 10: 1, 11: 2},
    )
    return mixed[None], g0[None], o_g, o_s, o_q, o_o, o_i, o_bi, o_f, o_bf


def solution(mesh):
    fine = Mesh(mesh.devices.reshape(2, 4, 2, 4, 2), AXES)
    seq = ("xh", "y", "core")
    tok = P(FS, seq, None)
    two = P(None, FS)
    three = P(None, FS, None)
    in_specs = (tok, P(FS, None), two, two, three, three, three, two, three, two, tok)
    out_specs = (tok, tok, two, two, three, three, three, two, three, two)
    return jax.shard_map(body, mesh=fine, in_specs=in_specs, out_specs=out_specs, check_vma=False)
```
